32 devices in a mesh: dp: 16 (over z, y, x), tensor: 2 (over core).
Axes of the slice: x: 2, y: 2, z: 4, core: 2. Of those that a mesh axis runs over, the one named last changes fastest.
Arguments:
- states: bfloat16 [128, 128, 768], P('dp'), may hold values from -6 to 6
- cotangent: bfloat16 [128, 128, 768], P('dp'), may hold values from -6 to 6
- word_counts: int32 [128], P('dp'), may hold values from 5 to 60, as said below
- region_counts: int32 [128], P('dp'), may hold values from 36 to 68, as said below
- attend_in: float32 [3, 768, 768], P(None, 'dp', 'tensor')
- attend_out: float32 [768, 768], P('tensor', 'dp')
- expand_up: float32 [768, 3072], P('dp', 'tensor')
- expand_down: float32 [3072, 768], P(('tensor', 'dp'))
- first_in: float32 [3, 768, 768], P(None, 'dp', 'tensor')
- first_out: float32 [768, 768], P('tensor', 'dp')
- first_up: float32 [768, 3072], P('dp', 'tensor')
- first_down: float32 [3072, 768], P(('tensor', 'dp'))
- second_in: float32 [3, 768, 768], P(None, 'dp', 'tensor'), may hold values from 8.192 to 32.768
- second_out: float32 [768, 768], P('tensor', 'dp'), may hold values from 0.32768 to 1.31072
- second_up: float32 [768, 3072], P('dp', 'tensor'), may hold values from 8.192 to 32.768
- second_down: float32 [3072, 768], P(('tensor', 'dp')), may hold values from 8.192 to 32.768
- vectors: float32 [12, 768], replicated, as said below
- vector_first: float32 [12, 768], replicated, may hold values from -64 to 64
- vector_second: float32 [12, 768], replicated, may hold values from 8.192 to 32.768
Outputs:
- layer_output: bfloat16 [128, 128, 768], P('dp')
- states_grad: float32 [128, 128, 768], P('dp')
- updated_in: float32 [3, 768, 768], P(None, 'dp', 'tensor')
- updated_out: float32 [768, 768], P('tensor', 'dp')
- updated_up: float32 [768, 3072], P('dp', 'tensor')
- updated_down: float32 [3072, 768], P(('tensor', 'dp'))
- moment_in: float32 [3, 768, 768], P(None, 'dp', 'tensor')
- moment_out: float32 [768, 768], P('tensor', 'dp')
- moment_up: float32 [768, 3072], P('dp', 'tensor')
- moment_down: float32 [3072, 768], P(('tensor', 'dp'))
- square_in: float32 [3, 768, 768], P(None, 'dp', 'tensor')
- square_out: float32 [768, 768], P('tensor', 'dp')
- square_up: float32 [768, 3072], P('dp', 'tensor')
- square_down: float32 [3072, 768], P(('tensor', 'dp'))
- copy_in: bfloat16 [3, 768, 768], P(None, 'dp', 'tensor')
- copy_out: bfloat16 [768, 768], P('tensor', 'dp')
- copy_up: bfloat16 [768, 3072], P('dp', 'tensor')
- copy_down: bfloat16 [3072, 768], P(('tensor', 'dp'))
- updated_vectors: float32 [12, 768], replicated
- moment_vectors: float32 [12, 768], replicated
- square_vectors: float32 [12, 768], replicated
- norm_pairs: float32 [6, 2], replicated
The draws below stay inside these ranges and needn't reach their ends.
Inputs may be any that keep to these rules, and one draw needn't show every extreme that they name: `word_counts`: each pair's number of words; in every draw some pair has exactly 60 and some pair exactly 5, most pairs few. `region_counts`: each pair's number of image regions; in every draw some pair has exactly 68 and some pair exactly 36. `vectors`: rows 3 and 6 are positive.
All inputs are finite; a program needn't handle non-finite values.
Results may differ from the reference program's by a relative error of at most 0.014.
Values may be sent and summed in bfloat16 or wider, within the bound.
No kernel may reach another device: no remote copies, remote signals or barrier semaphores. Data moves between devices by JAX's collectives and lax.ppermute only.
A program may use at most 128 MiB of HBM per device.

```python
import math
import jax
import jax.numpy as jnp
from jax import lax

HEADS = 12
HEAD_DIM = 64
D = 768
FF = 3072
WORDS_MIN = 5
WORDS_MAX = 60
REGIONS_MIN = 36
REGIONS_MAX = 68
STEP = 10
SEQ = 128
PAIRS = 128
VEC = 12


def ramp(count, top):
    return top ** (jnp.arange(count, dtype=jnp.float32) / max(count - 1, 1) - 0.5)


def rising_normal(key, shape, axis, scale, top):
    view = [1] * len(shape)
    view[axis] = shape[axis]
    return scale * jax.random.normal(key, shape, jnp.float32) * ramp(shape[axis], top).reshape(view)


def forced_counts(values, key, lowest, highest, count):
    spot = jax.random.randint(key, (), 0, count)
    index = jnp.arange(count)
    values = jnp.where(index == spot, highest, values)
    return jnp.where(index == (spot + 1) % count, lowest, values).astype(jnp.int32)


def draw_word_counts(key, part):
    key = jax.random.fold_in(key, 21)
    first_key, second_key, spot_key = jax.random.split(key, 3)
    span = WORDS_MAX - WORDS_MIN
    left = jax.random.randint(first_key, (PAIRS,), 0, span + 1)
    right = jax.random.randint(second_key, (PAIRS,), 0, span + 1)
    values = WORDS_MIN + left * right // span
    return forced_counts(values, spot_key, WORDS_MIN, WORDS_MAX, PAIRS)


def draw_region_counts(key, part):
    key = jax.random.fold_in(key, 22)
    value_key, spot_key = jax.random.split(key)
    values = jax.random.randint(value_key, (PAIRS,), REGIONS_MIN, REGIONS_MAX + 1)
    return forced_counts(values, spot_key, REGIONS_MIN, REGIONS_MAX, PAIRS)


def draw_attend_in(key, part):
    key = jax.random.fold_in(key, 1)
    top = 3.0 ** 0.5
    return rising_normal(key, (3, D, D), 1, D ** (-0.5), top)


def draw_attend_out(key, part):
    key = jax.random.fold_in(key, 2)
    top = 3.0 ** 0.5
    return rising_normal(key, (D, D), 1, 4.0 * D ** (-0.5), top)


def draw_expand_up(key, part):
    key = jax.random.fold_in(key, 3)
    top = 3.0 ** 0.5
    return rising_normal(key, (D, FF), 0, D ** (-0.5), top)


def draw_expand_down(key, part):
    key = jax.random.fold_in(key, 4)
    top = 3.0 ** 0.5
    return rising_normal(key, (FF, D), 0, FF ** (-0.5), top)


def draw_first_in(key, part):
    key = jax.random.fold_in(key, 5)
    top = 3.0 ** 0.5
    return rising_normal(key, (3, D, D), 1, 0.111 * (PAIRS * SEQ / 2) ** 0.5, top)


def draw_first_out(key, part):
    key = jax.random.fold_in(key, 6)
    top = 3.0 ** 0.5
    return rising_normal(key, (D, D), 1, 0.2 * 0.111 * (PAIRS * SEQ / 2) ** 0.5, top)


def draw_first_up(key, part):
    key = jax.random.fold_in(key, 7)
    top = 3.0 ** 0.5
    return rising_normal(key, (D, FF), 0, 0.111 * (PAIRS * SEQ / 2) ** 0.5, top)


def draw_first_down(key, part):
    key = jax.random.fold_in(key, 8)
    top = 3.0 ** 0.5
    return rising_normal(key, (FF, D), 0, 0.111 * (PAIRS * SEQ / 2) ** 0.5, top)


def draw_vectors(key, part):
    key = jax.random.fold_in(key, 9)
    top = 3.0
    base_key, gain_key = jax.random.split(key)
    base = 0.3 * jax.random.normal(base_key, (VEC, D), jnp.float32)
    gains = ramp(D, top)[None, :] * jax.random.uniform(gain_key, (VEC, D), jnp.float32, 0.85, 1.15)
    row_index = jnp.arange(VEC)[:, None]
    return jnp.where((row_index == 3) | (row_index == 6), gains, base)


def steps_of(stream_key, extent, shards, low, high):
    def one(axis_at, shards_of):
        steps = jax.random.uniform(jax.random.fold_in(jax.random.fold_in(stream_key, 6), axis_at), (shards_of,), jnp.float32, low / len(shards), high / len(shards))
        return jnp.repeat(jnp.exp(steps), extent[axis_at] // shards_of).reshape((-1,) + (1,) * (len(extent) - axis_at - 1))

    loudness = one(*shards[0])
    for cut in shards[1:]:
        loudness = loudness * one(*cut)
    return loudness


def noise(rng, shape, scale, most, pieces=(), kind=jnp.bfloat16):
    entries = jax.random.normal(rng, shape, jnp.float32) * scale
    if len(pieces) > 0:
        entries = steps_of(rng, shape, pieces, -0.22, 0.18) * entries
    return jnp.clip(entries, min=-most, max=most).astype(kind)


def setup_inputs(seed: int = 0) -> dict:
    splits = jax.random.split(jax.random.key(seed), 20)
    states = noise(splits[0], (PAIRS, SEQ, D), 1.0, 6.0, ((0, 16),))
    cotangent = noise(splits[1], (PAIRS, SEQ, D), 1.0, 6.0, ((0, 16),))
    word_counts = draw_word_counts(jax.random.fold_in(splits[19], 71), 0)
    region_counts = draw_region_counts(jax.random.fold_in(splits[19], 71), 0)
    attend_in = draw_attend_in(jax.random.fold_in(splits[19], 71), 0)
    attend_out = draw_attend_out(jax.random.fold_in(splits[19], 71), 0)
    expand_up = draw_expand_up(jax.random.fold_in(splits[19], 71), 0)
    expand_down = draw_expand_down(jax.random.fold_in(splits[19], 71), 0)
    first_in = draw_first_in(jax.random.fold_in(splits[19], 71), 0)
    first_out = draw_first_out(jax.random.fold_in(splits[19], 71), 0)
    first_up = draw_first_up(jax.random.fold_in(splits[19], 71), 0)
    first_down = draw_first_down(jax.random.fold_in(splits[19], 71), 0)
    second_in = jnp.clip(jnp.exp(math.log(32.768) - 1.3862944 * jax.random.uniform(splits[12], (3, D, D), jnp.float32) ** steps_of(splits[12], (3, D, D), ((1, 16), (2, 2)), -0.2, 0.2)), 8.192, 32.768)
    second_out = jnp.clip(jnp.exp(math.log(1.31072) - 1.3862944 * jax.random.uniform(splits[13], (D, D), jnp.float32) ** steps_of(splits[13], (D, D), ((0, 2), (1, 16)), -0.2, 0.2)), 0.32768, 1.31072)
    second_up = jnp.clip(jnp.exp(math.log(32.768) - 1.3862944 * jax.random.uniform(splits[14], (D, FF), jnp.float32) ** steps_of(splits[14], (D, FF), ((0, 16), (1, 2)), -0.2, 0.2)), 8.192, 32.768)
    second_down = jnp.clip(jnp.exp(math.log(32.768) - 1.3862944 * jax.random.uniform(splits[15], (FF, D), jnp.float32) ** steps_of(splits[15], (FF, D), ((0, 32),), -0.2, 0.2)), 8.192, 32.768)
    vectors = draw_vectors(jax.random.fold_in(splits[19], 71), 0)
    vector_first = noise(splits[17], (VEC, D), (0.111 * (PAIRS * SEQ / 2) ** 0.5), 64.0, (), jnp.float32)
    vector_second = jnp.clip(jnp.exp(jax.random.uniform(splits[18], (VEC, D), jnp.float32, math.log(8.192), math.log(32.768))), 8.192, 32.768)
    return {"states": states, "cotangent": cotangent, "word_counts": word_counts, "region_counts": region_counts, "attend_in": attend_in, "attend_out": attend_out, "expand_up": expand_up, "expand_down": expand_down, "first_in": first_in, "first_out": first_out, "first_up": first_up, "first_down": first_down, "second_in": second_in, "second_out": second_out, "second_up": second_up, "second_down": second_down, "vectors": vectors, "vector_first": vector_first, "vector_second": vector_second}


@jax.custom_vjp
def low(v):
    return lax.optimization_barrier(v.astype(jnp.bfloat16)).astype(jnp.float32)

@jax.custom_vjp
def low_back(v):
    return v

def low_keep(v):
    return (low(v), None)

def low_pass(kept, grad):
    return (grad,)

def back_keep(v):
    return (v, None)

def back_low(kept, grad):
    return (low(grad),)
low.defvjp(low_keep, low_pass)
low_back.defvjp(back_keep, back_low)
HIGH = lax.Precision.HIGHEST
NORM_EPS = 1e-05
BETA_ONE = 0.9
BETA_TWO = 0.999
ADAM_EPS = 1e-06
RATE = 0.3
DECAY = 0.01
MASKED = -1e+30

def layer_norm(values, gain, shift):
    center = values - lax.optimization_barrier(jnp.mean(values, axis=-1, keepdims=True))
    inverse = lax.rsqrt(lax.optimization_barrier(jnp.mean(center * center, axis=-1, keepdims=True)) + NORM_EPS)
    return center * inverse * gain + shift

def block_forward(weights, block, valid):
    weight_in, weight_out, weight_up, weight_down, vectors = weights
    group = block.shape[0]
    flat = block.reshape(group * SEQ, D)
    query = low(low_back(jnp.dot(flat, weight_in[0], precision=HIGH)) + vectors[0])
    key_rows = low(low_back(jnp.dot(flat, weight_in[1], precision=HIGH)))
    value = low(low_back(jnp.dot(flat, weight_in[2], precision=HIGH)) + vectors[1])
    shape_heads = (group, SEQ, HEADS, HEAD_DIM)
    scores = jnp.einsum('pqhd,pkhd->phqk', query.reshape(shape_heads), key_rows.reshape(shape_heads), precision=HIGH) * HEAD_DIM ** (-0.5)
    scores = low_back(jnp.where(valid[:, None, None, :], scores, MASKED))
    probs = low(jax.nn.softmax(scores, axis=-1))
    context = jnp.einsum('phqk,pkhd->pqhd', probs, value.reshape(shape_heads), precision=HIGH).reshape(group * SEQ, D)
    context = low_back(low(context))
    attended = low_back(jnp.dot(context, weight_out, precision=HIGH))
    hidden = layer_norm(flat + attended + vectors[2], vectors[3], vectors[4])
    lifted = low_back(jnp.dot(low(hidden), weight_up, precision=HIGH)) + vectors[8:].reshape(FF)
    activated = low(jax.nn.gelu(lifted, approximate=False))
    lowered = low_back(jnp.dot(activated, weight_down, precision=HIGH))
    output = layer_norm(hidden + lowered + vectors[5], vectors[6], vectors[7])
    return output.reshape(group, SEQ, D)

def adam_terms(grad, first, second):
    first_new = BETA_ONE * first + (1.0 - BETA_ONE) * grad
    second_new = BETA_TWO * second + (1.0 - BETA_TWO) * grad * grad
    corrected = first_new / (1.0 - BETA_ONE ** STEP)
    spread = jnp.sqrt(second_new / (1.0 - BETA_TWO ** STEP))
    return (first_new, second_new, corrected / (spread + ADAM_EPS))

def weight_squares(mats):
    rest = jnp.stack([jnp.sum(item * item) for item in mats[1:]])
    return jnp.concatenate([lax.optimization_barrier(jnp.sum(mats[0] * mats[0], axis=(1, 2))), rest])

def reference(states, cotangent, word_counts, region_counts, attend_in, attend_out, expand_up, expand_down, first_in, first_out, first_up, first_down, second_in, second_out, second_up, second_down, vectors, vector_first, vector_second):
    lengths = word_counts + region_counts
    valid = jnp.arange(SEQ, dtype=jnp.int32)[None, :] < lengths[:, None]
    group = math.gcd(PAIRS, max(1, 4096 // SEQ))
    count = PAIRS // group

    def forward(weights, inputs):
        lowered = (low(weights[0]), low(weights[1]), low(weights[2]), low(weights[3]), weights[4])
        step_fn = jax.checkpoint(lambda pair: block_forward(lowered, pair[0], pair[1]))
        result = lax.map(step_fn, (inputs.reshape(count, group, SEQ, D), valid.reshape(count, group, SEQ)))
        return result.reshape(PAIRS, SEQ, D)
    weights = (attend_in, attend_out, expand_up, expand_down, vectors)
    output, pullback = jax.vjp(forward, weights, states.astype(jnp.float32))
    upstream = cotangent.astype(jnp.float32) * valid[:, :, None].astype(jnp.float32)
    grads, states_grad = pullback(upstream)
    masters = (attend_in, attend_out, expand_up, expand_down)
    firsts = (first_in, first_out, first_up, first_down)
    seconds = (second_in, second_out, second_up, second_down)
    terms = [adam_terms(grad, first, second) for grad, first, second in zip(grads[:4], firsts, seconds)]
    directions = [term[2] + DECAY * master for term, master in zip(terms, masters)]
    norm_pairs = jnp.sqrt(jnp.stack([weight_squares(masters), weight_squares(directions)], axis=1))
    trust = norm_pairs[:, 0] / norm_pairs[:, 1]
    factors = (trust[0:3].reshape(3, 1, 1), trust[3], trust[4], trust[5])
    updated = [master - RATE * factor * direction for master, factor, direction in zip(masters, factors, directions)]
    vector_moment, vector_square, vector_direction = adam_terms(grads[4], vector_first, vector_second)
    updated_vectors = vectors - RATE * vector_direction
    return (output.astype(jnp.bfloat16), states_grad, updated[0], updated[1], updated[2], updated[3], terms[0][0], terms[1][0], terms[2][0], terms[3][0], terms[0][1], terms[1][1], terms[2][1], terms[3][1], updated[0].astype(jnp.bfloat16), updated[1].astype(jnp.bfloat16), updated[2].astype(jnp.bfloat16), updated[3].astype(jnp.bfloat16), updated_vectors, vector_moment, vector_square, norm_pairs)
```

```python
import math

import jax
import jax.numpy as jnp
import numpy as np
from jax import lax
from jax.experimental import pallas as pl
from jax.experimental.pallas import tpu as pltpu
from jax.sharding import PartitionSpec as P

HEAD_DIM = 64
STEP = 10
NORM_EPS = 1e-05
BETA_ONE = 0.9
BETA_TWO = 0.999
ADAM_EPS = 1e-06
RATE = 0.3
DECAY = 0.01
MASKED = -1e30
AXES = ("dp", "tensor")
F32, BF16 = jnp.float32, jnp.bfloat16
VMEM = pltpu.VMEM
LANES = 128
NT = (((1,), (1,)), ((), ()))
TN = (((0,), (0,)), ((), ()))
MIB = 1 << 20


class Grid:
    def __init__(self, mesh):
        self.dp, self.cores = mesh.shape["dp"], mesh.shape["tensor"]
        chips = mesh.devices.reshape(self.dp, self.cores)[:, 0]
        spots = [tuple(getattr(chip, "coords", ())) for chip in chips]
        if any(len(spot) != 3 for spot in spots) or len(set(spots)) != self.dp:
            side = 1 << ((self.dp.bit_length() - 1) // 3)
            spots = [(i % side, i // side % side, i // (side * side)) for i in range(self.dp)]
        spots = np.array(spots) - np.min(spots, axis=0)
        sizes = spots.max(axis=0) + 1
        order = sorted(range(3), key=lambda k: -sizes[k])
        order = order[:1] + sorted(order[1:])
        self.spots = spots[:, order].tolist()
        self.long, self.side, _ = (int(sizes[k]) for k in order)
        self.at = {tuple(spot): i for i, spot in enumerate(self.spots)}
        unit = [tuple(int(j == k) for j in range(3)) for k in range(3)]
        self.stride = [self.at.get(u, 0) for u in unit]
        self.sizes = [int(sizes[k]) for k in order]

    def send(self, value, hop):
        pairs = []
        for i, spot in enumerate(self.spots):
            for core in range(self.cores):
                offsets, turn = hop(core)
                target = self.at[tuple(u ^ v for u, v in zip(spot, offsets))]
                pairs.append((i * self.cores + core, target * self.cores + (core ^ turn)))
        return lax.ppermute(value, AXES, pairs)

    def place(self):
        index = lax.axis_index("dp")
        spot = [lax.rem(lax.div(index, s), n) if n > 1 else index * 0 for s, n in zip(self.stride, self.sizes)]
        return jnp.stack(spot + [lax.axis_index("tensor")]).astype(jnp.int32)

    def first(self, k):
        return lambda core: ((0, k, 0) if core == 0 else (0, 0, k), 0)

    def second(self, k):
        return lambda core: ((0, 0, k) if core == 0 else (0, k, 0), 0)

    def along(self, k):
        return lambda core: ((k, 0, 0), 0)

    def cross(self, j, k):
        return lambda core: ((0, j, k), 0)

    def core(self, value):
        return self.send(value, lambda core: ((0, 0, 0), 1))

    def slot(self, s, k, m, a):
        zero = s[3] == 0
        b = s[1] ^ jnp.where(zero, k, m)
        c = s[2] ^ jnp.where(zero, m, k)
        return self.stride[0] * a + self.stride[1] * b + self.stride[2] * c


def kernel_call(body, outs, ins, place=None, limit=4, flops=0, moved=0, exps=0, scratch=(), spill=()):
    specs = [pl.BlockSpec(memory_space=VMEM)] * len(ins)
    ins = [pltpu.with_memory_space_constraint(v, VMEM) for v in ins]
    if place is not None:
        specs = [pl.BlockSpec(memory_space=pltpu.SMEM)] + specs
        ins = [place] + ins
    shapes = [
        jax.ShapeDtypeStruct(s, d) if i in spill else VMEM(s, d) for i, (s, d) in enumerate(outs)
    ]
    return pl.pallas_call(
        body,
        out_shape=shapes,
        in_specs=specs,
        out_specs=[pl.BlockSpec(memory_space=VMEM)] * len(outs),
        scratch_shapes=list(scratch),
        cost_estimate=pl.CostEstimate(flops=flops, bytes_accessed=moved, transcendentals=exps),
        compiler_params=pltpu.CompilerParams(vmem_limit_bytes=limit * MIB),
    )(*ins)


def gather(grid, place, shard):
    long, side = grid.long, grid.side
    many, rows, width = shard.shape
    got = [shard] + [grid.send(shard, grid.along(k)) for k in range(1, long)]

    def line(s, *refs):
        for k in range(long):
            refs[-1][s[0] ^ k] = refs[k][...]

    block = kernel_call(line, [((long, many, rows, width), BF16)], got, place)[0]
    pieces = {(0, 0): block}
    for k in range(1, side):
        pieces[k, 0] = grid.send(block, grid.first(k))
    for m in range(1, side):
        for k in range(side):
            pieces[k, m] = grid.send(pieces[k, 0], grid.second(m))
    keys = list(pieces)

    def whole(s, *refs):
        for (k, m), ref in zip(keys, refs[:-1]):
            for a in range(long):
                spot = grid.slot(s, k, m, a)
                for j in range(many):
                    refs[-1][j, spot] = ref[a, j]

    full = kernel_call(
        whole, [((many, grid.dp, rows, width), BF16)], [pieces[key] for key in keys], place
    )[0]
    return full, grid.core(full)


def scatter(grid, place, own, other):
    long, side = grid.long, grid.side
    many, _, rows, width = own.shape
    got = grid.core(other)
    block = (side, long, many, rows, width)

    def pair(s, own_ref, got_ref, keep, *sends):
        for m in range(side):
            out = keep if m == 0 else sends[m - 1]
            for k in range(side):
                for a in range(long):
                    spot = grid.slot(s, k, m, a)
                    for j in range(many):
                        total = own_ref[j, spot] + got_ref[j, spot].astype(F32)
                        out[k, a, j] = total.astype(out.dtype)

    keep, *sends = kernel_call(
        pair, [(block, F32)] + [(block, BF16)] * (side - 1), [own, got], place, limit=6
    )
    came = [grid.send(v, grid.second(m + 1)) for m, v in enumerate(sends)]

    def sides(*refs):
        came_refs, outs = refs[1:side], refs[side:]
        for k in range(side):
            total = refs[0][k]
            for ref in came_refs:
                total = total + ref[k].astype(F32)
            outs[k][...] = total.astype(outs[k].dtype)

    keep, *sends = kernel_call(
        sides, [(block[1:], F32)] + [(block[1:], BF16)] * (side - 1), [keep] + came, limit=6
    )
    came = [grid.send(v, grid.first(k + 1)) for k, v in enumerate(sends)]

    def line(s, *refs):
        outs = refs[side:]
        for k in range(long):
            total = refs[0][s[0] ^ k]
            for ref in refs[1:side]:
                total = total + ref[s[0] ^ k].astype(F32)
            outs[k][...] = total.astype(outs[k].dtype)

    keep, *sends = kernel_call(
        line, [(block[2:], F32)] + [(block[2:], BF16)] * (long - 1), [keep] + came, place
    )
    return [keep] + [grid.send(v, grid.along(k + 1)) for k, v in enumerate(sends)]


def tree(values):
    values = list(values)
    while len(values) > 1:
        values = [a + b for a, b in zip(values[::2], values[1::2])]
    return values[0]


def add_kernel(*refs):
    refs[-1][...] = tree(ref[...] for ref in refs[:-1])


def total_of(grid, value):
    shape = [(value.shape, F32)]
    value = kernel_call(
        add_kernel, shape, [value] + [grid.send(value, grid.along(k)) for k in range(1, grid.long)]
    )[0]
    offsets = [(j, k) for j in range(grid.side) for k in range(grid.side)]
    value = kernel_call(
        add_kernel, shape, [value] + [grid.send(value, grid.cross(j, k)) for j, k in offsets[1:]]
    )[0]
    return value, grid.core(value)


def normed_of(values):
    center = values - jnp.mean(values, axis=-1, keepdims=True)
    inverse = lax.rsqrt(jnp.mean(center * center, axis=-1, keepdims=True) + NORM_EPS)
    return center * inverse, inverse


def norm_back(upstream, normed, inverse, gain):
    scaled = upstream * gain
    inner = jnp.mean(scaled * normed, axis=-1, keepdims=True)
    return inverse * (scaled - jnp.mean(scaled, axis=-1, keepdims=True) - normed * inner)


def sum_rows(values):
    return jnp.sum(values, axis=0, keepdims=True)


def adam(grad, first, second):
    first_new = BETA_ONE * first + (1.0 - BETA_ONE) * grad
    second_new = BETA_TWO * second + (1.0 - BETA_TWO) * grad * grad
    corrected = first_new / (1.0 - BETA_ONE**STEP)
    spread = jnp.sqrt(second_new / (1.0 - BETA_TWO**STEP))
    return first_new, second_new, corrected / (spread + ADAM_EPS)


def squares(values):
    return jnp.sum(sum_rows(values * values), axis=1, keepdims=True)


def norm_tile(entries):
    row = lax.broadcasted_iota(jnp.int32, (8, LANES), 0)
    lane = lax.broadcasted_iota(jnp.int32, (8, LANES), 1)
    tile = jnp.zeros((8, LANES), F32)
    for index, weight, direction in entries:
        tile = jnp.where((row == index) & (lane == 0), squares(weight), tile)
        tile = jnp.where((row == index) & (lane == 1), squares(direction), tile)
    return tile


def make_body(grid):
    def body(
        states, cotangent, word_counts, region_counts,
        attend_in, attend_out, expand_up, expand_down,
        first_in, first_out, first_up, first_down,
        second_in, second_out, second_up, second_down,
        vectors, vector_first, vector_second,
    ):
        cores = grid.cores
        pairs, length, width = states.shape
        mine = pairs // cores
        rows = mine * length
        cols = attend_in.shape[2]
        units = expand_up.shape[1]
        twins = width // LANES
        scale = HEAD_DIM**-0.5
        place = grid.place()
        rank = place[3]
        shard_rows = attend_in.shape[1]

        shard_a = jnp.concatenate([attend_in, attend_out.T[None]]).astype(BF16)
        a_own, a_oth = gather(grid, place, shard_a)
        b_own, b_oth = gather(grid, place, expand_up.astype(BF16)[None])
        c_own, c_oth = gather(grid, place, expand_down.astype(BF16)[None])
        a_own, a_oth = (v.reshape(4, width, cols) for v in (a_own, a_oth))
        b_own, b_oth = (v.reshape(width, units) for v in (b_own, b_oth))
        c_own, c_oth = (v.reshape(units, width) for v in (c_own, c_oth))

        part = lambda v: lax.dynamic_slice_in_dim(v, rank * mine, mine, 0)
        x = part(states).reshape(rows, width)
        cot = part(cotangent).reshape(rows, width)
        lengths = part(word_counts + region_counts)

        def turned(v):
            return jnp.where(rank == 0, v, jnp.roll(v, v.shape[-1] // 2, axis=-1))

        bias_up = turned(vectors[8:].reshape(1, -1))
        bias_in = turned(jnp.stack([vectors[0], jnp.zeros_like(vectors[0]), vectors[1]])).reshape(3, 1, width)

        def project(x_ref, own, oth, bias, out, x_t):
            x_t[...] = x_ref[...].T

            @pl.loop(0, 3)
            def _(j):
                for h, ref in enumerate((own, oth)):
                    at = slice(h * cols, (h + 1) * cols)
                    value = jnp.dot(x_ref[...], ref[j], preferred_element_type=F32)
                    out[j, :, at] = (value + bias[j, :, at]).astype(BF16)

        qkv, x_t = kernel_call(
            project, [((3, rows, width), BF16), ((width, rows), BF16)], [x, a_own, a_oth, bias_in],
            limit=8, flops=6 * rows * width * width, moved=8 * MIB,
        )

        def split(v):
            low = lax.broadcasted_iota(jnp.int32, v.shape, 1) < HEAD_DIM
            zero = jnp.zeros_like(v)
            return jnp.concatenate([jnp.where(low, v, zero), jnp.where(low, zero, v)], axis=0)

        def join(v):
            low = lax.broadcasted_iota(jnp.int32, (length, LANES), 1) < HEAD_DIM
            return jnp.where(low, v[:length], v[length:])

        def attend(count, qkv_ref, probs, context):
            @pl.loop(0, mine)
            def _(p):
                at = pl.ds(pl.multiple_of(p * length, length), length)
                known = lax.broadcasted_iota(jnp.int32, (length, length), 1) < count[p]
                for u in range(twins):
                    lanes = slice(u * LANES, (u + 1) * LANES)
                    both = lax.dot_general(
                        qkv_ref[0, at, lanes], split(qkv_ref[1, at, lanes]), NT, preferred_element_type=F32
                    )
                    soft = []
                    for h in range(2):
                        score = jnp.where(known, both[:, h * length : (h + 1) * length] * scale, MASKED)
                        power = jnp.exp(score - jnp.max(score, axis=-1, keepdims=True))
                        soft.append(power / jnp.sum(power, axis=-1, keepdims=True))
                    prob = jnp.concatenate(soft, axis=1).astype(BF16)
                    probs[at, 2 * u * length : 2 * (u + 1) * length] = prob
                    context[at, lanes] = jnp.dot(
                        prob, split(qkv_ref[2, at, lanes]), preferred_element_type=F32
                    ).astype(BF16)

        probs, context = kernel_call(
            attend, [((rows, 2 * twins * length), BF16), ((rows, width), BF16)], [qkv], lengths,
            limit=4, flops=4 * rows * length * width * 4, moved=5 * MIB, exps=rows * twins * 2 * length,
        )

        block = min(rows, 256)

        def hide(context_ref, x_ref, own, oth, vec, hidden, hidden_t, normed, inverse):
            for r in range(0, rows, block):
                at = slice(r, r + block)
                value = x_ref[at].astype(F32) + vec[2:3]
                for h, ref in enumerate((own, oth)):
                    value += lax.dot_general(
                        context_ref[at, h * cols : (h + 1) * cols], ref[3], NT, preferred_element_type=F32
                    )
                normal, spread = normed_of(value)
                normed[at], inverse[at] = normal, spread
                hidden[at] = (normal * vec[3:4] + vec[4:5]).astype(BF16)
            hidden_t[...] = hidden[...].T

        hidden, hidden_t, normed_one, inverse_one = kernel_call(
            hide,
            [((rows, width), BF16), ((width, rows), BF16), ((rows, width), F32), ((rows, 1), F32)],
            [context, x, a_own, a_oth, vectors],
            limit=8, flops=2 * rows * width * width, moved=6 * MIB,
        )

        tile = 256

        def lift(hidden_ref, up, bias, active, active_t, slope):
            @pl.loop(0, units // tile)
            def _(i):
                at = pl.ds(pl.multiple_of(i * tile, tile), tile)
                value = jnp.dot(hidden_ref[...], up[:, at], preferred_element_type=F32) + bias[:, at]
                half = 0.5 * (1.0 + lax.erf(value * math.sqrt(0.5)))
                result = (value * half).astype(BF16)
                active[:, at] = result
                active_t[at, :] = result.T
                bell = jnp.exp(-0.5 * value * value) * (1.0 / math.sqrt(2.0 * math.pi))
                slope[:, at] = (half + value * bell).astype(BF16)

        lifted = [
            kernel_call(
                lift, [((rows, units), BF16), ((units, rows), BF16), ((rows, units), BF16)],
                [hidden, up, bias_up[:, h * units : (h + 1) * units]],
                limit=8, flops=2 * rows * width * units, moved=8 * MIB, exps=2 * rows * units,
            )
            for h, up in enumerate((b_own, b_oth))
        ]

        def lower(count, active_own, active_oth, own, oth, normed, cot_ref, vec, output, top, top16, sums, work):
            @pl.loop(0, width // tile)
            def _(i):
                at = pl.ds(pl.multiple_of(i * tile, tile), tile)
                work[:, at] = jnp.dot(active_own[...], own[:, at], preferred_element_type=F32) + jnp.dot(
                    active_oth[...], oth[:, at], preferred_element_type=F32
                )

            sums[...] = jnp.zeros_like(sums)

            @pl.loop(0, mine)
            def _(p):
                at = pl.ds(pl.multiple_of(p * length, length), length)
                value = normed[at] * vec[3:4] + vec[4:5] + work[at] + vec[5:6]
                normal, spread = normed_of(value)
                output[at] = (normal * vec[6:7] + vec[7:8]).astype(BF16)
                live = lax.broadcasted_iota(jnp.int32, (length, 1), 0) < count[p]
                upstream = jnp.where(live, cot_ref[at].astype(F32), 0.0)
                grad = norm_back(upstream, normal, spread, vec[6:7])
                top[at] = grad
                top16[at] = grad.astype(BF16)
                sums[0:1] += sum_rows(grad)
                sums[1:2] += sum_rows(upstream * normal)
                sums[2:3] += sum_rows(upstream)

        output, top, top16, sums_two = kernel_call(
            lower,
            [((rows, width), BF16), ((rows, width), F32), ((rows, width), BF16), ((8, width), F32)],
            [lifted[0][0], lifted[1][0], c_own, c_oth, normed_one, cot, vectors],
            lengths, limit=8, flops=4 * rows * width * units, moved=14 * MIB,
            scratch=[VMEM((rows, width), F32)],
        )

        def product(left, right, out):
            step = min(left.shape[0], 256)

            @pl.loop(0, left.shape[0] // step)
            def _(i):
                at = pl.ds(pl.multiple_of(i * step, step), step)
                out[at, :] = jnp.dot(left[at, :], right[...], preferred_element_type=F32).astype(out.dtype)

        def weight_grad(left, right, kind):
            shape = (left.shape[0], right.shape[1])
            return kernel_call(
                product, [(shape, kind)], [left, right],
                limit=6, flops=2 * shape[0] * shape[1] * rows, moved=8 * MIB,
            )[0]

        down_oth = weight_grad(lifted[1][1], top16, BF16)
        down_own = weight_grad(lifted[0][1], top16, F32)
        sharded = lambda v, many: v.reshape(many, grid.dp, -1, v.shape[-1])
        down_parts = scatter(grid, place, sharded(down_own, 1), sharded(down_oth, 1))

        def sink(top16_ref, down, slope, grad, sums):
            @pl.loop(0, units // tile)
            def _(i):
                at = pl.ds(pl.multiple_of(i * tile, tile), tile)
                value = lax.dot_general(top16_ref[...], down[at, :], NT, preferred_element_type=F32)
                value = value * slope[:, at].astype(F32)
                grad[:, at] = value.astype(BF16)
                sums[:, at] = sum_rows(value)

        sunk = [
            kernel_call(
                sink, [((rows, units), BF16), ((1, units), F32)], [top16, down, lifted[h][2]],
                limit=8, flops=2 * rows * width * units, moved=8 * MIB,
            )
            for h, down in enumerate((c_own, c_oth))
        ]
        up_oth = weight_grad(hidden_t, sunk[1][0], BF16)
        up_own = weight_grad(hidden_t, sunk[0][0], F32)
        up_parts = scatter(grid, place, sharded(up_own, 1), sharded(up_oth, 1))

        def surface(grad_own, grad_oth, own, oth, top_ref, normed, inverse, vec, a_own_ref, a_oth_ref,
                    mid, mid_t, back, sums, work, mid16):
            @pl.loop(0, width // tile)
            def _(i):
                at = pl.ds(pl.multiple_of(i * tile, tile), tile)
                work[:, at] = (
                    top_ref[:, at]
                    + lax.dot_general(grad_own[...], own[at, :], NT, preferred_element_type=F32)
                    + lax.dot_general(grad_oth[...], oth[at, :], NT, preferred_element_type=F32)
                )

            sums[...] = jnp.zeros_like(sums)

            @pl.loop(0, mine)
            def _(p):
                at = pl.ds(pl.multiple_of(p * length, length), length)
                upstream, normal = work[at], normed[at]
                grad = norm_back(upstream, normal, inverse[at], vec[3:4])
                mid[at] = grad
                mid16[at] = grad.astype(BF16)
                sums[0:1] += sum_rows(grad)
                sums[1:2] += sum_rows(upstream * normal)
                sums[2:3] += sum_rows(upstream)

            mid_t[...] = mid16[...].T
            for h, ref in enumerate((a_own_ref, a_oth_ref)):
                back[:, h * cols : (h + 1) * cols] = jnp.dot(
                    mid16[...], ref[3], preferred_element_type=F32
                ).astype(BF16)

        mid, mid_t, back, sums_one = kernel_call(
            surface,
            [((rows, width), F32), ((width, rows), BF16), ((rows, width), BF16), ((8, width), F32)],
            [sunk[0][0], sunk[1][0], b_own, b_oth, top, normed_one, inverse_one, vectors, a_own, a_oth],
            limit=14, flops=4 * rows * width * units + 2 * rows * width * width, moved=14 * MIB,
            scratch=[VMEM((rows, width), F32), VMEM((rows, width), BF16)],
        )

        def values_back(probs_ref, back_ref, grad, sums):
            sums[...] = jnp.zeros_like(sums)

            @pl.loop(0, mine)
            def _(p):
                at = pl.ds(pl.multiple_of(p * length, length), length)
                for u in range(twins):
                    lanes = slice(u * LANES, (u + 1) * LANES)
                    value = join(lax.dot_general(
                        probs_ref[at, 2 * u * length : 2 * (u + 1) * length], back_ref[at, lanes], TN,
                        preferred_element_type=F32,
                    ))
                    grad[at, lanes] = value.astype(BF16)
                    sums[:, lanes] += sum_rows(value)

        grad_v, sum_v = kernel_call(
            values_back, [((rows, width), BF16), ((1, width), F32)], [probs, back],
            limit=4, flops=4 * rows * length * width, moved=3 * MIB,
        )

        def halves(left_v, right_v, h, kind, left_w, right_w):
            def both(left_v_ref, right_v_ref, left_w_ref, right_w_ref, out):
                at = slice(h * cols, (h + 1) * cols)
                for j, (left, right) in enumerate(((left_v_ref, right_v_ref), (left_w_ref, right_w_ref))):
                    out[j] = jnp.dot(left[...], right[:, at], preferred_element_type=F32).astype(out.dtype)

            return kernel_call(
                both, [((2, width, cols), kind)], [left_v, right_v, left_w, right_w],
                limit=6, flops=4 * rows * width * cols, moved=5 * MIB,
            )[0]

        vo_oth = halves(x_t, grad_v, 1, BF16, mid_t, context)
        vo_own = halves(x_t, grad_v, 0, F32, mid_t, context)
        vo_parts = scatter(grid, place, sharded(vo_own, 2), sharded(vo_oth, 2))

        def attend_back(probs_ref, back_ref, qkv_ref, grad_q, grad_k, sums):
            sums[...] = jnp.zeros_like(sums)

            @pl.loop(0, mine)
            def _(p):
                at = pl.ds(pl.multiple_of(p * length, length), length)
                for u in range(twins):
                    lanes = slice(u * LANES, (u + 1) * LANES)
                    prob = probs_ref[at, 2 * u * length : 2 * (u + 1) * length].astype(F32)
                    both = lax.dot_general(
                        back_ref[at, lanes], split(qkv_ref[2, at, lanes]), NT, preferred_element_type=F32
                    )
                    parts = []
                    for h in range(2):
                        half = slice(h * length, (h + 1) * length)
                        inner = jnp.sum(prob[:, half] * both[:, half], axis=-1, keepdims=True)
                        parts.append(prob[:, half] * (both[:, half] - inner))
                    grad = jnp.concatenate(parts, axis=1).astype(BF16)
                    value = jnp.dot(grad, split(qkv_ref[1, at, lanes]), preferred_element_type=F32) * scale
                    grad_q[at, lanes] = value.astype(BF16)
                    sums[:, lanes] += sum_rows(value)
                    value = join(lax.dot_general(grad, qkv_ref[0, at, lanes], TN, preferred_element_type=F32))
                    grad_k[at, lanes] = (value * scale).astype(BF16)

        grad_q, grad_k, sum_q = kernel_call(
            attend_back, [((rows, width), BF16), ((rows, width), BF16), ((1, width), F32)], [probs, back, qkv],
            limit=4, flops=16 * rows * length * width, moved=6 * MIB,
        )
        qk_oth = halves(x_t, grad_q, 1, BF16, x_t, grad_k)
        qk_own = halves(x_t, grad_q, 0, F32, x_t, grad_k)
        qk_parts = scatter(grid, place, sharded(qk_own, 2), sharded(qk_oth, 2))

        def states_back(grad_q_ref, grad_k_ref, grad_v_ref, own, oth, mid_ref, out):
            @pl.loop(0, width // tile)
            def _(i):
                at = pl.ds(pl.multiple_of(i * tile, tile), tile)
                value = mid_ref[:, at]
                for j, ref in enumerate((grad_q_ref, grad_k_ref, grad_v_ref)):
                    for h, weight in enumerate((own, oth)):
                        value += lax.dot_general(
                            ref[:, h * cols : (h + 1) * cols], weight[j, at, :], NT, preferred_element_type=F32
                        )
                out[:, at] = value

        states_own = kernel_call(
            states_back, [((rows, width), F32)], [grad_q, grad_k, grad_v, a_own, a_oth, mid],
            limit=8, flops=6 * rows * width * width, moved=8 * MIB,
        )[0]

        def pair_up(s, own, oth, out):
            out[s[3]] = own[...]
            out[1 - s[3]] = oth[...]

        def paired(value):
            shape = ((cores,) + value.shape, value.dtype)
            result = kernel_call(pair_up, [shape], [value, grid.core(value)], place, limit=8, spill=(0,))[0]
            return result.reshape(pairs, length, width)

        layer_output = paired(output)
        states_grad = paired(states_own)

        def collect(s, sum_q_ref, sum_v_ref, one, two, up_own_ref, up_oth_ref, out):
            for t in range(cores):

                @pl.when(s[3] == t)
                def _():
                    for row, ref in enumerate((sum_q_ref, sum_v_ref)):
                        for h in range(2):
                            out[row : row + 1, (h ^ t) * cols : ((h ^ t) + 1) * cols] = ref[
                                :, h * cols : (h + 1) * cols
                            ]
                    for h, ref in enumerate((up_own_ref, up_oth_ref)):
                        for i in range(units // width):
                            row = 8 + (h ^ t) * (units // width) + i
                            out[row : row + 1] = ref[:, i * width : (i + 1) * width]

            out[2:5] = one[0:3]
            out[5:8] = two[0:3]

        vector_part = kernel_call(
            collect, [(vectors.shape, F32)], [sum_q, sum_v, sums_one, sums_two, sunk[0][1], sunk[1][1]], place
        )[0]
        vector_own, vector_oth = total_of(grid, vector_part)

        def vector_step(own, oth, vec, first, second, out, moment, square):
            one, two, direction = adam(own[...] + oth[...], first[...], second[...])
            moment[...], square[...] = one, two
            out[...] = vec[...] - RATE * direction

        updated_vectors, moment_vectors, square_vectors = kernel_call(
            vector_step, [(vectors.shape, F32)] * 3,
            [vector_own, vector_oth, vectors, vector_first, vector_second], spill=(0, 1, 2),
        )

        def matrix_step(index):
            def step(*refs):
                grad = sum((ref[0].astype(F32) for ref in refs[1 : grid.long]), refs[0][0])
                master, first, second, moment, square, direction, tile_ref = refs[grid.long :]
                one, two, way = adam(grad, first[...], second[...])
                way = way + DECAY * master[...]
                moment[...], square[...], direction[...] = one, two, way
                tile_ref[...] = norm_tile([(index, master[...], way)])

            return step

        def stepped(step, parts, masters, shapes):
            outs = [(s, F32) for s in shapes for _ in range(2)] + [(s, F32) for s in shapes] + [((8, LANES), F32)]
            return kernel_call(step, outs, parts + masters, limit=6, spill=tuple(range(2 * len(shapes))))

        moment_down, square_down, way_down, tile_down = stepped(
            matrix_step(5), down_parts, [expand_down, first_down, second_down], [expand_down.shape]
        )
        moment_up, square_up, way_up, tile_up = stepped(
            matrix_step(4), up_parts, [expand_up, first_up, second_up], [expand_up.shape]
        )

        def attend_step(*refs):
            n = grid.long
            vo, qk = refs[:n], refs[n : 2 * n]
            m_in, f_in, s_in, m_out, f_out, s_out = refs[2 * n : 2 * n + 6]
            mo_in, sq_in, mo_out, sq_out, way_in, way_out, tile_ref = refs[2 * n + 6 :]
            whole = lambda parts, j: sum((ref[j].astype(F32) for ref in parts[1:]), parts[0][j])
            entries = []
            for j, grad in enumerate((whole(qk, 0), whole(qk, 1), whole(vo, 0))):
                mo_in[j], sq_in[j], way = adam(grad, f_in[j], s_in[j])
                way_in[j] = way + DECAY * m_in[j]
                entries.append((j, m_in[j], way_in[j]))
            mo_out[...], sq_out[...], way = adam(whole(vo, 1).T, f_out[...], s_out[...])
            way_out[...] = way + DECAY * m_out[...]
            entries.append((3, m_out[...], way_out[...]))
            tile_ref[...] = norm_tile(entries)

        moment_in, square_in, moment_out, square_out, way_in, way_out, tile_attend = stepped(
            attend_step, vo_parts + qk_parts,
            [attend_in, first_in, second_in, attend_out, first_out, second_out],
            [attend_in.shape, attend_out.shape],
        )

        def add_tiles(*refs):
            refs[-1][...] = refs[0][...] + refs[1][...] + refs[2][...]

        tiles = kernel_call(add_tiles, [((8, LANES), F32)], [tile_attend, tile_up, tile_down])[0]
        tile_own, tile_oth = total_of(grid, tiles)

        def update(own, oth, *refs):
            masters, ways, outs = refs[:4], refs[4:8], refs[8:]
            norms = jnp.sqrt(own[...] + oth[...])
            outs[8][...] = norms[0:6, 0:2]
            trust = RATE * (norms[:, 0:1] / norms[:, 1:2])
            for j in range(3):
                value = masters[0][j] - trust[j : j + 1] * ways[0][j]
                outs[0][j], outs[4][j] = value, value.astype(BF16)
            for i in range(1, 4):
                value = masters[i][...] - trust[i + 2 : i + 3] * ways[i][...]
                outs[i][...], outs[4 + i][...] = value, value.astype(BF16)

        masters = [attend_in, attend_out, expand_up, expand_down]
        results = kernel_call(
            update,
            [(m.shape, F32) for m in masters] + [(m.shape, BF16) for m in masters] + [((6, 2), F32)],
            [tile_own, tile_oth] + masters + [way_in, way_out, way_up, way_down],
            limit=6, spill=tuple(range(9)),
        )
        return (
            layer_output, states_grad, *results[:4],
            moment_in, moment_out, moment_up, moment_down,
            square_in, square_out, square_up, square_down,
            *results[4:8], updated_vectors, moment_vectors, square_vectors, results[8],
        )

    return body


def solution(mesh):
    rows = P("dp", None, None)
    matrices = (P(None, "dp", "tensor"), P("tensor", "dp"), P("dp", "tensor"), P(("tensor", "dp"), None))
    in_specs = (rows, rows, P("dp"), P("dp")) + matrices * 3 + (P(), P(), P())
    out_specs = (rows, rows) + matrices * 4 + (P(), P(), P(), P())
    body = make_body(Grid(mesh))
    return jax.shard_map(body, mesh=mesh, in_specs=in_specs, out_specs=out_specs, check_vma=False)
```

```python
import math

import jax
import jax.numpy as jnp
import numpy as np
from jax import lax
from jax.experimental import pallas as pl
from jax.experimental.pallas import tpu as pltpu
from jax.sharding import PartitionSpec as P

HEAD_DIM = 64
STEP = 10
NORM_EPS = 1e-05
BETA_ONE = 0.9
BETA_TWO = 0.999
ADAM_EPS = 1e-06
RATE = 0.3
DECAY = 0.01
MASKED = -1e30
AXES = ("dp", "tensor")
F32, BF16 = jnp.float32, jnp.bfloat16
VMEM = pltpu.VMEM
LANES = 128
NT = (((1,), (1,)), ((), ()))
TN = (((0,), (0,)), ((), ()))
MIB = 1 << 20


class Grid:
    def __init__(self, mesh):
        self.dp, self.cores = mesh.shape["dp"], mesh.shape["tensor"]
        chips = mesh.devices.reshape(self.dp, self.cores)[:, 0]
        spots = [tuple(getattr(chip, "coords", ())) for chip in chips]
        if any(len(spot) != 3 for spot in spots) or len(set(spots)) != self.dp:
            side = 1 << ((self.dp.bit_length() - 1) // 3)
            spots = [(i % side, i // side % side, i // (side * side)) for i in range(self.dp)]
        spots = np.array(spots) - np.min(spots, axis=0)
        sizes = spots.max(axis=0) + 1
        order = sorted(range(3), key=lambda k: -sizes[k])
        order = order[:1] + sorted(order[1:])
        self.spots = spots[:, order].tolist()
        self.long, self.side, _ = (int(sizes[k]) for k in order)
        self.at = {tuple(spot): i for i, spot in enumerate(self.spots)}
        unit = [tuple(int(j == k) for j in range(3)) for k in range(3)]
        self.stride = [self.at.get(u, 0) for u in unit]
        self.sizes = [int(sizes[k]) for k in order]

    def send(self, value, hop):
        pairs = []
        for i, spot in enumerate(self.spots):
            for core in range(self.cores):
                offsets, turn = hop(core)
                target = self.at[tuple(u ^ v for u, v in zip(spot, offsets))]
                pairs.append((i * self.cores + core, target * self.cores + (core ^ turn)))
        return lax.ppermute(value, AXES, pairs)

    def place(self):
        index = lax.axis_index("dp")
        spot = [lax.rem(lax.div(index, s), n) if n > 1 else index * 0 for s, n in zip(self.stride, self.sizes)]
        return jnp.stack(spot + [lax.axis_index("tensor")]).astype(jnp.int32)

    def first(self, k):
        return lambda core: ((0, k, 0) if core == 0 else (0, 0, k), 0)

    def second(self, k):
        return lambda core: ((0, 0, k) if core == 0 else (0, k, 0), 0)

    def along(self, k):
        return lambda core: ((k, 0, 0), 0)

    def cross(self, j, k):
        return lambda core: ((0, j, k), 0)

    def core(self, value):
        return self.send(value, lambda core: ((0, 0, 0), 1))

    def slot(self, s, k, m, a):
        zero = s[3] == 0
        b = s[1] ^ jnp.where(zero, k, m)
        c = s[2] ^ jnp.where(zero, m, k)
        return self.stride[0] * a + self.stride[1] * b + self.stride[2] * c


class Tape:
    def __init__(self, place):
        self.place = place
        self.token = None

    def run(self, body, outs, ins, place=False, limit=4, flops=0, moved=0, exps=0, scratch=(), spill=(), plain=(), name=None):
        ins = [v if i in plain else pltpu.with_memory_space_constraint(v, VMEM) for i, v in enumerate(ins)]
        specs = [pl.BlockSpec(memory_space=VMEM)] * len(ins)
        first = []
        if place:
            first.append((self.place, pltpu.SMEM))
        if self.token is not None:
            first.append((pltpu.with_memory_space_constraint(self.token, VMEM), VMEM))
        chained = self.token is not None
        count, results = len(ins), len(outs)

        def chain(*refs):
            refs = list(refs)
            head = [refs.pop(0)] if place else []
            if chained:
                refs.pop(0)
            last = refs.pop(count + results)
            last[...] = jnp.zeros_like(last)
            body(*head, *refs)

        shapes = [
            jax.ShapeDtypeStruct(s, d) if i in spill else VMEM(s, d) for i, (s, d) in enumerate(outs)
        ] + [VMEM((8, LANES), F32)]
        *values, self.token = pl.pallas_call(
            chain,
            out_shape=shapes,
            in_specs=[pl.BlockSpec(memory_space=m) for _, m in first] + specs,
            out_specs=[pl.BlockSpec(memory_space=VMEM)] * len(shapes),
            scratch_shapes=list(scratch),
            name=name or body.__name__,
            cost_estimate=pl.CostEstimate(flops=flops, bytes_accessed=moved, transcendentals=exps),
            compiler_params=pltpu.CompilerParams(vmem_limit_bytes=limit * MIB),
        )(*[v for v, _ in first], *ins)
        return values


class Gather:
    def __init__(self, grid, tape, shard):
        self.grid, self.tape = grid, tape
        self.many, self.rows, self.width = shard.shape
        self.got = [shard] + [grid.send(shard, grid.along(k)) for k in range(1, grid.long)]

    def line(self):
        grid = self.grid
        long, side = grid.long, grid.side

        def body(s, *refs):
            for k in range(long):
                refs[-1][s[0] ^ k] = refs[k][...]

        block = self.tape.run(body, [((long, self.many, self.rows, self.width), BF16)], self.got, True)[0]
        self.pieces = {(0, 0): block}
        for k in range(1, side):
            self.pieces[k, 0] = grid.send(block, grid.first(k))
        for m in range(1, side):
            for k in range(side):
                self.pieces[k, m] = grid.send(self.pieces[k, 0], grid.second(m))

    def whole(self):
        grid = self.grid
        keys = list(self.pieces)

        def body(s, *refs):
            for (k, m), ref in zip(keys, refs[:-1]):
                for a in range(grid.long):
                    spot = grid.slot(s, k, m, a)
                    for j in range(self.many):
                        refs[-1][j, spot] = ref[a, j]

        full = self.tape.run(
            body, [((self.many, grid.dp, self.rows, self.width), BF16)], [self.pieces[key] for key in keys], True
        )[0]
        return full, grid.core(full)


class Scatter:
    def __init__(self, grid, tape, other):
        self.grid, self.tape = grid, tape
        self.many, _, self.rows, self.width = other.shape
        self.got = grid.core(other)
        self.block = (grid.side, grid.long, self.many, self.rows, self.width)

    def pair(self, own):
        grid, side = self.grid, self.grid.side

        def body(s, own_ref, got_ref, keep, *sends):
            for m in range(side):
                out = keep if m == 0 else sends[m - 1]
                for k in range(side):
                    for a in range(grid.long):
                        spot = grid.slot(s, k, m, a)
                        for j in range(self.many):
                            total = own_ref[j, spot] + got_ref[j, spot].astype(F32)
                            out[k, a, j] = total.astype(out.dtype)

        self.keep, *sends = self.tape.run(
            body, [(self.block, F32)] + [(self.block, BF16)] * (side - 1), [own, self.got], True
        )
        self.came = [grid.send(v, grid.second(m + 1)) for m, v in enumerate(sends)]

    def sides(self):
        grid, side = self.grid, self.grid.side

        def body(*refs):
            outs = refs[side:]
            for k in range(side):
                total = refs[0][k]
                for ref in refs[1:side]:
                    total = total + ref[k].astype(F32)
                outs[k][...] = total.astype(outs[k].dtype)

        shape = self.block[1:]
        self.keep, *sends = self.tape.run(
            body, [(shape, F32)] + [(shape, BF16)] * (side - 1), [self.keep] + self.came
        )
        self.came = [grid.send(v, grid.first(k + 1)) for k, v in enumerate(sends)]

    def line(self):
        grid, side, long = self.grid, self.grid.side, self.grid.long

        def body(s, *refs):
            outs = refs[side:]
            for k in range(long):
                total = refs[0][s[0] ^ k]
                for ref in refs[1:side]:
                    total = total + ref[s[0] ^ k].astype(F32)
                outs[k][...] = total.astype(outs[k].dtype)

        shape = self.block[2:]
        keep, *sends = self.tape.run(
            body, [(shape, F32)] + [(shape, BF16)] * (long - 1), [self.keep] + self.came, True
        )
        self.parts = [keep] + [grid.send(v, grid.along(k + 1)) for k, v in enumerate(sends)]


def tree(values):
    values = list(values)
    while len(values) > 1:
        values = [a + b for a, b in zip(values[::2], values[1::2])]
    return values[0]


class Total:
    def __init__(self, grid, tape, value):
        self.grid, self.tape = grid, tape
        self.got = [value] + [grid.send(value, grid.along(k)) for k in range(1, grid.long)]

    def add(self):
        def body(*refs):
            refs[-1][...] = tree(ref[...] for ref in refs[:-1])

        return self.tape.run(body, [(self.got[0].shape, F32)], self.got)[0]

    def line(self):
        grid, value = self.grid, self.add()
        offsets = [(j, k) for j in range(grid.side) for k in range(grid.side)]
        self.got = [value] + [grid.send(value, grid.cross(j, k)) for j, k in offsets[1:]]

    def sides(self):
        value = self.add()
        self.pair = [value, self.grid.core(value)]


def normed_of(values):
    center = values - jnp.mean(values, axis=-1, keepdims=True)
    inverse = lax.rsqrt(jnp.mean(center * center, axis=-1, keepdims=True) + NORM_EPS)
    return center * inverse, inverse


def norm_back(upstream, normed, inverse, gain):
    scaled = upstream * gain
    inner = jnp.mean(scaled * normed, axis=-1, keepdims=True)
    return inverse * (scaled - jnp.mean(scaled, axis=-1, keepdims=True) - normed * inner)


def sum_rows(values):
    return jnp.sum(values, axis=0, keepdims=True)


def adam(grad, first, second):
    first_new = BETA_ONE * first + (1.0 - BETA_ONE) * grad
    second_new = BETA_TWO * second + (1.0 - BETA_TWO) * grad * grad
    corrected = first_new / (1.0 - BETA_ONE**STEP)
    spread = jnp.sqrt(second_new / (1.0 - BETA_TWO**STEP))
    return first_new, second_new, corrected / (spread + ADAM_EPS)


def squares(values):
    return jnp.sum(sum_rows(values * values), axis=1, keepdims=True)


def norm_tile(entries):
    row = lax.broadcasted_iota(jnp.int32, (8, LANES), 0)
    lane = lax.broadcasted_iota(jnp.int32, (8, LANES), 1)
    tile = jnp.zeros((8, LANES), F32)
    for index, weight, direction in entries:
        tile = jnp.where((row == index) & (lane == 0), squares(weight), tile)
        tile = jnp.where((row == index) & (lane == 1), squares(direction), tile)
    return tile


def make_body(grid):
    def body(
        states, cotangent, word_counts, region_counts,
        attend_in, attend_out, expand_up, expand_down,
        first_in, first_out, first_up, first_down,
        second_in, second_out, second_up, second_down,
        vectors, vector_first, vector_second,
    ):
        cores = grid.cores
        pairs, length, width = states.shape
        mine = pairs // cores
        rows = mine * length
        cols = attend_in.shape[2]
        units = expand_up.shape[1]
        twins = width // LANES
        scale = HEAD_DIM**-0.5
        rank = lax.axis_index("tensor")
        counts = lax.dynamic_slice_in_dim(word_counts + region_counts, rank * mine, mine, 0)
        tape = Tape(jnp.concatenate([grid.place(), counts]))
        attend_out, first_out, second_out = (v.T[None] for v in (attend_out, first_out, second_out))

        def cast(*refs):
            spot = 0
            for ref in refs[:-1]:
                refs[-1][spot : spot + ref.shape[0]] = ref[...].astype(BF16)
                spot += ref.shape[0]

        def casted(*mats):
            many = sum(m.shape[0] for m in mats)
            shape = (many,) + mats[0].shape[1:]
            return tape.run(cast, [(shape, BF16)], mats, plain=range(len(mats)))[0]

        gather_a = Gather(grid, tape, casted(attend_in, attend_out))
        gather_b = Gather(grid, tape, casted(expand_up[None]))

        def prepare(s, states_ref, cot_ref, vec, x_ref, x_t, mine_cot, bias_in, bias_up):
            @pl.loop(0, mine)
            def _(p):
                at = pl.ds(pl.multiple_of(p * length, length), length)
                x_ref[at, :] = states_ref[s[3] * mine + p]
                mine_cot[at, :] = cot_ref[s[3] * mine + p]

            x_t[...] = x_ref[...].T
            bias_in[1:2] = jnp.zeros((1, width), F32)
            for t in range(cores):

                @pl.when(s[3] == t)
                def _():
                    for h in range(2):
                        at, source = slice(h * cols, (h + 1) * cols), slice((h ^ t) * cols, ((h ^ t) + 1) * cols)
                        bias_in[0:1, at] = vec[0:1, source]
                        bias_in[2:3, at] = vec[1:2, source]
                        for i in range(units // width):
                            row = 8 + (h ^ t) * (units // width) + i
                            spot = h * units + i * width
                            bias_up[:, spot : spot + width] = vec[row : row + 1]

        x, x_t, cot, bias_in, bias_up = tape.run(
            prepare,
            [((rows, width), BF16), ((width, rows), BF16), ((rows, width), BF16), ((3, width), F32),
             ((1, 2 * units), F32)],
            [states, cotangent, vectors], True, limit=12, moved=6 * MIB, plain=(0, 1),
        )
        gather_a.line()
        gather_c = Gather(grid, tape, casted(expand_down[None]))
        gather_b.line()
        a_own, a_oth = (v.reshape(4, width, cols) for v in gather_a.whole())
        gather_c.line()

        def project(x_ref, own, oth, bias, out):
            @pl.loop(0, 3)
            def _(j):
                for h, ref in enumerate((own, oth)):
                    at = slice(h * cols, (h + 1) * cols)
                    value = jnp.dot(x_ref[...], ref[j], preferred_element_type=F32)
                    out[j, :, at] = (value + bias[pl.ds(j, 1), at]).astype(BF16)

        qkv = tape.run(
            project, [((3, rows, width), BF16)], [x, a_own, a_oth, bias_in],
            limit=8, flops=6 * rows * width * width, moved=8 * MIB,
        )[0]

        def split(v):
            low = lax.broadcasted_iota(jnp.int32, v.shape, 1) < HEAD_DIM
            zero = jnp.zeros_like(v)
            return jnp.concatenate([jnp.where(low, v, zero), jnp.where(low, zero, v)], axis=0)

        def join(v):
            low = lax.broadcasted_iota(jnp.int32, (length, LANES), 1) < HEAD_DIM
            return jnp.where(low, v[:length], v[length:])

        def attend(count, qkv_ref, probs, context):
            @pl.loop(0, mine)
            def _(p):
                at = pl.ds(pl.multiple_of(p * length, length), length)
                known = lax.broadcasted_iota(jnp.int32, (length, length), 1) < count[4 + p]
                for u in range(twins):
                    lanes = slice(u * LANES, (u + 1) * LANES)
                    both = lax.dot_general(
                        qkv_ref[0, at, lanes], split(qkv_ref[1, at, lanes]), NT, preferred_element_type=F32
                    )
                    soft = []
                    for h in range(2):
                        score = jnp.where(known, both[:, h * length : (h + 1) * length] * scale, MASKED)
                        power = jnp.exp(score - jnp.max(score, axis=-1, keepdims=True))
                        soft.append(power / jnp.sum(power, axis=-1, keepdims=True))
                    prob = jnp.concatenate(soft, axis=1).astype(BF16)
                    probs[at, 2 * u * length : 2 * (u + 1) * length] = prob
                    context[at, lanes] = jnp.dot(
                        prob, split(qkv_ref[2, at, lanes]), preferred_element_type=F32
                    ).astype(BF16)

        probs, context = tape.run(
            attend, [((rows, 2 * twins * length), BF16), ((rows, width), BF16)], [qkv], True,
            limit=4, flops=4 * rows * length * width * 4, moved=5 * MIB, exps=rows * twins * 2 * length,
        )

        block = min(rows, 256)

        def hide(context_ref, x_ref, own, oth, vec, hidden, normed, inverse):
            for r in range(0, rows, block):
                at = slice(r, r + block)
                value = x_ref[at].astype(F32) + vec[2:3]
                for h, ref in enumerate((own, oth)):
                    value += lax.dot_general(
                        context_ref[at, h * cols : (h + 1) * cols], ref[3], NT, preferred_element_type=F32
                    )
                normal, spread = normed_of(value)
                normed[at], inverse[at] = normal, spread
                hidden[at] = (normal * vec[3:4] + vec[4:5]).astype(BF16)

        hidden, normed_one, inverse_one = tape.run(
            hide,
            [((rows, width), BF16), ((rows, width), F32), ((rows, 1), F32)],
            [context, x, a_own, a_oth, vectors],
            limit=8, flops=2 * rows * width * width, moved=6 * MIB,
        )

        b_own, b_oth = (v.reshape(width, units) for v in gather_b.whole())
        tile = 256

        def lift(hidden_ref, up, bias, active, active_t, slope):
            @pl.loop(0, units // tile)
            def _(i):
                at = pl.ds(pl.multiple_of(i * tile, tile), tile)
                value = jnp.dot(hidden_ref[...], up[:, at], preferred_element_type=F32) + bias[:, at]
                half = 0.5 * (1.0 + lax.erf(value * math.sqrt(0.5)))
                result = (value * half).astype(BF16)
                active[:, at] = result
                active_t[at, :] = result.T
                bell = jnp.exp(-0.5 * value * value) * (1.0 / math.sqrt(2.0 * math.pi))
                slope[:, at] = (half + value * bell).astype(BF16)

        def lift_half(h, up):
            return tape.run(
                lambda hidden_ref, up_ref, bias, *outs: lift(hidden_ref, up_ref, bias.at[:, h * units : (h + 1) * units], *outs),
                [((rows, units), BF16), ((units, rows), BF16), ((rows, units), BF16)],
                [hidden, up, bias_up],
                limit=8, flops=2 * rows * width * units, moved=8 * MIB, exps=2 * rows * units,
            )

        def turn(value, out):
            out[...] = value[...].T

        lifted = [lift_half(0, b_own), lift_half(1, b_oth)]
        hidden_t = tape.run(turn, [((width, rows), BF16)], [hidden], limit=8, moved=2 * MIB)[0]
        c_own, c_oth = (v.reshape(units, width) for v in gather_c.whole())

        def lower_half(active, down, out):
            @pl.loop(0, width // tile)
            def _(i):
                at = pl.ds(pl.multiple_of(i * tile, tile), tile)
                out[:, at] = jnp.dot(active[...], down[:, at], preferred_element_type=F32)

        lowered = tape.run(
            lower_half, [((rows, width), F32)], [lifted[0][0], c_own],
            limit=6, flops=2 * rows * width * units, moved=6 * MIB,
        )[0]

        def lower(count, lowered_ref, active, down, normed, cot_ref, vec, output, top, top16, sums, work):
            @pl.loop(0, width // tile)
            def _(i):
                at = pl.ds(pl.multiple_of(i * tile, tile), tile)
                work[:, at] = lowered_ref[:, at] + jnp.dot(active[...], down[:, at], preferred_element_type=F32)

            sums[...] = jnp.zeros_like(sums)

            @pl.loop(0, mine)
            def _(p):
                at = pl.ds(pl.multiple_of(p * length, length), length)
                value = normed[at] * vec[3:4] + vec[4:5] + work[at] + vec[5:6]
                normal, spread = normed_of(value)
                output[at] = (normal * vec[6:7] + vec[7:8]).astype(BF16)
                live = lax.broadcasted_iota(jnp.int32, (length, 1), 0) < count[4 + p]
                upstream = jnp.where(live, cot_ref[at].astype(F32), 0.0)
                grad = norm_back(upstream, normal, spread, vec[6:7])
                top[at] = grad
                top16[at] = grad.astype(BF16)
                sums[0:1] += sum_rows(grad)
                sums[1:2] += sum_rows(upstream * normal)
                sums[2:3] += sum_rows(upstream)

        output, top, top16, sums_two = tape.run(
            lower,
            [((rows, width), BF16), ((rows, width), F32), ((rows, width), BF16), ((8, width), F32)],
            [lowered, lifted[1][0], c_oth, normed_one, cot, vectors],
            True, limit=8, flops=2 * rows * width * units, moved=14 * MIB,
            scratch=[VMEM((rows, width), F32)],
        )

        def product(left, right, out):
            step = min(left.shape[0], 256)

            @pl.loop(0, left.shape[0] // step)
            def _(i):
                at = pl.ds(pl.multiple_of(i * step, step), step)
                out[at, :] = jnp.dot(left[at, :], right[...], preferred_element_type=F32).astype(out.dtype)

        def weight_grad(left, right, kind):
            shape = (left.shape[0], right.shape[1])
            return tape.run(
                product, [(shape, kind)], [left, right],
                limit=6, flops=2 * shape[0] * shape[1] * rows, moved=8 * MIB,
            )[0]

        sharded = lambda v, many: v.reshape(many, grid.dp, -1, v.shape[-1])
        scatter_c = Scatter(grid, tape, sharded(weight_grad(lifted[1][1], top16, BF16), 1))
        down_own = weight_grad(lifted[0][1], top16, F32)
        output_oth = grid.core(output)

        def sink(top16_ref, down, slope, grad, sums):
            @pl.loop(0, units // tile)
            def _(i):
                at = pl.ds(pl.multiple_of(i * tile, tile), tile)
                value = lax.dot_general(top16_ref[...], down[at, :], NT, preferred_element_type=F32)
                value = value * slope[:, at].astype(F32)
                grad[:, at] = value.astype(BF16)
                sums[:, at] = sum_rows(value)

        def sink_half(h, down):
            return tape.run(
                sink, [((rows, units), BF16), ((1, units), F32)], [top16, down, lifted[h][2]],
                limit=8, flops=2 * rows * width * units, moved=8 * MIB,
            )

        sunk = [None, sink_half(1, c_oth)]
        scatter_c.pair(sharded(down_own, 1))
        sunk[0] = sink_half(0, c_own)
        scatter_b = Scatter(grid, tape, sharded(weight_grad(hidden_t, sunk[1][0], BF16), 1))
        up_own = weight_grad(hidden_t, sunk[0][0], F32)

        def surface(grad_own, grad_oth, own, oth, top_ref, normed, inverse, vec, a_own_ref, a_oth_ref,
                    mid, mid_t, back, sums, work, mid16):
            @pl.loop(0, width // tile)
            def _(i):
                at = pl.ds(pl.multiple_of(i * tile, tile), tile)
                work[:, at] = (
                    top_ref[:, at]
                    + lax.dot_general(grad_own[...], own[at, :], NT, preferred_element_type=F32)
                    + lax.dot_general(grad_oth[...], oth[at, :], NT, preferred_element_type=F32)
                )

            sums[...] = jnp.zeros_like(sums)

            @pl.loop(0, mine)
            def _(p):
                at = pl.ds(pl.multiple_of(p * length, length), length)
                upstream, normal = work[at], normed[at]
                grad = norm_back(upstream, normal, inverse[at], vec[3:4])
                mid[at] = grad
                mid16[at] = grad.astype(BF16)
                sums[0:1] += sum_rows(grad)
                sums[1:2] += sum_rows(upstream * normal)
                sums[2:3] += sum_rows(upstream)

            mid_t[...] = mid16[...].T
            for h, ref in enumerate((a_own_ref, a_oth_ref)):
                back[:, h * cols : (h + 1) * cols] = jnp.dot(
                    mid16[...], ref[3], preferred_element_type=F32
                ).astype(BF16)

        mid, mid_t, back, sums_one = tape.run(
            surface,
            [((rows, width), F32), ((width, rows), BF16), ((rows, width), BF16), ((8, width), F32)],
            [sunk[0][0], sunk[1][0], b_own, b_oth, top, normed_one, inverse_one, vectors, a_own, a_oth],
            limit=14, flops=4 * rows * width * units + 2 * rows * width * width, moved=14 * MIB,
            scratch=[VMEM((rows, width), F32), VMEM((rows, width), BF16)],
        )

        scatter_b.pair(sharded(up_own, 1))
        scatter_c.sides()

        def values_back(probs_ref, back_ref, grad, sums):
            sums[...] = jnp.zeros_like(sums)

            @pl.loop(0, mine)
            def _(p):
                at = pl.ds(pl.multiple_of(p * length, length), length)
                for u in range(twins):
                    lanes = slice(u * LANES, (u + 1) * LANES)
                    value = join(lax.dot_general(
                        probs_ref[at, 2 * u * length : 2 * (u + 1) * length], back_ref[at, lanes], TN,
                        preferred_element_type=F32,
                    ))
                    grad[at, lanes] = value.astype(BF16)
                    sums[:, lanes] += sum_rows(value)

        grad_v, sum_v = tape.run(
            values_back, [((rows, width), BF16), ((1, width), F32)], [probs, back],
            limit=4, flops=4 * rows * length * width, moved=3 * MIB,
        )

        def halves(left_v, right_v, h, kind, left_w, right_w):
            def both(left_v_ref, right_v_ref, left_w_ref, right_w_ref, out):
                at = slice(h * cols, (h + 1) * cols)
                for j, (left, right) in enumerate(((left_v_ref, right_v_ref), (left_w_ref, right_w_ref))):
                    out[j] = jnp.dot(left[...], right[:, at], preferred_element_type=F32).astype(out.dtype)

            return tape.run(
                both, [((2, width, cols), kind)], [left_v, right_v, left_w, right_w],
                limit=6, flops=4 * rows * width * cols, moved=5 * MIB,
            )[0]

        scatter_vo = Scatter(grid, tape, sharded(halves(x_t, grad_v, 1, BF16, mid_t, context), 2))
        vo_own = halves(x_t, grad_v, 0, F32, mid_t, context)

        def attend_back(probs_ref, back_ref, qkv_ref, grad_q, grad_k, sums):
            sums[...] = jnp.zeros_like(sums)

            @pl.loop(0, mine)
            def _(p):
                at = pl.ds(pl.multiple_of(p * length, length), length)
                for u in range(twins):
                    lanes = slice(u * LANES, (u + 1) * LANES)
                    prob = probs_ref[at, 2 * u * length : 2 * (u + 1) * length].astype(F32)
                    both = lax.dot_general(
                        back_ref[at, lanes], split(qkv_ref[2, at, lanes]), NT, preferred_element_type=F32
                    )
                    parts = []
                    for h in range(2):
                        half = slice(h * length, (h + 1) * length)
                        inner = jnp.sum(prob[:, half] * both[:, half], axis=-1, keepdims=True)
                        parts.append(prob[:, half] * (both[:, half] - inner))
                    grad = jnp.concatenate(parts, axis=1).astype(BF16)
                    value = jnp.dot(grad, split(qkv_ref[1, at, lanes]), preferred_element_type=F32) * scale
                    grad_q[at, lanes] = value.astype(BF16)
                    sums[:, lanes] += sum_rows(value)
                    value = join(lax.dot_general(grad, qkv_ref[0, at, lanes], TN, preferred_element_type=F32))
                    grad_k[at, lanes] = (value * scale).astype(BF16)

        grad_q, grad_k, sum_q = tape.run(
            attend_back, [((rows, width), BF16), ((rows, width), BF16), ((1, width), F32)], [probs, back, qkv],
            limit=4, flops=16 * rows * length * width, moved=6 * MIB,
        )
        scatter_vo.pair(sharded(vo_own, 2))
        scatter_b.sides()
        scatter_c.line()
        scatter_qk = Scatter(grid, tape, sharded(halves(x_t, grad_q, 1, BF16, x_t, grad_k), 2))
        qk_own = halves(x_t, grad_q, 0, F32, x_t, grad_k)

        def states_back(grad_q_ref, grad_k_ref, grad_v_ref, own, oth, mid_ref, out):
            @pl.loop(0, width // tile)
            def _(i):
                at = pl.ds(pl.multiple_of(i * tile, tile), tile)
                value = mid_ref[:, at]
                for j, ref in enumerate((grad_q_ref, grad_k_ref, grad_v_ref)):
                    for h, weight in enumerate((own, oth)):
                        value += lax.dot_general(
                            ref[:, h * cols : (h + 1) * cols], weight[j, at, :], NT, preferred_element_type=F32
                        )
                out[:, at] = value

        states_own = tape.run(
            states_back, [((rows, width), F32)], [grad_q, grad_k, grad_v, a_own, a_oth, mid],
            limit=8, flops=6 * rows * width * width, moved=8 * MIB,
        )[0]

        states_oth = grid.core(states_own)
        scatter_qk.pair(sharded(qk_own, 2))

        def collect(s, sum_q_ref, sum_v_ref, one, two, up_own_ref, up_oth_ref, out):
            for t in range(cores):

                @pl.when(s[3] == t)
                def _():
                    for row, ref in enumerate((sum_q_ref, sum_v_ref)):
                        for h in range(2):
                            out[row : row + 1, (h ^ t) * cols : ((h ^ t) + 1) * cols] = ref[
                                :, h * cols : (h + 1) * cols
                            ]
                    for h, ref in enumerate((up_own_ref, up_oth_ref)):
                        for i in range(units // width):
                            row = 8 + (h ^ t) * (units // width) + i
                            out[row : row + 1] = ref[:, i * width : (i + 1) * width]

            out[2:5] = one[0:3]
            out[5:8] = two[0:3]

        vector_part = tape.run(
            collect, [(vectors.shape, F32)], [sum_q, sum_v, sums_one, sums_two, sunk[0][1], sunk[1][1]], True
        )[0]
        vector_total = Total(grid, tape, vector_part)
        scatter_vo.sides()
        scatter_b.line()

        def pair_up(s, own, oth, out):
            out[s[3]] = own[...]
            out[1 - s[3]] = oth[...]

        def paired(own, oth):
            shape = ((cores,) + own.shape, own.dtype)
            result = tape.run(pair_up, [shape], [own, oth], True, limit=8, spill=(0,))[0]
            return result.reshape(pairs, length, width)

        layer_output = paired(output, output_oth)
        states_grad = paired(states_own, states_oth)
        vector_total.line()
        scatter_qk.sides()
        scatter_vo.line()
        vector_total.sides()

        def vector_step(own, oth, vec, first, second, out, moment, square):
            one, two, direction = adam(own[...] + oth[...], first[...], second[...])
            moment[...], square[...] = one, two
            out[...] = vec[...] - RATE * direction

        def matrix_step(index):
            def step(*refs):
                grad = sum((ref[...].astype(F32) for ref in refs[1 : grid.long]), refs[0][...])
                master, first, second, moment, square, way, kept, tile_ref = refs[grid.long :]
                moment[...], square[...], value = adam(grad, first[...], second[...])
                kept[...] = master[...]
                way[...] = value + DECAY * kept[...]
                tile_ref[...] = norm_tile([(index, kept[0], way[0])])

            return step

        def stepped(step, parts, masters, shapes):
            outs = [(s, F32) for _ in range(4) for s in shapes] + [((8, LANES), F32)]
            n, m = len(parts), len(masters)
            return tape.run(
                step, outs, parts + masters, limit=6, spill=range(2 * len(shapes)), plain=range(n, n + m), moved=2 * MIB
            )

        ups = [v[None] for v in (expand_up, first_up, second_up)]
        downs = [v[None] for v in (expand_down, first_down, second_down)]
        moment_down, square_down, way_down, kept_down, tile_down = stepped(
            matrix_step(5), scatter_c.parts, downs, [downs[0].shape]
        )
        scatter_qk.line()
        moment_up, square_up, way_up, kept_up, tile_up = stepped(
            matrix_step(4), scatter_b.parts, ups, [ups[0].shape]
        )
        updated_vectors, moment_vectors, square_vectors = tape.run(
            vector_step, [(vectors.shape, F32)] * 3,
            vector_total.pair + [vectors, vector_first, vector_second], spill=(0, 1, 2), plain=(2, 3, 4),
        )

        def attend_step(*refs):
            n = grid.long
            vo, qk = refs[:n], refs[n : 2 * n]
            m_in, f_in, s_in, m_out, f_out, s_out, tile_up_ref, tile_down_ref = refs[2 * n : 2 * n + 8]
            mo_in, mo_out, sq_in, sq_out, way_in, way_out, kept_in, kept_out, tile_ref = refs[2 * n + 8 :]
            whole = lambda parts, j: sum((ref[j].astype(F32) for ref in parts[1:]), parts[0][j])
            entries = []
            for j, grad in enumerate((whole(qk, 0), whole(qk, 1), whole(vo, 0), whole(vo, 1))):
                i = j if j < 3 else 0
                m, f, s, mo, sq, kept, way = (
                    (m_in, f_in, s_in, mo_in, sq_in, kept_in, way_in)
                    if j < 3
                    else (m_out, f_out, s_out, mo_out, sq_out, kept_out, way_out)
                )
                mo[i], sq[i], value = adam(grad, f[i], s[i])
                kept[i] = m[i]
                way[i] = value + DECAY * kept[i]
                entries.append((j, kept[i], way[i]))
            tile_ref[...] = norm_tile(entries) + tile_up_ref[...] + tile_down_ref[...]

        ins = scatter_vo.parts + scatter_qk.parts + [attend_in, first_in, second_in, attend_out, first_out, second_out]
        shapes = [attend_in.shape, attend_out.shape]
        (
            moment_in, moment_out, square_in, square_out, way_in, way_out, kept_in, kept_out, tiles
        ) = tape.run(
            attend_step, [(s, F32) for _ in range(4) for s in shapes] + [((8, LANES), F32)], ins + [tile_up, tile_down],
            limit=6, spill=range(4), plain=range(2 * grid.long, 2 * grid.long + 6), moved=2 * MIB,
        )
        tile_total = Total(grid, tape, tiles)
        tile_total.line()
        tile_total.sides()

        def update(own, oth, *refs):
            masters, ways, outs = refs[:4], refs[4:8], refs[8:]
            norms = jnp.sqrt(own[...] + oth[...])
            outs[8][...] = norms.T[0:2, 0:6]
            trust = RATE * (norms[:, 0:1] / norms[:, 1:2])
            for i, first in enumerate((0, 3, 4, 5)):
                for j in range(masters[i].shape[0]):
                    value = masters[i][j] - trust[first + j : first + j + 1] * ways[i][j]
                    outs[i][j], outs[4 + i][j] = value, value.astype(BF16)

        masters = [kept_in, kept_out, kept_up, kept_down]
        results = tape.run(
            update,
            [(m.shape, F32) for m in masters] + [(m.shape, BF16) for m in masters] + [((2, 6), F32)],
            tile_total.pair + masters + [way_in, way_out, way_up, way_down],
            limit=6, spill=range(9), moved=2 * MIB,
        )

        def native(values):
            values = list(values)
            return (values[0], values[1][0].T, values[2][0], values[3][0])

        return (
            layer_output, states_grad, *native(results[:4]),
            *native([moment_in, moment_out, moment_up, moment_down]),
            *native([square_in, square_out, square_up, square_down]),
            *native(results[4:8]), updated_vectors, moment_vectors, square_vectors, results[8].T,
        )

    return body


def solution(mesh):
    rows = P("dp", None, None)
    matrices = (P(None, "dp", "tensor"), P("tensor", "dp"), P("dp", "tensor"), P(("tensor", "dp"), None))
    in_specs = (rows, rows, P("dp"), P("dp")) + matrices * 3 + (P(), P(), P())
    out_specs = (rows, rows) + matrices * 4 + (P(), P(), P(), P())
    body = make_body(Grid(mesh))
    return jax.shard_map(body, mesh=mesh, in_specs=in_specs, out_specs=out_specs, check_vma=False)
```

```python
import itertools
import math

import jax
import jax.numpy as jnp
import numpy as np
from jax import lax
from jax.experimental import pallas as pl
from jax.experimental.pallas import tpu as pltpu
from jax.sharding import PartitionSpec as P

HEAD_DIM = 64
STEP = 10
NORM_EPS = 1e-05
BETA_ONE = 0.9
BETA_TWO = 0.999
ADAM_EPS = 1e-06
RATE = 0.3
DECAY = 0.01
MASKED = -1e30
AXES = ("dp", "tensor")
F32, BF16 = jnp.float32, jnp.bfloat16
VMEM = pltpu.VMEM
LANES = 128
NT = (((1,), (1,)), ((), ()))
TN = (((0,), (0,)), ((), ()))
MIB = 1 << 20


class Grid:
    def __init__(self, mesh):
        self.dp, self.cores = mesh.shape["dp"], mesh.shape["tensor"]
        chips = mesh.devices.reshape(self.dp, self.cores)[:, 0]
        spots = [tuple(getattr(chip, "coords", ())) for chip in chips]
        if any(len(spot) != 3 for spot in spots) or len(set(spots)) != self.dp:
            side = 1 << ((self.dp.bit_length() - 1) // 3)
            spots = [(i % side, i // side % side, i // (side * side)) for i in range(self.dp)]
        spots = np.array(spots) - np.min(spots, axis=0)
        sizes = spots.max(axis=0) + 1
        order = sorted(range(3), key=lambda k: -sizes[k])
        order = order[:1] + sorted(order[1:])
        self.spots = spots[:, order].tolist()
        self.long, self.side, _ = (int(sizes[k]) for k in order)
        self.at = {tuple(spot): i for i, spot in enumerate(self.spots)}
        unit = [tuple(int(j == k) for j in range(3)) for k in range(3)]
        self.stride = [self.at.get(u, 0) for u in unit]
        self.sizes = [int(sizes[k]) for k in order]

    def send(self, value, hop):
        pairs = []
        for i, spot in enumerate(self.spots):
            for core in range(self.cores):
                offsets, turn = hop(core)
                target = self.at[tuple(u ^ v for u, v in zip(spot, offsets))]
                pairs.append((i * self.cores + core, target * self.cores + (core ^ turn)))
        return lax.ppermute(value, AXES, pairs)

    def place(self):
        index = lax.axis_index("dp")
        spot = [lax.rem(lax.div(index, s), n) if n > 1 else index * 0 for s, n in zip(self.stride, self.sizes)]
        return jnp.stack(spot + [lax.axis_index("tensor")]).astype(jnp.int32)

    def path(self):
        bits = [[1 << b for b in reversed(range((n - 1).bit_length()))] for n in (self.long, self.side, self.side)]
        return [(side, k) for side in range(3) for k in bits[side]]

    def exchange(self, value, step):
        side, k = step
        offsets = [(k, 0, 0), (0, k, 0), (0, 0, k)]
        return self.send(value, lambda core: (offsets[side if core == 0 else (0, 2, 1)[side]], 0))

    def bit(self, s, step):
        side, k = step
        spot = s[0] if side == 0 else jnp.where(s[3] == 0, s[side], s[3 - side])
        return lax.rem(lax.div(spot, k), 2)

    def spot(self, s, steps, bits):
        place = 0
        for (side, k), bit in zip(steps, bits):
            stride = self.stride[0] if side == 0 else jnp.where(s[3] == 0, self.stride[side], self.stride[3 - side])
            place = place + bit * k * stride
        return place

    def long_steps(self):
        return [step for step in self.path() if step[0] == 0]

    def long_bits(self, s, k):
        spot = s[0] ^ k
        return tuple(lax.rem(lax.div(spot, distance), 2) for _, distance in reversed(self.long_steps()))

    def along(self, k):
        return lambda core: ((k, 0, 0), 0)

    def cross(self, j, k):
        return lambda core: ((0, j, k), 0)

    def core(self, value):
        return self.send(value, lambda core: ((0, 0, 0), 1))


class Tape:
    def __init__(self, place):
        self.place = place
        self.token = None

    def run(self, body, outs, ins, place=False, limit=4, flops=0, moved=0, exps=0, scratch=(), spill=(), plain=(), name=None):
        ins = [v if i in plain else pltpu.with_memory_space_constraint(v, VMEM) for i, v in enumerate(ins)]
        specs = [pl.BlockSpec(memory_space=VMEM)] * len(ins)
        first = []
        if place:
            first.append((self.place, pltpu.SMEM))
        if self.token is not None:
            first.append((pltpu.with_memory_space_constraint(self.token, VMEM), VMEM))
        chained = self.token is not None
        count, results = len(ins), len(outs)

        def chain(*refs):
            refs = list(refs)
            head = [refs.pop(0)] if place else []
            if chained:
                refs.pop(0)
            last = refs.pop(count + results)
            last[...] = jnp.zeros_like(last)
            body(*head, *refs)

        shapes = [
            jax.ShapeDtypeStruct(s, d) if i in spill else VMEM(s, d) for i, (s, d) in enumerate(outs)
        ] + [VMEM((8, LANES), F32)]
        *values, self.token = pl.pallas_call(
            chain,
            out_shape=shapes,
            in_specs=[pl.BlockSpec(memory_space=m) for _, m in first] + specs,
            out_specs=[pl.BlockSpec(memory_space=VMEM)] * len(shapes),
            scratch_shapes=list(scratch),
            name=name or body.__name__,
            cost_estimate=pl.CostEstimate(flops=flops, bytes_accessed=moved, transcendentals=0),
            compiler_params=pltpu.CompilerParams(vmem_limit_bytes=limit * MIB),
        )(*[v for v, _ in first], *ins)
        return values


def part(count, group, groups=3):
    return range(count * group // groups, count * (group + 1) // groups)


class Gather:
    def __init__(self, grid, tape, shard, direct=False):
        self.grid, self.tape, self.block = grid, tape, shard
        self.path = grid.path()
        if direct:
            self.got = [grid.send(shard, grid.along(k)) for k in range(1, grid.long)]
        else:
            self.got = grid.exchange(shard, self.path[0])

    def merge_long(self):
        grid = self.grid
        steps = grid.long_steps()

        def gather_long(s, *refs):
            for k, ref in enumerate(refs[:-1]):
                refs[-1][grid.long_bits(s, k)] = ref[...]

        shape = (2,) * len(steps) + self.block.shape
        self.block = self.tape.run(gather_long, [(shape, BF16)], [self.block] + self.got, True)[0]
        self.got = grid.exchange(self.block, self.path[len(steps)])

    def merge(self, group):
        self.merges(part(len(self.path) - 1, group))

    def merge_short(self):
        self.merges(range(len(self.grid.long_steps()), len(self.path) - 1))

    def merges(self, steps):
        grid = self.grid
        for i in steps:
            step = self.path[i]

            def gather_merge(s, own, got, out):
                bit = grid.bit(s, step)
                out[bit] = own[...]
                out[1 - bit] = got[...]

            shape = (2,) + self.block.shape
            self.block = self.tape.run(gather_merge, [(shape, BF16)], [self.block, self.got], True)[0]
            self.got = grid.exchange(self.block, self.path[i + 1])

    def whole(self):
        grid, path = self.grid, self.path
        many, rows, width = self.block.shape[-3:]

        def gather_whole(s, own, got, out):
            last = grid.bit(s, path[-1])
            for bits in itertools.product(range(2), repeat=len(path) - 1):
                for ref, bit in ((own, last), (got, 1 - last)):
                    spot = grid.spot(s, path, bits[::-1] + (bit,))
                    for j in range(many):
                        out[j, spot] = ref[bits + (j,)]

        shape = (many, grid.dp, rows, width)
        full = self.tape.run(gather_whole, [(shape, BF16)], [self.block, self.got], True)[0]
        return full, grid.core(full)


class Scatter:
    def __init__(self, grid, tape, other):
        self.grid, self.tape = grid, tape
        self.path = grid.path()
        self.got = [grid.core(v) for v in other]

    def pair(self, own):
        grid, path = self.grid, self.path
        each, _, rows, width = own[0].shape
        many, pieces = each * len(own), len(own)
        shape = (2,) * (len(path) - 1) + (many, rows, width)

        def scatter_pair(s, *refs):
            own_refs, got_refs, (keep, send) = refs[:pieces], refs[pieces : 2 * pieces], refs[2 * pieces :]
            last = grid.bit(s, path[-1])
            for bits in itertools.product(range(2), repeat=len(path) - 1):
                for out, bit in ((keep, last), (send, 1 - last)):
                    spot = grid.spot(s, path, bits[::-1] + (bit,))
                    for j in range(many):
                        g, i = divmod(j, each)
                        total = own_refs[g][i, spot] + got_refs[g][i, spot].astype(F32)
                        out[bits + (j,)] = total.astype(out.dtype)

        self.keep, value = self.tape.run(scatter_pair, [(shape, F32), (shape, BF16)], own + self.got, True)
        self.got = grid.exchange(value, path[-1])

    def split(self, group):
        self.splits(part(len(self.path) - 1, group))

    def split_short(self):
        self.splits(range(len(self.path) - 1 - len(self.grid.long_steps())))

    def split_long(self):
        grid, count = self.grid, len(self.grid.long_steps())

        def scatter_long(s, own, got, *outs):
            for k, out in enumerate(outs):
                at = grid.long_bits(s, k)
                out[...] = (own[at] + got[at].astype(F32)).astype(out.dtype)

        shape = self.keep.shape[count:]
        keep, *values = self.tape.run(
            scatter_long, [(shape, F32)] + [(shape, BF16)] * (grid.long - 1), [self.keep, self.got], True
        )
        self.parts = [keep] + [grid.send(v, grid.along(k + 1)) for k, v in enumerate(values)]

    def splits(self, steps):
        grid = self.grid
        for i in steps:
            step = self.path[len(self.path) - 2 - i]

            def scatter_split(s, own, got, keep, send):
                bit = grid.bit(s, step)
                keep[...] = own[bit] + got[bit].astype(F32)
                send[...] = (own[1 - bit] + got[1 - bit].astype(F32)).astype(BF16)

            shape = self.keep.shape[1:]
            self.keep, value = self.tape.run(
                scatter_split, [(shape, F32), (shape, BF16)], [self.keep, self.got], True
            )
            self.got = grid.exchange(value, step)
        self.parts = [self.keep, self.got]


def tree(values):
    values = list(values)
    while len(values) > 1:
        values = [a + b for a, b in zip(values[::2], values[1::2])]
    return values[0]


class Total:
    def __init__(self, grid, tape, value):
        self.grid, self.tape = grid, tape
        self.got = [value] + [grid.send(value, grid.along(k)) for k in range(1, grid.long)]

    def add(self):
        def body(*refs):
            refs[-1][...] = tree(ref[...] for ref in refs[:-1])

        return self.tape.run(body, [(self.got[0].shape, F32)], self.got)[0]

    def line(self):
        grid, value = self.grid, self.add()
        offsets = [(j, k) for j in range(grid.side) for k in range(grid.side)]
        self.got = [value] + [grid.send(value, grid.cross(j, k)) for j, k in offsets[1:]]

    def sides(self):
        value = self.add()
        self.pair = [value, self.grid.core(value)]


def normed_of(values):
    center = values - jnp.mean(values, axis=-1, keepdims=True)
    inverse = lax.rsqrt(jnp.mean(center * center, axis=-1, keepdims=True) + NORM_EPS)
    return center * inverse, inverse


def norm_back(upstream, normed, inverse, gain):
    scaled = upstream * gain
    inner = jnp.mean(scaled * normed, axis=-1, keepdims=True)
    return inverse * (scaled - jnp.mean(scaled, axis=-1, keepdims=True) - normed * inner)


def sum_rows(values):
    return jnp.sum(values, axis=0, keepdims=True)


def adam(grad, first, second):
    first_new = BETA_ONE * first + (1.0 - BETA_ONE) * grad
    second_new = BETA_TWO * second + (1.0 - BETA_TWO) * grad * grad
    corrected = first_new / (1.0 - BETA_ONE**STEP)
    spread = jnp.sqrt(second_new / (1.0 - BETA_TWO**STEP))
    return first_new, second_new, corrected / (spread + ADAM_EPS)


def squares(values):
    return jnp.sum(sum_rows(values * values), axis=1, keepdims=True)


def norm_row(entries):
    lane = lax.broadcasted_iota(jnp.int32, (1, LANES), 1)
    row = jnp.zeros((1, LANES), F32)
    for index, weight, direction in entries:
        row = jnp.where(lane == index, squares(weight), row)
        row = jnp.where(lane == index + 6, squares(direction), row)
    return row


def make_body(grid):
    def body(
        states, cotangent, word_counts, region_counts,
        attend_in, attend_out, expand_up, expand_down,
        first_in, first_out, first_up, first_down,
        second_in, second_out, second_up, second_down,
        vectors, vector_first, vector_second,
    ):
        cores = grid.cores
        pairs, length, width = states.shape
        mine = pairs // cores
        rows = mine * length
        cols = attend_in.shape[2]
        units = expand_up.shape[1]
        twins = width // LANES
        scale = HEAD_DIM**-0.5
        rank = lax.axis_index("tensor")
        counts = lax.dynamic_slice_in_dim(word_counts + region_counts, rank * mine, mine, 0)
        tape = Tape(jnp.concatenate([grid.place(), counts]))
        attend_out, first_out, second_out = (v.T[None] for v in (attend_out, first_out, second_out))

        def cast(*refs):
            spot = 0
            for ref in refs[:-1]:
                refs[-1][spot : spot + ref.shape[0]] = ref[...].astype(BF16)
                spot += ref.shape[0]

        def casted(*mats):
            many = sum(m.shape[0] for m in mats)
            shape = (many,) + mats[0].shape[1:]
            return tape.run(cast, [(shape, BF16)], mats, plain=range(len(mats)))[0]

        gather_a = Gather(grid, tape, casted(attend_in, attend_out), direct=True)

        def prepare(s, states_ref, cot_ref, vec, x_ref, x_t, mine_cot, bias_in, bias_up):
            @pl.loop(0, mine)
            def _(p):
                at = pl.ds(pl.multiple_of(p * length, length), length)
                x_ref[at, :] = states_ref[s[3] * mine + p]
                mine_cot[at, :] = cot_ref[s[3] * mine + p]

            x_t[...] = x_ref[...].T
            bias_in[1:2] = jnp.zeros((1, width), F32)
            for t in range(cores):

                @pl.when(s[3] == t)
                def _():
                    for h in range(2):
                        at, source = slice(h * cols, (h + 1) * cols), slice((h ^ t) * cols, ((h ^ t) + 1) * cols)
                        bias_in[0:1, at] = vec[0:1, source]
                        bias_in[2:3, at] = vec[1:2, source]
                        for i in range(units // width):
                            row = 8 + (h ^ t) * (units // width) + i
                            spot = h * units + i * width
                            bias_up[:, spot : spot + width] = vec[row : row + 1]

        x, x_t, cot, bias_in, bias_up = tape.run(
            prepare,
            [((rows, width), BF16), ((width, rows), BF16), ((rows, width), BF16), ((3, width), F32),
             ((1, 2 * units), F32)],
            [states, cotangent, vectors], True, limit=12, moved=6 * MIB, plain=(0, 1),
        )
        gather_b = Gather(grid, tape, casted(expand_up[None]))
        gather_a.merge_long()
        gather_b.merge(0)
        gather_a.merge_short()
        gather_c = Gather(grid, tape, casted(expand_down[None]))
        gather_b.merge(1)
        gather_c.merge(0)
        gather_b.merge(2)
        gather_c.merge(1)
        a_own, a_oth = (v.reshape(4, width, cols) for v in gather_a.whole())

        def project(x_ref, own, oth, bias, out):
            @pl.loop(0, 3)
            def _(j):
                for h, ref in enumerate((own, oth)):
                    at = slice(h * cols, (h + 1) * cols)
                    value = jnp.dot(x_ref[...], ref[j], preferred_element_type=F32)
                    out[j, :, at] = (value + bias[pl.ds(j, 1), at]).astype(BF16)

        qkv = tape.run(
            project, [((3, rows, width), BF16)], [x, a_own, a_oth, bias_in],
            limit=8, flops=6 * rows * width * width, moved=8 * MIB,
        )[0]

        def split(v):
            low = lax.broadcasted_iota(jnp.int32, v.shape, 1) < HEAD_DIM
            zero = jnp.zeros_like(v)
            return jnp.concatenate([jnp.where(low, v, zero), jnp.where(low, zero, v)], axis=0)

        def join(v):
            low = lax.broadcasted_iota(jnp.int32, (length, LANES), 1) < HEAD_DIM
            return jnp.where(low, v[:length], v[length:])

        def attend(count, qkv_ref, probs, context):
            @pl.loop(0, mine)
            def _(p):
                at = pl.ds(pl.multiple_of(p * length, length), length)
                known = lax.broadcasted_iota(jnp.int32, (length, length), 1) < count[4 + p]
                for u in range(twins):
                    lanes = slice(u * LANES, (u + 1) * LANES)
                    both = lax.dot_general(
                        qkv_ref[0, at, lanes], split(qkv_ref[1, at, lanes]), NT, preferred_element_type=F32
                    )
                    soft = []
                    for h in range(2):
                        score = jnp.where(known, both[:, h * length : (h + 1) * length] * scale, MASKED)
                        power = jnp.exp(score - jnp.max(score, axis=-1, keepdims=True))
                        soft.append(power / jnp.sum(power, axis=-1, keepdims=True))
                    prob = jnp.concatenate(soft, axis=1).astype(BF16)
                    probs[at, 2 * u * length : 2 * (u + 1) * length] = prob
                    context[at, lanes] = jnp.dot(
                        prob, split(qkv_ref[2, at, lanes]), preferred_element_type=F32
                    ).astype(BF16)

        probs, context = tape.run(
            attend, [((rows, 2 * twins * length), BF16), ((rows, width), BF16)], [qkv], True,
            limit=4, flops=4 * rows * length * width * 4, moved=5 * MIB, exps=rows * twins * 2 * length,
        )

        gather_c.merge(2)
        b_own, b_oth = (v.reshape(width, units) for v in gather_b.whole())
        block = min(rows, 256)

        def hide(context_ref, x_ref, own, oth, vec, hidden, normed, inverse):
            for r in range(0, rows, block):
                at = slice(r, r + block)
                value = x_ref[at].astype(F32) + vec[2:3]
                for h, ref in enumerate((own, oth)):
                    value += lax.dot_general(
                        context_ref[at, h * cols : (h + 1) * cols], ref[3], NT, preferred_element_type=F32
                    )
                normal, spread = normed_of(value)
                normed[at], inverse[at] = normal, spread
                hidden[at] = (normal * vec[3:4] + vec[4:5]).astype(BF16)

        hidden, normed_one, inverse_one = tape.run(
            hide,
            [((rows, width), BF16), ((rows, width), F32), ((rows, 1), F32)],
            [context, x, a_own, a_oth, vectors],
            limit=8, flops=2 * rows * width * width, moved=6 * MIB,
        )

        tile = 256

        def lift(hidden_ref, up, bias, active, active_t, slope):
            @pl.loop(0, units // tile)
            def _(i):
                at = pl.ds(pl.multiple_of(i * tile, tile), tile)
                value = jnp.dot(hidden_ref[...], up[:, at], preferred_element_type=F32) + bias[:, at]
                half = 0.5 * (1.0 + lax.erf(value * math.sqrt(0.5)))
                result = (value * half).astype(BF16)
                active[:, at] = result
                active_t[at, :] = result.T
                bell = jnp.exp(-0.5 * value * value) * (1.0 / math.sqrt(2.0 * math.pi))
                slope[:, at] = (half + value * bell).astype(BF16)

        def lift_half(h, up):
            return tape.run(
                lambda hidden_ref, up_ref, bias, *outs: lift(hidden_ref, up_ref, bias.at[:, h * units : (h + 1) * units], *outs),
                [((rows, units), BF16), ((units, rows), BF16), ((rows, units), BF16)],
                [hidden, up, bias_up],
                limit=8, flops=2 * rows * width * units, moved=8 * MIB, exps=2 * rows * units,
            )

        def turn(value, out):
            out[...] = value[...].T

        lifted = [lift_half(0, b_own), lift_half(1, b_oth)]
        hidden_t = tape.run(turn, [((width, rows), BF16)], [hidden], limit=8, moved=2 * MIB)[0]
        c_own, c_oth = (v.reshape(units, width) for v in gather_c.whole())

        def lower_half(active, down, out):
            @pl.loop(0, width // tile)
            def _(i):
                at = pl.ds(pl.multiple_of(i * tile, tile), tile)
                out[:, at] = jnp.dot(active[...], down[:, at], preferred_element_type=F32)

        lowered = tape.run(
            lower_half, [((rows, width), F32)], [lifted[0][0], c_own],
            limit=6, flops=2 * rows * width * units, moved=6 * MIB,
        )[0]

        def lower(count, lowered_ref, active, down, normed, cot_ref, vec, output, top, top16, sums, work):
            @pl.loop(0, width // tile)
            def _(i):
                at = pl.ds(pl.multiple_of(i * tile, tile), tile)
                work[:, at] = lowered_ref[:, at] + jnp.dot(active[...], down[:, at], preferred_element_type=F32)

            sums[...] = jnp.zeros_like(sums)

            @pl.loop(0, mine)
            def _(p):
                at = pl.ds(pl.multiple_of(p * length, length), length)
                value = normed[at] * vec[3:4] + vec[4:5] + work[at] + vec[5:6]
                normal, spread = normed_of(value)
                output[at] = (normal * vec[6:7] + vec[7:8]).astype(BF16)
                live = lax.broadcasted_iota(jnp.int32, (length, 1), 0) < count[4 + p]
                upstream = jnp.where(live, cot_ref[at].astype(F32), 0.0)
                grad = norm_back(upstream, normal, spread, vec[6:7])
                top[at] = grad
                top16[at] = grad.astype(BF16)
                sums[0:1] += sum_rows(grad)
                sums[1:2] += sum_rows(upstream * normal)
                sums[2:3] += sum_rows(upstream)

        output, top, top16, sums_two = tape.run(
            lower,
            [((rows, width), BF16), ((rows, width), F32), ((rows, width), BF16), ((8, width), F32)],
            [lowered, lifted[1][0], c_oth, normed_one, cot, vectors],
            True, limit=8, flops=2 * rows * width * units, moved=14 * MIB,
            scratch=[VMEM((rows, width), F32)],
        )

        def product(left, right, *outs):
            step = min(left.shape[0], 256)

            @pl.loop(0, left.shape[0] // step)
            def _(i):
                at = pl.ds(pl.multiple_of(i * step, step), step)
                value = jnp.dot(left[at, :], right[...], preferred_element_type=F32)
                share = value.shape[1] // len(outs)
                for g, out in enumerate(outs):
                    out[at, :] = value[:, g * share : (g + 1) * share].astype(out.dtype)

        def weight_grad(left, right, kind, pieces=1):
            shape = (left.shape[0], right.shape[1])
            return tape.run(
                product, [((shape[0], shape[1] // pieces), kind)] * pieces, [left, right],
                limit=6, flops=2 * shape[0] * shape[1] * rows, moved=8 * MIB,
            )

        sharded = lambda values, many: [v.reshape(many, grid.dp, -1, v.shape[-1]) for v in values]
        scatter_c = Scatter(grid, tape, sharded(weight_grad(lifted[1][1], top16, BF16), 1))
        down_own = weight_grad(lifted[0][1], top16, F32)
        output_oth = grid.core(output)

        def sink(top16_ref, down, slope, grad, sums):
            @pl.loop(0, units // tile)
            def _(i):
                at = pl.ds(pl.multiple_of(i * tile, tile), tile)
                value = lax.dot_general(top16_ref[...], down[at, :], NT, preferred_element_type=F32)
                value = value * slope[:, at].astype(F32)
                grad[:, at] = value.astype(BF16)
                sums[:, at] = sum_rows(value)

        def sink_half(h, down):
            return tape.run(
                sink, [((rows, units), BF16), ((1, units), F32)], [top16, down, lifted[h][2]],
                limit=8, flops=2 * rows * width * units, moved=8 * MIB,
            )

        sunk = [None, sink_half(1, c_oth)]
        scatter_b = Scatter(grid, tape, sharded(weight_grad(hidden_t, sunk[1][0], BF16), 1))
        scatter_c.pair(sharded(down_own, 1))
        sunk[0] = sink_half(0, c_own)
        up_own = weight_grad(hidden_t, sunk[0][0], F32)

        def surface(grad_own, grad_oth, own, oth, top_ref, normed, inverse, vec, a_own_ref, a_oth_ref,
                    mid, mid_t, back, sums, work, mid16):
            @pl.loop(0, width // tile)
            def _(i):
                at = pl.ds(pl.multiple_of(i * tile, tile), tile)
                work[:, at] = (
                    top_ref[:, at]
                    + lax.dot_general(grad_own[...], own[at, :], NT, preferred_element_type=F32)
                    + lax.dot_general(grad_oth[...], oth[at, :], NT, preferred_element_type=F32)
                )

            sums[...] = jnp.zeros_like(sums)

            @pl.loop(0, mine)
            def _(p):
                at = pl.ds(pl.multiple_of(p * length, length), length)
                upstream, normal = work[at], normed[at]
                grad = norm_back(upstream, normal, inverse[at], vec[3:4])
                mid[at] = grad
                mid16[at] = grad.astype(BF16)
                sums[0:1] += sum_rows(grad)
                sums[1:2] += sum_rows(upstream * normal)
                sums[2:3] += sum_rows(upstream)

            mid_t[...] = mid16[...].T
            for h, ref in enumerate((a_own_ref, a_oth_ref)):
                back[:, h * cols : (h + 1) * cols] = jnp.dot(
                    mid16[...], ref[3], preferred_element_type=F32
                ).astype(BF16)

        mid, mid_t, back, sums_one = tape.run(
            surface,
            [((rows, width), F32), ((width, rows), BF16), ((rows, width), BF16), ((8, width), F32)],
            [sunk[0][0], sunk[1][0], b_own, b_oth, top, normed_one, inverse_one, vectors, a_own, a_oth],
            limit=14, flops=4 * rows * width * units + 2 * rows * width * width, moved=14 * MIB,
            scratch=[VMEM((rows, width), F32), VMEM((rows, width), BF16)],
        )

        def pair_up(s, own, oth, out):
            out[s[3]] = own[...]
            out[1 - s[3]] = oth[...]

        def paired(own, oth):
            shape = ((cores,) + own.shape, own.dtype)
            result = tape.run(pair_up, [shape], [own, oth], True, limit=8, spill=(0,))[0]
            return result.reshape(pairs, length, width)

        def values_back(probs_ref, back_ref, grad, sums):
            sums[...] = jnp.zeros_like(sums)

            @pl.loop(0, mine)
            def _(p):
                at = pl.ds(pl.multiple_of(p * length, length), length)
                for u in range(twins):
                    lanes = slice(u * LANES, (u + 1) * LANES)
                    value = join(lax.dot_general(
                        probs_ref[at, 2 * u * length : 2 * (u + 1) * length], back_ref[at, lanes], TN,
                        preferred_element_type=F32,
                    ))
                    grad[at, lanes] = value.astype(BF16)
                    sums[:, lanes] += sum_rows(value)

        grad_v, sum_v = tape.run(
            values_back, [((rows, width), BF16), ((1, width), F32)], [probs, back],
            limit=4, flops=4 * rows * length * width, moved=3 * MIB,
        )

        def attend_grad(h, kind, lefts, rights):
            def attend_grad_half(*refs):
                at = slice(h * cols, (h + 1) * cols)
                for left, right, out in zip(refs[:2], refs[2:4], refs[4:]):
                    out[...] = jnp.dot(left[...], right[:, at], preferred_element_type=F32).astype(out.dtype)

            return tape.run(
                attend_grad_half, [((width, cols), kind)] * 2, lefts + rights,
                limit=6, flops=4 * rows * width * cols, moved=5 * MIB,
            )

        lefts_vo, rights_vo = [x_t, mid_t], [grad_v, context]
        vo_oth = attend_grad(1, BF16, lefts_vo, rights_vo)
        layer_output = paired(output, output_oth)
        scatter_c.split(0)
        scatter_b.pair(sharded(up_own, 1))

        def attend_back(probs_ref, back_ref, qkv_ref, grad_q, grad_k, sums):
            sums[...] = jnp.zeros_like(sums)

            @pl.loop(0, mine)
            def _(p):
                at = pl.ds(pl.multiple_of(p * length, length), length)
                for u in range(twins):
                    lanes = slice(u * LANES, (u + 1) * LANES)
                    prob = probs_ref[at, 2 * u * length : 2 * (u + 1) * length].astype(F32)
                    both = lax.dot_general(
                        back_ref[at, lanes], split(qkv_ref[2, at, lanes]), NT, preferred_element_type=F32
                    )
                    parts = []
                    for h in range(2):
                        half = slice(h * length, (h + 1) * length)
                        inner = jnp.sum(prob[:, half] * both[:, half], axis=-1, keepdims=True)
                        parts.append(prob[:, half] * (both[:, half] - inner))
                    grad = jnp.concatenate(parts, axis=1).astype(BF16)
                    value = jnp.dot(grad, split(qkv_ref[1, at, lanes]), preferred_element_type=F32) * scale
                    grad_q[at, lanes] = value.astype(BF16)
                    sums[:, lanes] += sum_rows(value)
                    value = join(lax.dot_general(grad, qkv_ref[0, at, lanes], TN, preferred_element_type=F32))
                    grad_k[at, lanes] = (value * scale).astype(BF16)

        grad_q, grad_k, sum_q = tape.run(
            attend_back, [((rows, width), BF16), ((rows, width), BF16), ((1, width), F32)], [probs, back, qkv],
            limit=4, flops=16 * rows * length * width, moved=6 * MIB,
        )
        qk_oth = attend_grad(1, BF16, [x_t, x_t], [grad_q, grad_k])
        scatter_a = Scatter(grid, tape, sharded([*qk_oth, *vo_oth], 1))
        scatter_c.split(1)
        qk_own = attend_grad(0, F32, [x_t, x_t], [grad_q, grad_k])
        vo_own = attend_grad(0, F32, lefts_vo, rights_vo)


        def matrix_step(index):
            def step(*refs):
                grad = refs[0][...] + refs[1][...].astype(F32)
                master, first, second, moment, square, way, kept, tile_ref = refs[2:]
                moment[...], square[...], value = adam(grad, first[...], second[...])
                kept[...] = master[...]
                way[...] = value + DECAY * kept[...]
                tile_ref[...] = norm_row([(index, kept[0], way[0])])

            return step

        def stepped(step, parts, masters, shapes):
            outs = [(s, F32) for _ in range(4) for s in shapes] + [((1, LANES), F32)]
            n, m = len(parts), len(masters)
            return tape.run(
                step, outs, parts + masters, limit=6, spill=range(2 * len(shapes)), plain=range(n, n + m), moved=2 * MIB
            )

        ups = [v[None] for v in (expand_up, first_up, second_up)]
        downs = [v[None] for v in (expand_down, first_down, second_down)]
        scatter_b.split(0)
        scatter_a.pair(sharded([*qk_own, *vo_own], 1))
        scatter_c.split(2)

        def states_back(grad_q_ref, grad_k_ref, grad_v_ref, own, oth, mid_ref, out):
            @pl.loop(0, width // tile)
            def _(i):
                at = pl.ds(pl.multiple_of(i * tile, tile), tile)
                value = mid_ref[:, at]
                for j, ref in enumerate((grad_q_ref, grad_k_ref, grad_v_ref)):
                    for h, weight in enumerate((own, oth)):
                        value += lax.dot_general(
                            ref[:, h * cols : (h + 1) * cols], weight[j, at, :], NT, preferred_element_type=F32
                        )
                out[:, at] = value

        states_own = tape.run(
            states_back, [((rows, width), F32)], [grad_q, grad_k, grad_v, a_own, a_oth, mid],
            limit=8, flops=6 * rows * width * width, moved=8 * MIB,
        )[0]

        states_oth = grid.core(states_own)
        def collect(s, sum_q_ref, sum_v_ref, one, two, up_own_ref, up_oth_ref, out):
            for t in range(cores):

                @pl.when(s[3] == t)
                def _():
                    for row, ref in enumerate((sum_q_ref, sum_v_ref)):
                        for h in range(2):
                            out[row : row + 1, (h ^ t) * cols : ((h ^ t) + 1) * cols] = ref[
                                :, h * cols : (h + 1) * cols
                            ]
                    for h, ref in enumerate((up_own_ref, up_oth_ref)):
                        for i in range(units // width):
                            row = 8 + (h ^ t) * (units // width) + i
                            out[row : row + 1] = ref[:, i * width : (i + 1) * width]

            out[2:5] = one[0:3]
            out[5:8] = two[0:3]

        vector_part = tape.run(
            collect, [(vectors.shape, F32)], [sum_q, sum_v, sums_one, sums_two, sunk[0][1], sunk[1][1]], True
        )[0]
        vector_oth = grid.core(vector_part)
        half = vectors.shape[0] // cores

        def vector_half(s, own, oth, out):
            for t in range(cores):

                @pl.when(s[3] == t)
                def _():
                    at = slice(t * half, (t + 1) * half)
                    out[...] = own[at] + oth[at]

        vector_share = tape.run(vector_half, [((half, width), F32)], [vector_part, vector_oth], True)[0]
        moment_down, square_down, way_down, kept_down, tile_down = stepped(
            matrix_step(5), scatter_c.parts, downs, [downs[0].shape]
        )
        scatter_b.split(1)
        scatter_a.split_short()
        states_grad = paired(states_own, states_oth)
        scatter_b.split(2)
        scatter_a.split_long()
        moment_up, square_up, way_up, kept_up, tile_up = stepped(
            matrix_step(4), scatter_b.parts, ups, [ups[0].shape]
        )

        def attend_step(*refs):
            n = len(scatter_a.parts)
            m_in, f_in, s_in, m_out, f_out, s_out, tile_up_ref, tile_down_ref, share = refs[n : n + 9]
            mo_in, mo_out, sq_in, sq_out, way_in, way_out, kept_in, kept_out, load = refs[n + 9 :]
            entries = []
            for j in range(4):
                grad = sum((ref[j].astype(F32) for ref in refs[1:n]), refs[0][j])
                i = j if j < 3 else 0
                m, f, s, mo, sq, kept, way = (
                    (m_in, f_in, s_in, mo_in, sq_in, kept_in, way_in)
                    if j < 3
                    else (m_out, f_out, s_out, mo_out, sq_out, kept_out, way_out)
                )
                mo[i], sq[i], value = adam(grad, f[i], s[i])
                kept[i] = m[i]
                way[i] = value + DECAY * kept[i]
                entries.append((j, kept[i], way[i]))
            load[...] = jnp.zeros_like(load)
            load[0:half] = share[...]
            load[half : half + 1, 0:LANES] = norm_row(entries) + tile_up_ref[...] + tile_down_ref[...]

        shapes = [attend_in.shape, attend_out.shape]
        masters = [attend_in, first_in, second_in, attend_out, first_out, second_out]
        moment_in, moment_out, square_in, square_out, way_in, way_out, kept_in, kept_out, load = tape.run(
            attend_step, [(s, F32) for _ in range(4) for s in shapes] + [((8, width), F32)],
            scatter_a.parts + masters + [tile_up, tile_down, vector_share],
            limit=6, spill=range(4), plain=range(grid.long, grid.long + 6), moved=2 * MIB,
        )
        total = Total(grid, tape, load)
        total.line()
        total.sides()

        def update(s, own, oth, vec, vec_first, vec_second, *refs):
            masters, ways, outs, grad = refs[:4], refs[4:8], refs[8:-1], refs[-1]
            norms = jnp.sqrt(own[half : half + 1, 0:LANES] + oth[half : half + 1, 0:LANES])
            outs[8][0:1] = norms[:, 0:6]
            outs[8][1:2] = norms[:, 6:12]
            for i, first in enumerate((0, 3, 4, 5)):
                for j in range(masters[i].shape[0]):
                    m = first + j
                    trust = RATE * (norms[:, m : m + 1] / norms[:, 6 + m : 7 + m])
                    value = masters[i][j] - trust * ways[i][j]
                    outs[i][j], outs[4 + i][j] = value, value.astype(BF16)
            for t in range(cores):

                @pl.when(s[3] == t)
                def _():
                    grad[t * half : (t + 1) * half] = own[0:half]
                    grad[(1 - t) * half : (2 - t) * half] = oth[0:half]

            outs[10][...], outs[11][...], direction = adam(grad[...], vec_first[...], vec_second[...])
            outs[9][...] = vec[...] - RATE * direction

        masters = [kept_in, kept_out, kept_up, kept_down]
        results = tape.run(
            update,
            [(m.shape, F32) for m in masters] + [(m.shape, BF16) for m in masters] + [((2, 6), F32)]
            + [(vectors.shape, F32)] * 3,
            total.pair + [vectors, vector_first, vector_second] + masters + [way_in, way_out, way_up, way_down],
            True, limit=6, spill=range(12), plain=(2, 3, 4), moved=2 * MIB,
            scratch=[VMEM(vectors.shape, F32)],
        )
        updated_vectors, moment_vectors, square_vectors = results[9:12]

        def native(values):
            values = list(values)
            return (values[0], values[1][0].T, values[2][0], values[3][0])

        return (
            layer_output, states_grad, *native(results[:4]),
            *native([moment_in, moment_out, moment_up, moment_down]),
            *native([square_in, square_out, square_up, square_down]),
            *native(results[4:8]), updated_vectors, moment_vectors, square_vectors, results[8].T,
        )

    return body


def solution(mesh):
    rows = P("dp", None, None)
    matrices = (P(None, "dp", "tensor"), P("tensor", "dp"), P("dp", "tensor"), P(("tensor", "dp"), None))
    in_specs = (rows, rows, P("dp"), P("dp")) + matrices * 3 + (P(), P(), P())
    out_specs = (rows, rows) + matrices * 4 + (P(), P(), P(), P())
    body = make_body(Grid(mesh))
    return jax.shard_map(body, mesh=mesh, in_specs=in_specs, out_specs=out_specs, check_vma=False)
```

```python
import itertools
import math
import types

import jax
import jax.numpy as jnp
import numpy as np
from jax import lax
from jax.experimental import pallas as pl
from jax.experimental.pallas import tpu as pltpu
from jax.sharding import PartitionSpec as P

HEAD_DIM = 64
STEP = 10
NORM_EPS = 1e-05
BETA_ONE = 0.9
BETA_TWO = 0.999
ADAM_EPS = 1e-06
RATE = 0.3
DECAY = 0.01
MASKED = -1e30
AXES = ("dp", "tensor")
F32, BF16 = jnp.float32, jnp.bfloat16
VMEM = pltpu.VMEM
LANES = 128
NT = (((1,), (1,)), ((), ()))
TN = (((0,), (0,)), ((), ()))
MIB = 1 << 20
PATHS = ("zzab", "azzb", "azzb", "azzb")
COUNTS = (1, 4)
ORDER = (
    "castA", "prep", "castB", "a0", "b0", "a1", "castC", "c0", "b1", "c1", "b2", "wholeA", "project",
    "attend", "c2", "wholeB", "hide", "liftOwn", "liftOth", "turn", "wholeC", "lowerOwn", "lower", "sinkOth",
    "downOth", "downOwn", "upOth", "pairC", "sinkOwn", "upOwn", "pairB", "surface", "values", "voOth", "C0",
    "back", "qkOth", "qkOwn", "voOwn", "voSum", "B0", "C1", "pairA", "states", "collect", "share", "C2", "A0",
    "B1", "A1", "A2", "stepC", "B2", "pairS", "pairO", "stepB", "stepA",
)


class Grid:
    def __init__(self, mesh):
        self.dp, self.cores = mesh.shape["dp"], mesh.shape["tensor"]
        chips = mesh.devices.reshape(self.dp, self.cores)[:, 0]
        spots = [tuple(getattr(chip, "coords", ())) for chip in chips]
        if any(len(spot) != 3 for spot in spots) or len(set(spots)) != self.dp:
            side = 1 << ((self.dp.bit_length() - 1) // 3)
            spots = [(i % side, i // side % side, i // (side * side)) for i in range(self.dp)]
        spots = np.array(spots) - np.min(spots, axis=0)
        sizes = spots.max(axis=0) + 1
        order = sorted(range(3), key=lambda k: -sizes[k])
        order = order[:1] + sorted(order[1:])
        self.spots = spots[:, order].tolist()
        self.long, self.side, _ = (int(sizes[k]) for k in order)
        self.at = {tuple(spot): i for i, spot in enumerate(self.spots)}
        unit = [tuple(int(j == k) for j in range(3)) for k in range(3)]
        self.stride = [self.at.get(u, 0) for u in unit]
        self.sizes = [int(sizes[k]) for k in order]

    def send(self, value, hop):
        pairs = []
        for i, spot in enumerate(self.spots):
            for core in range(self.cores):
                offsets, turn = hop(core)
                target = self.at[tuple(u ^ v for u, v in zip(spot, offsets))]
                pairs.append((i * self.cores + core, target * self.cores + (core ^ turn)))
        return lax.ppermute(value, AXES, pairs)

    def place(self):
        index = lax.axis_index("dp")
        spot = [lax.rem(lax.div(index, s), n) if n > 1 else index * 0 for s, n in zip(self.stride, self.sizes)]
        return jnp.stack(spot + [lax.axis_index("tensor")]).astype(jnp.int32)

    def path(self, order="zzab"):
        bits = [[1 << b for b in reversed(range((n - 1).bit_length()))] for n in (self.long, self.side, self.side)]
        steps = [[(side, k) for k in bits[side]] for side in range(3)]
        stock = {"z": [steps[0][:-1], steps[0][-1:]], "a": [steps[1]], "b": [steps[2]]}
        return sum((stock[kind].pop(0) for kind in order), [])

    def exchange(self, value, step):
        side, k = step
        offsets = [(k, 0, 0), (0, k, 0), (0, 0, k)]
        return self.send(value, lambda core: (offsets[side if core == 0 else (0, 2, 1)[side]], 0))

    def bit(self, s, step):
        side, k = step
        spot = s[0] if side == 0 else jnp.where(s[3] == 0, s[side], s[3 - side])
        return lax.rem(lax.div(spot, k), 2)

    def spot(self, s, steps, bits):
        place = 0
        for (side, k), bit in zip(steps, bits):
            stride = self.stride[0] if side == 0 else jnp.where(s[3] == 0, self.stride[side], self.stride[3 - side])
            place = place + bit * k * stride
        return place

    def long_steps(self):
        return [step for step in self.path() if step[0] == 0]

    def long_bits(self, s, k):
        spot = s[0] ^ k
        return tuple(lax.rem(lax.div(spot, distance), 2) for _, distance in reversed(self.long_steps()))

    def along(self, k):
        return lambda core: ((k, 0, 0), 0)

    def cross(self, j, k):
        return lambda core: ((0, j, k), 0)

    def core(self, value):
        return self.send(value, lambda core: ((0, 0, 0), 1))


class Tape:
    def __init__(self, place):
        self.place = place
        self.token = None

    def run(self, body, outs, ins, place=False, limit=4, flops=0, moved=0, exps=0, scratch=(), spill=(), plain=(), name=None):
        ins = [v if i in plain else pltpu.with_memory_space_constraint(v, VMEM) for i, v in enumerate(ins)]
        specs = [pl.BlockSpec(memory_space=VMEM)] * len(ins)
        first = []
        if place:
            first.append((self.place, pltpu.SMEM))
        if self.token is not None:
            first.append((pltpu.with_memory_space_constraint(self.token, VMEM), VMEM))
        chained = self.token is not None
        count, results = len(ins), len(outs)

        def chain(*refs):
            refs = list(refs)
            head = [refs.pop(0)] if place else []
            if chained:
                refs.pop(0)
            last = refs.pop(count + results)
            last[...] = jnp.zeros_like(last)
            body(*head, *refs)

        shapes = [
            jax.ShapeDtypeStruct(s, d) if i in spill else VMEM(s, d) for i, (s, d) in enumerate(outs)
        ] + [VMEM((8, LANES), F32)]
        *values, self.token = pl.pallas_call(
            chain,
            out_shape=shapes,
            in_specs=[pl.BlockSpec(memory_space=m) for _, m in first] + specs,
            out_specs=[pl.BlockSpec(memory_space=VMEM)] * len(shapes),
            scratch_shapes=list(scratch),
            name=name or body.__name__,
            cost_estimate=pl.CostEstimate(flops=flops, bytes_accessed=moved, transcendentals=0),
            compiler_params=pltpu.CompilerParams(vmem_limit_bytes=limit * MIB),
        )(*[v for v, _ in first], *ins)
        return values


def part(count, group, groups=3):
    return range(count * group // groups, count * (group + 1) // groups)


class Gather:
    def __init__(self, grid, tape, shard, direct=False, order="zzab"):
        self.grid, self.tape, self.block = grid, tape, shard
        self.path = grid.path(order)
        if direct:
            self.got = [grid.send(shard, grid.along(k)) for k in range(1, grid.long)]
        else:
            self.got = grid.exchange(shard, self.path[0])

    def merge_long(self):
        grid = self.grid
        steps = grid.long_steps()

        def gather_long(s, *refs):
            for k, ref in enumerate(refs[:-1]):
                refs[-1][grid.long_bits(s, k)] = ref[...]

        shape = (2,) * len(steps) + self.block.shape
        self.block = self.tape.run(gather_long, [(shape, BF16)], [self.block] + self.got, True)[0]
        self.got = grid.exchange(self.block, self.path[len(steps)])

    def merge(self, group):
        self.merges(part(len(self.path) - 1, group))

    def merge_short(self):
        self.merges(range(len(self.grid.long_steps()), len(self.path) - 1))

    def merges(self, steps):
        grid = self.grid
        for i in steps:
            step = self.path[i]

            def gather_merge(s, own, got, out):
                bit = grid.bit(s, step)
                out[bit] = own[...]
                out[1 - bit] = got[...]

            shape = (2,) + self.block.shape
            self.block = self.tape.run(gather_merge, [(shape, BF16)], [self.block, self.got], True)[0]
            self.got = grid.exchange(self.block, self.path[i + 1])

    def whole(self):
        grid, path = self.grid, self.path
        many, rows, width = self.block.shape[-3:]

        def gather_whole(s, own, got, out):
            last = grid.bit(s, path[-1])
            for bits in itertools.product(range(2), repeat=len(path) - 1):
                for ref, bit in ((own, last), (got, 1 - last)):
                    spot = grid.spot(s, path, bits[::-1] + (bit,))
                    for j in range(many):
                        out[j, spot] = ref[bits + (j,)]

        shape = (many, grid.dp, rows, width)
        full = self.tape.run(gather_whole, [(shape, BF16)], [self.block, self.got], True)[0]
        return full, grid.core(full)


class Scatter:
    def __init__(self, grid, tape, other, order="zzab"):
        self.grid, self.tape = grid, tape
        self.path = grid.path(order)
        self.got = [grid.core(v) for v, _, _ in other]
        self.spots = [(j, c) for _, j, c in other]

    def pair(self, own):
        grid, path = self.grid, self.path
        _, _, rows, width = own[0].shape
        own_spots = [(g, i) for g, v in enumerate(own) for i in range(v.shape[0])]
        many, pieces, got = len(own_spots), len(own), len(self.got)
        shapes = [v.shape for v in self.got]
        shape = (2,) * (len(path) - 1) + (many, rows, width)

        def scatter_pair(s, *refs):
            own_refs, got_refs, (keep, send) = refs[:pieces], refs[pieces : pieces + got], refs[pieces + got :]
            last = grid.bit(s, path[-1])
            for bits in itertools.product(range(2), repeat=len(path) - 1):
                for out, bit in ((keep, last), (send, 1 - last)):
                    spot = grid.spot(s, path, bits[::-1] + (bit,))
                    for j, (g, i) in enumerate(own_spots):
                        found = False
                        for ref, (first, column), piece in zip(got_refs, self.spots, shapes):
                            if first <= j < first + piece[0]:
                                at = slice(column, column + piece[3])
                                total = own_refs[g][i, spot, :, at] + ref[j - first, spot].astype(F32)
                                out[bits + (j, slice(None), at)] = total.astype(out.dtype)
                                found = True
                        if not found:
                            out[bits + (j,)] = own_refs[g][i, spot].astype(out.dtype)

        self.keep, value = self.tape.run(scatter_pair, [(shape, F32), (shape, BF16)], own + self.got, True)
        self.got = grid.exchange(value, path[-1])

    def split(self, group):
        self.splits(part(len(self.path) - 1, group))

    def split_short(self):
        self.splits(range(len(self.path) - 1 - len(self.grid.long_steps())))

    def split_long(self):
        grid, count = self.grid, len(self.grid.long_steps())

        def scatter_long(s, own, got, *outs):
            for k, out in enumerate(outs):
                at = grid.long_bits(s, k)
                out[...] = (own[at] + got[at].astype(F32)).astype(out.dtype)

        shape = self.keep.shape[count:]
        keep, *values = self.tape.run(
            scatter_long, [(shape, F32)] + [(shape, BF16)] * (grid.long - 1), [self.keep, self.got], True
        )
        self.parts = [keep] + [grid.send(v, grid.along(k + 1)) for k, v in enumerate(values)]

    def splits(self, steps):
        grid = self.grid
        for i in steps:
            step = self.path[len(self.path) - 2 - i]

            def scatter_split(s, own, got, keep, send):
                bit = grid.bit(s, step)
                keep[...] = own[bit] + got[bit].astype(F32)
                send[...] = (own[1 - bit] + got[1 - bit].astype(F32)).astype(BF16)

            shape = self.keep.shape[1:]
            self.keep, value = self.tape.run(
                scatter_split, [(shape, F32), (shape, BF16)], [self.keep, self.got], True
            )
            self.got = grid.exchange(value, step)
        self.parts = [self.keep, self.got]


def tree(values):
    values = list(values)
    while len(values) > 1:
        values = [a + b for a, b in zip(values[::2], values[1::2])]
    return values[0]


class Total:
    def __init__(self, grid, tape, value):
        self.grid, self.tape = grid, tape
        self.got = [value] + [grid.send(value, grid.along(k)) for k in range(1, grid.long)]

    def add(self):
        def body(*refs):
            refs[-1][...] = tree(ref[...] for ref in refs[:-1])

        return self.tape.run(body, [(self.got[0].shape, F32)], self.got)[0]

    def line(self):
        grid, value = self.grid, self.add()
        offsets = [(j, k) for j in range(grid.side) for k in range(grid.side)]
        self.got = [value] + [grid.send(value, grid.cross(j, k)) for j, k in offsets[1:]]

    def sides(self):
        value = self.add()
        self.pair = [value, self.grid.core(value)]


def normed_of(values):
    center = values - jnp.mean(values, axis=-1, keepdims=True)
    inverse = lax.rsqrt(jnp.mean(center * center, axis=-1, keepdims=True) + NORM_EPS)
    return center * inverse, inverse


def norm_back(upstream, normed, inverse, gain):
    scaled = upstream * gain
    inner = jnp.mean(scaled * normed, axis=-1, keepdims=True)
    return inverse * (scaled - jnp.mean(scaled, axis=-1, keepdims=True) - normed * inner)


def sum_rows(values):
    return jnp.sum(values, axis=0, keepdims=True)


def adam(grad, first, second):
    first_new = BETA_ONE * first + (1.0 - BETA_ONE) * grad
    second_new = BETA_TWO * second + (1.0 - BETA_TWO) * grad * grad
    corrected = first_new / (1.0 - BETA_ONE**STEP)
    spread = jnp.sqrt(second_new / (1.0 - BETA_TWO**STEP))
    return first_new, second_new, corrected / (spread + ADAM_EPS)


def squares(values):
    return jnp.sum(sum_rows(values * values), axis=1, keepdims=True)


def norm_row(entries):
    lane = lax.broadcasted_iota(jnp.int32, (1, LANES), 1)
    row = jnp.zeros((1, LANES), F32)
    for index, weight, direction in entries:
        row = jnp.where(lane == index, squares(weight), row)
        row = jnp.where(lane == index + 6, squares(direction), row)
    return row


def make_body(grid):
    def body(
        states, cotangent, word_counts, region_counts,
        attend_in, attend_out, expand_up, expand_down,
        first_in, first_out, first_up, first_down,
        second_in, second_out, second_up, second_down,
        vectors, vector_first, vector_second,
    ):
        w = types.SimpleNamespace()
        paths, counts_of = PATHS, COUNTS
        cores = grid.cores
        pairs, length, width = states.shape
        mine = pairs // cores
        rows = mine * length
        cols = attend_in.shape[2]
        units = expand_up.shape[1]
        twins = width // LANES
        scale = HEAD_DIM**-0.5
        rank = lax.axis_index("tensor")
        counts = lax.dynamic_slice_in_dim(word_counts + region_counts, rank * mine, mine, 0)
        tape = Tape(jnp.concatenate([grid.place(), counts]))
        attend_out, first_out, second_out = (v.T[None] for v in (attend_out, first_out, second_out))

        def cast(*refs):
            spot = 0
            for ref in refs[:-1]:
                refs[-1][spot : spot + ref.shape[0]] = ref[...].astype(BF16)
                spot += ref.shape[0]

        def casted(*mats):
            many = sum(m.shape[0] for m in mats)
            shape = (many,) + mats[0].shape[1:]
            return tape.run(cast, [(shape, BF16)], mats, plain=range(len(mats)))[0]

        def cast_a():
            w.gather_a = Gather(grid, tape, casted(attend_in, attend_out), direct=True)

        def cast_b():
            w.gather_b = Gather(grid, tape, casted(expand_up[None]), order=paths[0])

        def cast_c():
            w.gather_c = Gather(grid, tape, casted(expand_down[None]), order=paths[1])


        def prepare(s, states_ref, cot_ref, vec, x_ref, x_t, mine_cot, bias_in, bias_up):
            @pl.loop(0, mine)
            def _(p):
                at = pl.ds(pl.multiple_of(p * length, length), length)
                x_ref[at, :] = states_ref[s[3] * mine + p]
                mine_cot[at, :] = cot_ref[s[3] * mine + p]

            x_t[...] = x_ref[...].T
            bias_in[1:2] = jnp.zeros((1, width), F32)
            for t in range(cores):

                @pl.when(s[3] == t)
                def _():
                    for h in range(2):
                        at, source = slice(h * cols, (h + 1) * cols), slice((h ^ t) * cols, ((h ^ t) + 1) * cols)
                        bias_in[0:1, at] = vec[0:1, source]
                        bias_in[2:3, at] = vec[1:2, source]
                        for i in range(units // width):
                            row = 8 + (h ^ t) * (units // width) + i
                            spot = h * units + i * width
                            bias_up[:, spot : spot + width] = vec[row : row + 1]

        def prepared():
            w.x, w.x_t, w.cot, w.bias_in, w.bias_up = tape.run(
                prepare,
                [((rows, width), BF16), ((width, rows), BF16), ((rows, width), BF16), ((3, width), F32),
                 ((1, 2 * units), F32)],
                [states, cotangent, vectors], True, limit=12, moved=6 * MIB, plain=(0, 1),
            )

        def whole_a():
            w.a_own, w.a_oth = (v.reshape(4, width, cols) for v in w.gather_a.whole())

        def whole_b():
            w.b_own, w.b_oth = (v.reshape(width, units) for v in w.gather_b.whole())

        def whole_c():
            w.c_own, w.c_oth = (v.reshape(units, width) for v in w.gather_c.whole())

        def project(x_ref, own, oth, bias, out):
            @pl.loop(0, 3)
            def _(j):
                for h, ref in enumerate((own, oth)):
                    at = slice(h * cols, (h + 1) * cols)
                    value = jnp.dot(x_ref[...], ref[j], preferred_element_type=F32)
                    out[j, :, at] = (value + bias[pl.ds(j, 1), at]).astype(BF16)

        def projected():
            w.qkv = tape.run(
                project, [((3, rows, width), BF16)], [w.x, w.a_own, w.a_oth, w.bias_in],
                limit=8, flops=6 * rows * width * width, moved=8 * MIB,
            )[0]

        def split(v):
            low = lax.broadcasted_iota(jnp.int32, v.shape, 1) < HEAD_DIM
            zero = jnp.zeros_like(v)
            return jnp.concatenate([jnp.where(low, v, zero), jnp.where(low, zero, v)], axis=0)

        def join(v):
            low = lax.broadcasted_iota(jnp.int32, (length, LANES), 1) < HEAD_DIM
            return jnp.where(low, v[:length], v[length:])

        def attend(count, qkv_ref, probs, context):
            @pl.loop(0, mine)
            def _(p):
                at = pl.ds(pl.multiple_of(p * length, length), length)
                known = lax.broadcasted_iota(jnp.int32, (length, length), 1) < count[4 + p]
                for u in range(twins):
                    lanes = slice(u * LANES, (u + 1) * LANES)
                    both = lax.dot_general(
                        qkv_ref[0, at, lanes], split(qkv_ref[1, at, lanes]), NT, preferred_element_type=F32
                    )
                    soft = []
                    for h in range(2):
                        score = jnp.where(known, both[:, h * length : (h + 1) * length] * scale, MASKED)
                        power = jnp.exp(score - jnp.max(score, axis=-1, keepdims=True))
                        soft.append(power / jnp.sum(power, axis=-1, keepdims=True))
                    prob = jnp.concatenate(soft, axis=1).astype(BF16)
                    probs[at, 2 * u * length : 2 * (u + 1) * length] = prob
                    context[at, lanes] = jnp.dot(
                        prob, split(qkv_ref[2, at, lanes]), preferred_element_type=F32
                    ).astype(BF16)

        def attended():
            w.probs, w.context = tape.run(
                attend, [((rows, 2 * twins * length), BF16), ((rows, width), BF16)], [w.qkv], True,
                limit=4, flops=4 * rows * length * width * 4, moved=5 * MIB, exps=rows * twins * 2 * length,
            )

        block = min(rows, 256)

        def hide(context_ref, x_ref, own, oth, vec, hidden, normed, inverse):
            for r in range(0, rows, block):
                at = slice(r, r + block)
                value = x_ref[at].astype(F32) + vec[2:3]
                for h, ref in enumerate((own, oth)):
                    value += lax.dot_general(
                        context_ref[at, h * cols : (h + 1) * cols], ref[3], NT, preferred_element_type=F32
                    )
                normal, spread = normed_of(value)
                normed[at], inverse[at] = normal, spread
                hidden[at] = (normal * vec[3:4] + vec[4:5]).astype(BF16)

        def hid():
            w.hidden, w.normed_one, w.inverse_one = tape.run(
                hide,
                [((rows, width), BF16), ((rows, width), F32), ((rows, 1), F32)],
                [w.context, w.x, w.a_own, w.a_oth, vectors],
                limit=8, flops=2 * rows * width * width, moved=6 * MIB,
            )

        tile = 256

        def lift(hidden_ref, up, bias, active, active_t, slope):
            @pl.loop(0, units // tile)
            def _(i):
                at = pl.ds(pl.multiple_of(i * tile, tile), tile)
                value = jnp.dot(hidden_ref[...], up[:, at], preferred_element_type=F32) + bias[:, at]
                half = 0.5 * (1.0 + lax.erf(value * math.sqrt(0.5)))
                result = (value * half).astype(BF16)
                active[:, at] = result
                active_t[at, :] = result.T
                bell = jnp.exp(-0.5 * value * value) * (1.0 / math.sqrt(2.0 * math.pi))
                slope[:, at] = (half + value * bell).astype(BF16)

        def lift_half(h, up):
            return tape.run(
                lambda hidden_ref, up_ref, bias, *outs: lift(hidden_ref, up_ref, bias.at[:, h * units : (h + 1) * units], *outs),
                [((rows, units), BF16), ((units, rows), BF16), ((rows, units), BF16)],
                [w.hidden, up, w.bias_up],
                limit=8, flops=2 * rows * width * units, moved=8 * MIB, exps=2 * rows * units,
            )

        def turn(value, out):
            out[...] = value[...].T

        def lift_own():
            w.lift_own = lift_half(0, w.b_own)

        def lift_oth():
            w.lift_oth = lift_half(1, w.b_oth)

        def turned():
            w.hidden_t = tape.run(turn, [((width, rows), BF16)], [w.hidden], limit=8)[0]

        def lower_half(active, down, out):
            @pl.loop(0, width // tile)
            def _(i):
                at = pl.ds(pl.multiple_of(i * tile, tile), tile)
                out[:, at] = jnp.dot(active[...], down[:, at], preferred_element_type=F32)

        def lowered_own():
            w.lowered = tape.run(
                lower_half, [((rows, width), F32)], [w.lift_own[0], w.c_own],
                limit=6, flops=2 * rows * width * units, moved=6 * MIB,
            )[0]

        def lower(count, lowered_ref, active, down, normed, cot_ref, vec, output, top, top16, sums, work):
            @pl.loop(0, width // tile)
            def _(i):
                at = pl.ds(pl.multiple_of(i * tile, tile), tile)
                work[:, at] = lowered_ref[:, at] + jnp.dot(active[...], down[:, at], preferred_element_type=F32)

            sums[...] = jnp.zeros_like(sums)

            @pl.loop(0, mine)
            def _(p):
                at = pl.ds(pl.multiple_of(p * length, length), length)
                value = normed[at] * vec[3:4] + vec[4:5] + work[at] + vec[5:6]
                normal, spread = normed_of(value)
                output[at] = (normal * vec[6:7] + vec[7:8]).astype(BF16)
                live = lax.broadcasted_iota(jnp.int32, (length, 1), 0) < count[4 + p]
                upstream = jnp.where(live, cot_ref[at].astype(F32), 0.0)
                grad = norm_back(upstream, normal, spread, vec[6:7])
                top[at] = grad
                top16[at] = grad.astype(BF16)
                sums[0:1] += sum_rows(grad)
                sums[1:2] += sum_rows(upstream * normal)
                sums[2:3] += sum_rows(upstream)

        def lowered_all():
            w.output, w.top, w.top16, w.sums_two = tape.run(
                lower,
                [((rows, width), BF16), ((rows, width), F32), ((rows, width), BF16), ((8, width), F32)],
                [w.lowered, w.lift_oth[0], w.c_oth, w.normed_one, w.cot, vectors],
                True, limit=8, flops=2 * rows * width * units, moved=14 * MIB,
                scratch=[VMEM((rows, width), F32)],
            )

        def product(left, right, *outs):
            step = min(left.shape[0], 256)

            @pl.loop(0, left.shape[0] // step)
            def _(i):
                at = pl.ds(pl.multiple_of(i * step, step), step)
                value = jnp.dot(left[at, :], right[...], preferred_element_type=F32)
                share = value.shape[1] // len(outs)
                for g, out in enumerate(outs):
                    out[at, :] = value[:, g * share : (g + 1) * share].astype(out.dtype)

        def weight_grad(left, right, kind, pieces=2):
            shape = (left.shape[0], right.shape[1])
            return tape.run(
                product, [((shape[0], shape[1] // pieces), kind)] * pieces, [left, right],
                limit=6, flops=2 * shape[0] * shape[1] * rows, moved=8 * MIB,
            )

        sharded = lambda values, many: [v.reshape(many, grid.dp, -1, v.shape[-1]) for v in values]
        numbered = lambda values: [(v, i, 0) for i, v in enumerate(values)]

        def down_oth():
            other = sharded(weight_grad(w.lift_oth[1], w.top16, BF16, counts_of[0]), 1)
            w.scatter_c = Scatter(grid, tape, numbered(other), order=paths[3])

        def down_own():
            w.down_own = weight_grad(w.lift_own[1], w.top16, F32, counts_of[0])

        def pair_c():
            w.scatter_c.pair(sharded(w.down_own, 1))

        def up_oth():
            other = sharded(weight_grad(w.hidden_t, w.sink_oth[0], BF16, counts_of[1]), 1)
            w.scatter_b = Scatter(grid, tape, numbered(other), order=paths[2])

        def up_own():
            w.up_own = weight_grad(w.hidden_t, w.sink_own[0], F32, counts_of[1])

        def pair_b():
            w.scatter_b.pair(sharded(w.up_own, 1))

        def sink(top16_ref, down, slope, grad, sums):
            @pl.loop(0, units // tile)
            def _(i):
                at = pl.ds(pl.multiple_of(i * tile, tile), tile)
                value = lax.dot_general(top16_ref[...], down[at, :], NT, preferred_element_type=F32)
                value = value * slope[:, at].astype(F32)
                grad[:, at] = value.astype(BF16)
                sums[:, at] = sum_rows(value)

        def sink_half(lifted, down):
            return tape.run(
                sink, [((rows, units), BF16), ((1, units), F32)], [w.top16, down, lifted[2]], limit=8
            )

        def sink_own():
            w.sink_own = sink_half(w.lift_own, w.c_own)

        def sink_oth():
            w.sink_oth = sink_half(w.lift_oth, w.c_oth)

        def surface(grad_own, grad_oth, own, oth, top_ref, normed, inverse, vec, a_own_ref, a_oth_ref,
                    mid, mid_t, back, sums, work, mid16):
            @pl.loop(0, width // tile)
            def _(i):
                at = pl.ds(pl.multiple_of(i * tile, tile), tile)
                work[:, at] = (
                    top_ref[:, at]
                    + lax.dot_general(grad_own[...], own[at, :], NT, preferred_element_type=F32)
                    + lax.dot_general(grad_oth[...], oth[at, :], NT, preferred_element_type=F32)
                )

            sums[...] = jnp.zeros_like(sums)

            @pl.loop(0, mine)
            def _(p):
                at = pl.ds(pl.multiple_of(p * length, length), length)
                upstream, normal = work[at], normed[at]
                grad = norm_back(upstream, normal, inverse[at], vec[3:4])
                mid[at] = grad
                mid16[at] = grad.astype(BF16)
                sums[0:1] += sum_rows(grad)
                sums[1:2] += sum_rows(upstream * normal)
                sums[2:3] += sum_rows(upstream)

            mid_t[...] = mid16[...].T
            for h, ref in enumerate((a_own_ref, a_oth_ref)):
                back[:, h * cols : (h + 1) * cols] = jnp.dot(
                    mid16[...], ref[3], preferred_element_type=F32
                ).astype(BF16)

        def surfaced():
            w.mid, w.mid_t, w.back, w.sums_one = tape.run(
                surface,
                [((rows, width), F32), ((width, rows), BF16), ((rows, width), BF16), ((8, width), F32)],
                [w.sink_own[0], w.sink_oth[0], w.b_own, w.b_oth, w.top, w.normed_one, w.inverse_one, vectors,
                 w.a_own, w.a_oth],
                limit=14, flops=4 * rows * width * units + 2 * rows * width * width, moved=14 * MIB,
                scratch=[VMEM((rows, width), F32), VMEM((rows, width), BF16)],
            )

        def pair_up(s, own, oth, out):
            out[s[3]] = own[...].astype(out.dtype)
            out[1 - s[3]] = oth[...].astype(out.dtype)

        def paired(own, oth, kind):
            shape = ((cores,) + own.shape, kind)
            result = tape.run(pair_up, [shape], [own, oth], True, limit=8, spill=(0,))[0]
            return result.reshape(pairs, length, width)

        def values_back(probs_ref, back_ref, grad, sums):
            sums[...] = jnp.zeros_like(sums)

            @pl.loop(0, mine)
            def _(p):
                at = pl.ds(pl.multiple_of(p * length, length), length)
                for u in range(twins):
                    lanes = slice(u * LANES, (u + 1) * LANES)
                    value = join(lax.dot_general(
                        probs_ref[at, 2 * u * length : 2 * (u + 1) * length], back_ref[at, lanes], TN,
                        preferred_element_type=F32,
                    ))
                    grad[at, lanes] = value.astype(BF16)
                    sums[:, lanes] += sum_rows(value)

        def valued():
            w.grad_v, w.sum_v = tape.run(
                values_back, [((rows, width), BF16), ((1, width), F32)], [w.probs, w.back],
                limit=4, flops=4 * rows * length * width, moved=3 * MIB,
            )

        def attend_grad(h, kind, lefts, rights, pieces=1):
            def attend_grad_half(*refs):
                at = slice(h * cols, (h + 1) * cols)
                share = cols // pieces
                for j, (left, right) in enumerate(zip(refs[:2], refs[2:4])):
                    value = jnp.dot(left[...], right[:, at], preferred_element_type=F32)
                    for g, out in enumerate(refs[4:]):
                        out[j] = value[:, g * share : (g + 1) * share].astype(kind)

            return tape.run(
                attend_grad_half, [((2, width, cols // pieces), kind)] * pieces, lefts + rights, limit=6
            )

        def vo_oth():
            w.vo_oth = grid.core(attend_grad(1, BF16, [w.x_t, w.mid_t], [w.grad_v, w.context])[0])

        def vo_own():
            w.vo_own = attend_grad(0, F32, [w.x_t, w.mid_t], [w.grad_v, w.context])

        def qk_oth():
            pieces = cols // LANES
            other = sharded(attend_grad(1, BF16, [w.x_t, w.x_t], [w.grad_q, w.grad_k], pieces), 2)
            w.scatter_a = Scatter(grid, tape, [(v, 0, LANES * i) for i, v in enumerate(other)])

        def qk_own():
            w.qk_own = attend_grad(0, F32, [w.x_t, w.x_t], [w.grad_q, w.grad_k])

        def vo_sum():
            w.vo_sum = tape.run(add_up, [((2, width, cols), F32)], [w.vo_own[0], w.vo_oth])

        def pair_a():
            w.scatter_a.pair(sharded(w.qk_own + w.vo_sum, 2))

        def attend_back(probs_ref, back_ref, qkv_ref, grad_q, grad_k, sums):
            sums[...] = jnp.zeros_like(sums)

            @pl.loop(0, mine)
            def _(p):
                at = pl.ds(pl.multiple_of(p * length, length), length)
                for u in range(twins):
                    lanes = slice(u * LANES, (u + 1) * LANES)
                    prob = probs_ref[at, 2 * u * length : 2 * (u + 1) * length].astype(F32)
                    both = lax.dot_general(
                        back_ref[at, lanes], split(qkv_ref[2, at, lanes]), NT, preferred_element_type=F32
                    )
                    parts = []
                    for h in range(2):
                        half = slice(h * length, (h + 1) * length)
                        inner = jnp.sum(prob[:, half] * both[:, half], axis=-1, keepdims=True)
                        parts.append(prob[:, half] * (both[:, half] - inner))
                    grad = jnp.concatenate(parts, axis=1).astype(BF16)
                    value = jnp.dot(grad, split(qkv_ref[1, at, lanes]), preferred_element_type=F32) * scale
                    grad_q[at, lanes] = value.astype(BF16)
                    sums[:, lanes] += sum_rows(value)
                    value = join(lax.dot_general(grad, qkv_ref[0, at, lanes], TN, preferred_element_type=F32))
                    grad_k[at, lanes] = (value * scale).astype(BF16)

        def attended_back():
            w.grad_q, w.grad_k, w.sum_q = tape.run(
                attend_back, [((rows, width), BF16), ((rows, width), BF16), ((1, width), F32)], [w.probs, w.back, w.qkv],
                limit=4, flops=16 * rows * length * width, moved=6 * MIB,
            )
        def add_up(own, oth, out):
            out[...] = own[...] + oth[...].astype(F32)

        def states_back(grad_q_ref, grad_k_ref, grad_v_ref, own, oth, mid_ref, out):
            @pl.loop(0, width // tile)
            def _(i):
                at = pl.ds(pl.multiple_of(i * tile, tile), tile)
                value = mid_ref[:, at]
                for j, ref in enumerate((grad_q_ref, grad_k_ref, grad_v_ref)):
                    for h, weight in enumerate((own, oth)):
                        value += lax.dot_general(
                            ref[:, h * cols : (h + 1) * cols], weight[j, at, :], NT, preferred_element_type=F32
                        )
                out[:, at] = value.astype(BF16)

        def states_own():
            w.states_own = tape.run(
                states_back, [((rows, width), BF16)], [w.grad_q, w.grad_k, w.grad_v, w.a_own, w.a_oth, w.mid],
                limit=8, flops=6 * rows * width * width, moved=8 * MIB,
            )[0]

        def matrix_step(index):
            def step(*refs):
                grad = refs[0][...] + refs[1][...].astype(F32)
                grad = jnp.concatenate([grad[j] for j in range(grad.shape[0])], axis=-1)[None]
                master, first, second, moment, square, way, kept, tile_ref = refs[2:]
                moment[...], square[...], value = adam(grad, first[...], second[...])
                kept[...] = master[...]
                way[...] = value + DECAY * kept[...]
                tile_ref[...] = norm_row([(index, kept[0], way[0])])

            return step

        def stepped(step, parts, masters, shapes):
            outs = [(s, F32) for _ in range(4) for s in shapes] + [((1, LANES), F32)]
            n, m = len(parts), len(masters)
            return tape.run(
                step, outs, parts + masters, limit=6, spill=range(2 * len(shapes)), plain=range(n, n + m), moved=2 * MIB
            )

        ups = [v[None] for v in (expand_up, first_up, second_up)]
        downs = [v[None] for v in (expand_down, first_down, second_down)]

        def collect(s, sum_q_ref, sum_v_ref, one, two, up_own_ref, up_oth_ref, out):
            for t in range(cores):

                @pl.when(s[3] == t)
                def _():
                    for row, ref in enumerate((sum_q_ref, sum_v_ref)):
                        for h in range(2):
                            out[row : row + 1, (h ^ t) * cols : ((h ^ t) + 1) * cols] = ref[
                                :, h * cols : (h + 1) * cols
                            ]
                    for h, ref in enumerate((up_own_ref, up_oth_ref)):
                        for i in range(units // width):
                            row = 8 + (h ^ t) * (units // width) + i
                            out[row : row + 1] = ref[:, i * width : (i + 1) * width]

            out[2:5] = one[0:3]
            out[5:8] = two[0:3]

        half = vectors.shape[0] // cores

        def collected():
            w.vector_part = tape.run(
                    collect, [(vectors.shape, F32)],
                    [w.sum_q, w.sum_v, w.sums_one, w.sums_two, w.sink_own[1], w.sink_oth[1]], True,
            )[0]

        def vector_half(s, own, oth, out):
            for t in range(cores):

                @pl.when(s[3] == t)
                def _():
                    at = slice(t * half, (t + 1) * half)
                    out[...] = own[at] + oth[at]

        def vector_shared():
            parts = [w.vector_part, grid.core(w.vector_part)]
            w.vector_share = tape.run(vector_half, [((half, width), F32)], parts, True)[0]

        def step_c():
            w.step_c = stepped(matrix_step(5), w.scatter_c.parts, downs, [downs[0].shape])

        def step_b():
            w.step_b = stepped(matrix_step(4), w.scatter_b.parts, ups, [ups[0].shape])

        def states_pair():
            w.states_grad = paired(w.states_own, grid.core(w.states_own), F32)

        def output_pair():
            w.layer_output = paired(w.output, grid.core(w.output), BF16)

        def attend_step(*refs):
            n = len(w.scatter_a.parts)
            m_in, f_in, s_in, m_out, f_out, s_out, tile_up_ref, tile_down_ref, share = refs[n : n + 9]
            mo_in, mo_out, sq_in, sq_out, way_in, way_out, kept_in, kept_out, load = refs[n + 9 :]
            entries = []
            for j in range(4):
                grad = sum((ref[j].astype(F32) for ref in refs[1:n]), refs[0][j])
                i = j if j < 3 else 0
                m, f, s, mo, sq, kept, way = (
                    (m_in, f_in, s_in, mo_in, sq_in, kept_in, way_in)
                    if j < 3
                    else (m_out, f_out, s_out, mo_out, sq_out, kept_out, way_out)
                )
                mo[i], sq[i], value = adam(grad, f[i], s[i])
                kept[i] = m[i]
                way[i] = value + DECAY * kept[i]
                entries.append((j, kept[i], way[i]))
            load[...] = jnp.zeros_like(load)
            load[0:half] = share[...]
            load[half : half + 1, 0:LANES] = norm_row(entries) + tile_up_ref[...] + tile_down_ref[...]

        shapes = [attend_in.shape, attend_out.shape]
        masters = [attend_in, first_in, second_in, attend_out, first_out, second_out]
        def step_a():
            w.step_a = tape.run(
                attend_step, [(s, F32) for _ in range(4) for s in shapes] + [((8, width), F32)],
                w.scatter_a.parts + masters + [w.step_b[4], w.step_c[4], w.vector_share],
                limit=6, spill=range(4), plain=range(len(w.scatter_a.parts), len(w.scatter_a.parts) + 6),
            )

        stages = {
            "a0": lambda: w.gather_a.merge_long(), "a1": lambda: w.gather_a.merge_short(),
            "b0": lambda: w.gather_b.merge(0), "b1": lambda: w.gather_b.merge(1), "b2": lambda: w.gather_b.merge(2),
            "c0": lambda: w.gather_c.merge(0), "c1": lambda: w.gather_c.merge(1), "c2": lambda: w.gather_c.merge(2),
            "A0": lambda: w.scatter_a.split(0), "A1": lambda: w.scatter_a.split(1), "A2": lambda: w.scatter_a.split(2),
            "B0": lambda: w.scatter_b.split(0), "B1": lambda: w.scatter_b.split(1), "B2": lambda: w.scatter_b.split(2),
            "C0": lambda: w.scatter_c.split(0), "C1": lambda: w.scatter_c.split(1), "C2": lambda: w.scatter_c.split(2),
            "castA": cast_a, "castB": cast_b, "castC": cast_c, "prep": prepared, "wholeA": whole_a, "wholeB": whole_b,
            "wholeC": whole_c, "project": projected, "attend": attended, "hide": hid, "liftOwn": lift_own,
            "liftOth": lift_oth, "turn": turned, "lowerOwn": lowered_own, "lower": lowered_all, "downOth": down_oth,
            "downOwn": down_own, "pairC": pair_c, "upOth": up_oth, "upOwn": up_own, "pairB": pair_b, "sinkOwn": sink_own,
            "sinkOth": sink_oth, "surface": surfaced, "values": valued, "voOth": vo_oth, "voOwn": vo_own,
            "qkOth": qk_oth, "qkOwn": qk_own, "voSum": vo_sum, "pairA": pair_a, "back": attended_back,
            "states": states_own, "collect": collected, "share": vector_shared, "stepC": step_c, "stepB": step_b,
            "pairS": states_pair, "pairO": output_pair, "stepA": step_a,
        }
        for name in ORDER:
            stages[name]()
        moment_down, square_down, way_down, kept_down, _ = w.step_c
        moment_up, square_up, way_up, kept_up, _ = w.step_b
        moment_in, moment_out, square_in, square_out, way_in, way_out, kept_in, kept_out, load = w.step_a
        total = Total(grid, tape, load)
        total.line()
        total.sides()

        def update(s, own, oth, vec, vec_first, vec_second, *refs):
            masters, ways, outs, grad = refs[:4], refs[4:8], refs[8:-1], refs[-1]
            norms = jnp.sqrt(own[half : half + 1, 0:LANES] + oth[half : half + 1, 0:LANES])
            outs[8][0:1] = norms[:, 0:6]
            outs[8][1:2] = norms[:, 6:12]
            for i, first in enumerate((0, 3, 4, 5)):
                for j in range(masters[i].shape[0]):
                    m = first + j
                    trust = RATE * (norms[:, m : m + 1] / norms[:, 6 + m : 7 + m])
                    value = masters[i][j] - trust * ways[i][j]
                    outs[i][j], outs[4 + i][j] = value, value.astype(BF16)
            for t in range(cores):

                @pl.when(s[3] == t)
                def _():
                    grad[t * half : (t + 1) * half] = own[0:half]
                    grad[(1 - t) * half : (2 - t) * half] = oth[0:half]

            outs[10][...], outs[11][...], direction = adam(grad[...], vec_first[...], vec_second[...])
            outs[9][...] = vec[...] - RATE * direction

        masters = [kept_in, kept_out, kept_up, kept_down]
        results = tape.run(
            update,
            [(m.shape, F32) for m in masters] + [(m.shape, BF16) for m in masters] + [((2, 6), F32)]
            + [(vectors.shape, F32)] * 3,
            total.pair + [vectors, vector_first, vector_second] + masters + [way_in, way_out, way_up, way_down],
            True, limit=6, spill=range(12), plain=(2, 3, 4), moved=2 * MIB,
            scratch=[VMEM(vectors.shape, F32)],
        )
        updated_vectors, moment_vectors, square_vectors = results[9:12]

        def native(values):
            values = list(values)
            return (values[0], values[1][0].T, values[2][0], values[3][0])

        return (
            w.layer_output, w.states_grad, *native(results[:4]),
            *native([moment_in, moment_out, moment_up, moment_down]),
            *native([square_in, square_out, square_up, square_down]),
            *native(results[4:8]), updated_vectors, moment_vectors, square_vectors, results[8].T,
        )

    return body


def solution(mesh):
    rows = P("dp", None, None)
    matrices = (P(None, "dp", "tensor"), P("tensor", "dp"), P("dp", "tensor"), P(("tensor", "dp"), None))
    in_specs = (rows, rows, P("dp"), P("dp")) + matrices * 3 + (P(), P(), P())
    out_specs = (rows, rows) + matrices * 4 + (P(), P(), P(), P())
    body = make_body(Grid(mesh))
    return jax.shard_map(body, mesh=mesh, in_specs=in_specs, out_specs=out_specs, check_vma=False)
```

```python
import itertools
import math
import types

import jax
import jax.numpy as jnp
import numpy as np
from jax import lax
from jax.experimental import pallas as pl
from jax.experimental.pallas import tpu as pltpu
from jax.sharding import PartitionSpec as P

HEAD_DIM = 64
STEP = 10
NORM_EPS = 1e-05
BETA_ONE = 0.9
BETA_TWO = 0.999
ADAM_EPS = 1e-06
RATE = 0.3
DECAY = 0.01
MASKED = -1e30
AXES = ("dp", "tensor")
F32, BF16 = jnp.float32, jnp.bfloat16
VMEM = pltpu.VMEM
LANES = 128
NT = (((1,), (1,)), ((), ()))
TN = (((0,), (0,)), ((), ()))
MIB = 1 << 20
PATHS = ("zzab", "azzb", "azzb", "azzb")
COUNTS = (1, 3, 1, 1, 2)
ORDER = (
    "castA", "castB", "prep", "a0", "b0", "a1", "castC", "c0", "b1", "wholeA", "c1", "b2", "otherA",
    "project", "attend", "c2", "wholeB", "otherB", "hide", "liftOwn", "liftOth", "turn", "wholeC", "lowerOwn",
    "otherC", "lower", "sinkOth", "downOth", "downOwn", "upOth", "pairC", "sinkOwn", "upOwn", "pairB",
    "surface", "values", "voOth", "C0", "back", "qkOwn", "qkOth", "voOwn", "voSum", "C1", "B0", "pairA",
    "states", "collect", "share", "C2", "B1", "A0", "pairO", "A1", "stepC", "B2", "A2", "stepB", "stepA",
    "pairS",
)


class Grid:
    def __init__(self, mesh):
        self.dp, self.cores = mesh.shape["dp"], mesh.shape["tensor"]
        chips = mesh.devices.reshape(self.dp, self.cores)[:, 0]
        spots = [tuple(getattr(chip, "coords", ())) for chip in chips]
        if any(len(spot) != 3 for spot in spots) or len(set(spots)) != self.dp:
            side = 1 << ((self.dp.bit_length() - 1) // 3)
            spots = [(i % side, i // side % side, i // (side * side)) for i in range(self.dp)]
        spots = np.array(spots) - np.min(spots, axis=0)
        sizes = spots.max(axis=0) + 1
        order = sorted(range(3), key=lambda k: -sizes[k])
        order = order[:1] + sorted(order[1:])
        self.spots = spots[:, order].tolist()
        self.long, self.side, _ = (int(sizes[k]) for k in order)
        self.at = {tuple(spot): i for i, spot in enumerate(self.spots)}
        unit = [tuple(int(j == k) for j in range(3)) for k in range(3)]
        self.stride = [self.at.get(u, 0) for u in unit]
        self.sizes = [int(sizes[k]) for k in order]

    def send(self, value, hop):
        pairs = []
        for i, spot in enumerate(self.spots):
            for core in range(self.cores):
                offsets, turn = hop(core)
                target = self.at[tuple(u ^ v for u, v in zip(spot, offsets))]
                pairs.append((i * self.cores + core, target * self.cores + (core ^ turn)))
        return lax.ppermute(value, AXES, pairs)

    def place(self):
        index = lax.axis_index("dp")
        spot = [lax.rem(lax.div(index, s), n) if n > 1 else index * 0 for s, n in zip(self.stride, self.sizes)]
        return jnp.stack(spot + [lax.axis_index("tensor")]).astype(jnp.int32)

    def path(self, order="zzab"):
        bits = [[1 << b for b in reversed(range((n - 1).bit_length()))] for n in (self.long, self.side, self.side)]
        steps = [[(side, k) for k in bits[side]] for side in range(3)]
        stock = {"z": [steps[0][:-1], steps[0][-1:]], "a": [steps[1]], "b": [steps[2]]}
        return sum((stock[kind].pop(0) for kind in order), [])

    def exchange(self, value, step):
        side, k = step
        offsets = [(k, 0, 0), (0, k, 0), (0, 0, k)]
        return self.send(value, lambda core: (offsets[side if core == 0 else (0, 2, 1)[side]], 0))

    def bit(self, s, step):
        side, k = step
        spot = s[0] if side == 0 else jnp.where(s[3] == 0, s[side], s[3 - side])
        return lax.rem(lax.div(spot, k), 2)

    def spot(self, s, steps, bits):
        place = 0
        for (side, k), bit in zip(steps, bits):
            stride = self.stride[0] if side == 0 else jnp.where(s[3] == 0, self.stride[side], self.stride[3 - side])
            place = place + bit * k * stride
        return place

    def long_steps(self):
        return [step for step in self.path() if step[0] == 0]

    def long_bits(self, s, k):
        spot = s[0] ^ k
        return tuple(lax.rem(lax.div(spot, distance), 2) for _, distance in reversed(self.long_steps()))

    def along(self, k):
        return lambda core: ((k, 0, 0), 0)

    def cross(self, j, k):
        return lambda core: ((0, j, k), 0)

    def core(self, value):
        return self.send(value, lambda core: ((0, 0, 0), 1))


class Tape:
    def __init__(self, place):
        self.place = place
        self.token = None

    def run(self, body, outs, ins, place=False, limit=4, flops=0, moved=0, exps=0, scratch=(), spill=(), plain=(), name=None):
        ins = [v if i in plain else pltpu.with_memory_space_constraint(v, VMEM) for i, v in enumerate(ins)]
        specs = [pl.BlockSpec(memory_space=VMEM)] * len(ins)
        first = []
        if place:
            first.append((self.place, pltpu.SMEM))
        if self.token is not None:
            first.append((pltpu.with_memory_space_constraint(self.token, VMEM), VMEM))
        chained = self.token is not None
        count, results = len(ins), len(outs)

        def chain(*refs):
            refs = list(refs)
            head = [refs.pop(0)] if place else []
            if chained:
                refs.pop(0)
            last = refs.pop(count + results)
            last[...] = jnp.zeros_like(last)
            body(*head, *refs)

        shapes = [
            jax.ShapeDtypeStruct(s, d) if i in spill else VMEM(s, d) for i, (s, d) in enumerate(outs)
        ] + [VMEM((8, LANES), F32)]
        *values, self.token = pl.pallas_call(
            chain,
            out_shape=shapes,
            in_specs=[pl.BlockSpec(memory_space=m) for _, m in first] + specs,
            out_specs=[pl.BlockSpec(memory_space=VMEM)] * len(shapes),
            scratch_shapes=list(scratch),
            name=name or body.__name__,
            cost_estimate=pl.CostEstimate(flops=flops, bytes_accessed=moved, transcendentals=0),
            compiler_params=pltpu.CompilerParams(vmem_limit_bytes=limit * MIB),
        )(*[v for v, _ in first], *ins)
        return values


def part(count, group, groups=3):
    return range(count * group // groups, count * (group + 1) // groups)


class Gather:
    def __init__(self, grid, tape, shard, direct=False, order="zzab"):
        self.grid, self.tape, self.block = grid, tape, shard
        self.path = grid.path(order)
        if direct:
            self.got = [grid.send(shard, grid.along(k)) for k in range(1, grid.long)]
        else:
            self.got = grid.exchange(shard, self.path[0])

    def merge_long(self):
        grid = self.grid
        steps = grid.long_steps()

        def gather_long(s, *refs):
            for k, ref in enumerate(refs[:-1]):
                refs[-1][grid.long_bits(s, k)] = ref[...]

        shape = (2,) * len(steps) + self.block.shape
        self.block = self.tape.run(gather_long, [(shape, BF16)], [self.block] + self.got, True)[0]
        self.got = grid.exchange(self.block, self.path[len(steps)])

    def merge(self, group):
        self.merges(part(len(self.path) - 1, group))

    def merge_short(self):
        self.merges(range(len(self.grid.long_steps()), len(self.path) - 1))

    def merges(self, steps):
        grid = self.grid
        for i in steps:
            step = self.path[i]

            def gather_merge(s, own, got, out):
                bit = grid.bit(s, step)
                out[bit] = own[...]
                out[1 - bit] = got[...]

            shape = (2,) + self.block.shape
            self.block = self.tape.run(gather_merge, [(shape, BF16)], [self.block, self.got], True)[0]
            self.got = grid.exchange(self.block, self.path[i + 1])

    def whole(self):
        full, self.came = self.put_together(self.block, self.got, False)
        return full

    def other(self):
        return self.put_together(self.grid.core(self.block), self.grid.core(self.came), True)[0]

    def put_together(self, block, came, other):
        grid, path = self.grid, self.path
        many, rows, width = block.shape[-3:]

        def gather_whole(s, own, got, out, *relay):
            for ref in relay:
                ref[...] = got[...]
            s = [s[0], s[1], s[2], 1 - s[3] if other else s[3]]
            last = grid.bit(s, path[-1])
            for bits in itertools.product(range(2), repeat=len(path) - 1):
                for ref, bit in ((own, last), (got, 1 - last)):
                    spot = grid.spot(s, path, bits[::-1] + (bit,))
                    for j in range(many):
                        out[j, spot] = ref[bits + (j,)]

        shapes = [((many, grid.dp, rows, width), BF16)] + [(came.shape, BF16)] * (not other)
        return self.tape.run(gather_whole, shapes, [block, came], True)


class Scatter:
    def __init__(self, grid, tape, other, order="zzab"):
        self.grid, self.tape = grid, tape
        self.path = grid.path(order)
        self.got = [grid.core(v) for v, _, _ in other]
        self.spots = [(j, c) for _, j, c in other]

    def pair(self, own, cut=1):
        grid, path = self.grid, self.path
        _, _, rows, width = own[0].shape
        own_spots = [(g, i) for g, v in enumerate(own) for i in range(v.shape[0])]
        many, pieces, got = len(own_spots), len(own), len(self.got)
        shapes = [v.shape for v in self.got]
        lead = (2,) * (len(path) - 1)
        shape = lead + (many, rows, width)
        each = many // cut
        sends = [(lead + (each, rows, width), BF16)] * cut

        def scatter_pair(s, *refs):
            own_refs, got_refs, outs = refs[:pieces], refs[pieces : pieces + got], refs[pieces + got :]
            last = grid.bit(s, path[-1])
            for bits in itertools.product(range(2), repeat=len(path) - 1):
                for sent, bit in ((False, last), (True, 1 - last)):
                    spot = grid.spot(s, path, bits[::-1] + (bit,))
                    for j, (g, i) in enumerate(own_spots):
                        out, m = (outs[1 + j // each], j % each) if sent else (outs[0], j)
                        found = False
                        for ref, (first, column), piece in zip(got_refs, self.spots, shapes):
                            if first <= j < first + piece[0]:
                                at = slice(column, column + piece[3])
                                total = own_refs[g][i, spot, :, at] + ref[j - first, spot].astype(F32)
                                out[bits + (m, slice(None), at)] = total.astype(out.dtype)
                                found = True
                        if not found:
                            out[bits + (m,)] = own_refs[g][i, spot].astype(out.dtype)

        self.keep, *values = self.tape.run(scatter_pair, [(shape, F32)] + sends, own + self.got, True)
        self.got = [grid.exchange(v, path[-1]) for v in values]

    def split(self, group):
        self.splits(part(len(self.path) - 1, group))

    def split_short(self):
        self.splits(range(len(self.path) - 1 - len(self.grid.long_steps())))

    def split_long(self):
        grid, count = self.grid, len(self.grid.long_steps())

        assert len(self.got) == 1

        def scatter_long(s, own, got, *outs):
            for k, out in enumerate(outs):
                at = grid.long_bits(s, k)
                out[...] = (own[at] + got[at].astype(F32)).astype(out.dtype)

        shape = self.keep.shape[count:]
        keep, *values = self.tape.run(
            scatter_long, [(shape, F32)] + [(shape, BF16)] * (grid.long - 1), [self.keep] + self.got, True
        )
        self.parts = [keep] + [grid.send(v, grid.along(k + 1)) for k, v in enumerate(values)]

    def splits(self, steps):
        grid = self.grid
        for i in steps:
            step = self.path[len(self.path) - 2 - i]

            count = len(self.got)
            each = self.keep.shape[-3] // count
            free = (slice(None),) * (len(self.keep.shape) - 4)

            def scatter_split(s, own, *refs):
                keep, send = refs[count:]
                bit = grid.bit(s, step)
                for g, got in enumerate(refs[:count]):
                    at = free + (slice(g * each, (g + 1) * each),)
                    keep[at] = own[(bit,) + at] + got[bit].astype(F32)
                    send[at] = (own[(1 - bit,) + at] + got[1 - bit].astype(F32)).astype(BF16)

            shape = self.keep.shape[1:]
            self.keep, value = self.tape.run(
                scatter_split, [(shape, F32), (shape, BF16)], [self.keep] + self.got, True
            )
            self.got = [grid.exchange(value, step)]
        self.parts = [self.keep] + self.got


def tree(values):
    values = list(values)
    while len(values) > 1:
        values = [a + b for a, b in zip(values[::2], values[1::2])]
    return values[0]


class Total:
    def __init__(self, grid, tape, value):
        self.grid, self.tape = grid, tape
        self.got = [value] + [grid.send(value, grid.along(k)) for k in range(1, grid.long)]

    def add(self):
        def body(*refs):
            refs[-1][...] = tree(ref[...] for ref in refs[:-1])

        return self.tape.run(body, [(self.got[0].shape, F32)], self.got)[0]

    def line(self):
        grid, value = self.grid, self.add()
        offsets = [(j, k) for j in range(grid.side) for k in range(grid.side)]
        self.got = [value] + [grid.send(value, grid.cross(j, k)) for j, k in offsets[1:]]

    def sides(self):
        value = self.add()
        self.pair = [value, self.grid.core(value)]


def normed_of(values):
    center = values - jnp.mean(values, axis=-1, keepdims=True)
    inverse = lax.rsqrt(jnp.mean(center * center, axis=-1, keepdims=True) + NORM_EPS)
    return center * inverse, inverse


def norm_back(upstream, normed, inverse, gain):
    scaled = upstream * gain
    inner = jnp.mean(scaled * normed, axis=-1, keepdims=True)
    return inverse * (scaled - jnp.mean(scaled, axis=-1, keepdims=True) - normed * inner)


def sum_rows(values):
    return jnp.sum(values, axis=0, keepdims=True)


def adam(grad, first, second):
    first_new = BETA_ONE * first + (1.0 - BETA_ONE) * grad
    second_new = BETA_TWO * second + (1.0 - BETA_TWO) * grad * grad
    corrected = first_new / (1.0 - BETA_ONE**STEP)
    spread = jnp.sqrt(second_new / (1.0 - BETA_TWO**STEP))
    return first_new, second_new, corrected / (spread + ADAM_EPS)


def squares(values):
    return jnp.sum(sum_rows(values * values), axis=1, keepdims=True)


def norm_row(entries):
    lane = lax.broadcasted_iota(jnp.int32, (1, LANES), 1)
    row = jnp.zeros((1, LANES), F32)
    for index, weight, direction in entries:
        row = jnp.where(lane == index, squares(weight), row)
        row = jnp.where(lane == index + 6, squares(direction), row)
    return row


def make_body(grid):
    def body(
        states, cotangent, word_counts, region_counts,
        attend_in, attend_out, expand_up, expand_down,
        first_in, first_out, first_up, first_down,
        second_in, second_out, second_up, second_down,
        vectors, vector_first, vector_second,
    ):
        w = types.SimpleNamespace()
        paths, counts_of = PATHS, COUNTS
        cores = grid.cores
        pairs, length, width = states.shape
        mine = pairs // cores
        rows = mine * length
        cols = attend_in.shape[2]
        units = expand_up.shape[1]
        twins = width // LANES
        scale = HEAD_DIM**-0.5
        rank = lax.axis_index("tensor")
        counts = lax.dynamic_slice_in_dim(word_counts + region_counts, rank * mine, mine, 0)
        tape = Tape(jnp.concatenate([grid.place(), counts]))
        attend_out, first_out, second_out = (v.T[None] for v in (attend_out, first_out, second_out))

        def cast(*refs):
            spot = 0
            for ref in refs[:-1]:
                refs[-1][spot : spot + ref.shape[0]] = ref[...].astype(BF16)
                spot += ref.shape[0]

        def casted(*mats):
            many = sum(m.shape[0] for m in mats)
            shape = (many,) + mats[0].shape[1:]
            return tape.run(cast, [(shape, BF16)], mats, plain=range(len(mats)))[0]

        def cast_a():
            w.gather_a = Gather(grid, tape, casted(attend_in, attend_out), direct=True)

        def cast_b():
            w.gather_b = Gather(grid, tape, casted(expand_up[None]), order=paths[0])

        def cast_c():
            w.gather_c = Gather(grid, tape, casted(expand_down[None]), order=paths[1])


        def prepare(s, states_ref, cot_ref, vec, x_ref, x_t, mine_cot, bias_in, bias_up):
            @pl.loop(0, mine)
            def _(p):
                at = pl.ds(pl.multiple_of(p * length, length), length)
                x_ref[at, :] = states_ref[s[3] * mine + p]
                mine_cot[at, :] = cot_ref[s[3] * mine + p]

            x_t[...] = x_ref[...].T
            bias_in[1:2] = jnp.zeros((1, width), F32)
            for t in range(cores):

                @pl.when(s[3] == t)
                def _():
                    for h in range(2):
                        at, source = slice(h * cols, (h + 1) * cols), slice((h ^ t) * cols, ((h ^ t) + 1) * cols)
                        bias_in[0:1, at] = vec[0:1, source]
                        bias_in[2:3, at] = vec[1:2, source]
                        for i in range(units // width):
                            row = 8 + (h ^ t) * (units // width) + i
                            spot = h * units + i * width
                            bias_up[:, spot : spot + width] = vec[row : row + 1]

        def prepared():
            w.x, w.x_t, w.cot, w.bias_in, w.bias_up = tape.run(
                prepare,
                [((rows, width), BF16), ((width, rows), BF16), ((rows, width), BF16), ((3, width), F32),
                 ((1, 2 * units), F32)],
                [states, cotangent, vectors], True, limit=12, moved=6 * MIB, plain=(0, 1),
            )

        def whole_a():
            w.a_own = w.gather_a.whole().reshape(4, width, cols)

        def other_a():
            w.a_oth = w.gather_a.other().reshape(4, width, cols)

        def whole_b():
            w.b_own = w.gather_b.whole().reshape(width, units)

        def other_b():
            w.b_oth = w.gather_b.other().reshape(width, units)

        def whole_c():
            w.c_own = w.gather_c.whole().reshape(units, width)

        def other_c():
            w.c_oth = w.gather_c.other().reshape(units, width)

        def project(x_ref, own, oth, bias, out):
            @pl.loop(0, 3)
            def _(j):
                for h, ref in enumerate((own, oth)):
                    at = slice(h * cols, (h + 1) * cols)
                    value = jnp.dot(x_ref[...], ref[j], preferred_element_type=F32)
                    out[j, :, at] = (value + bias[pl.ds(j, 1), at]).astype(BF16)

        def projected():
            w.qkv = tape.run(
                project, [((3, rows, width), BF16)], [w.x, w.a_own, w.a_oth, w.bias_in],
                limit=8, flops=6 * rows * width * width, moved=8 * MIB,
            )[0]

        def split(v):
            low = lax.broadcasted_iota(jnp.int32, v.shape, 1) < HEAD_DIM
            zero = jnp.zeros_like(v)
            return jnp.concatenate([jnp.where(low, v, zero), jnp.where(low, zero, v)], axis=0)

        def join(v):
            low = lax.broadcasted_iota(jnp.int32, (length, LANES), 1) < HEAD_DIM
            return jnp.where(low, v[:length], v[length:])

        def attend(count, qkv_ref, probs, context):
            @pl.loop(0, mine)
            def _(p):
                at = pl.ds(pl.multiple_of(p * length, length), length)
                known = lax.broadcasted_iota(jnp.int32, (length, length), 1) < count[4 + p]
                for u in range(twins):
                    lanes = slice(u * LANES, (u + 1) * LANES)
                    both = lax.dot_general(
                        qkv_ref[0, at, lanes], split(qkv_ref[1, at, lanes]), NT, preferred_element_type=F32
                    )
                    soft = []
                    for h in range(2):
                        score = jnp.where(known, both[:, h * length : (h + 1) * length] * scale, MASKED)
                        power = jnp.exp(score - jnp.max(score, axis=-1, keepdims=True))
                        soft.append(power / jnp.sum(power, axis=-1, keepdims=True))
                    prob = jnp.concatenate(soft, axis=1).astype(BF16)
                    probs[at, 2 * u * length : 2 * (u + 1) * length] = prob
                    context[at, lanes] = jnp.dot(
                        prob, split(qkv_ref[2, at, lanes]), preferred_element_type=F32
                    ).astype(BF16)

        def attended():
            w.probs, w.context = tape.run(
                attend, [((rows, 2 * twins * length), BF16), ((rows, width), BF16)], [w.qkv], True,
                limit=4, flops=4 * rows * length * width * 4, moved=5 * MIB, exps=rows * twins * 2 * length,
            )

        block = min(rows, 256)

        def hide(context_ref, x_ref, own, oth, vec, hidden, normed, inverse):
            for r in range(0, rows, block):
                at = slice(r, r + block)
                value = x_ref[at].astype(F32) + vec[2:3]
                for h, ref in enumerate((own, oth)):
                    value += lax.dot_general(
                        context_ref[at, h * cols : (h + 1) * cols], ref[3], NT, preferred_element_type=F32
                    )
                normal, spread = normed_of(value)
                normed[at], inverse[at] = normal, spread
                hidden[at] = (normal * vec[3:4] + vec[4:5]).astype(BF16)

        def hid():
            w.hidden, w.normed_one, w.inverse_one = tape.run(
                hide,
                [((rows, width), BF16), ((rows, width), F32), ((rows, 1), F32)],
                [w.context, w.x, w.a_own, w.a_oth, vectors],
                limit=8, flops=2 * rows * width * width, moved=6 * MIB,
            )

        tile = 256

        def lift(hidden_ref, up, bias, active, active_t, slope):
            @pl.loop(0, units // tile)
            def _(i):
                at = pl.ds(pl.multiple_of(i * tile, tile), tile)
                value = jnp.dot(hidden_ref[...], up[:, at], preferred_element_type=F32) + bias[:, at]
                half = 0.5 * (1.0 + lax.erf(value * math.sqrt(0.5)))
                result = (value * half).astype(BF16)
                active[:, at] = result
                active_t[at, :] = result.T
                bell = jnp.exp(-0.5 * value * value) * (1.0 / math.sqrt(2.0 * math.pi))
                slope[:, at] = (half + value * bell).astype(BF16)

        def lift_half(h, up):
            return tape.run(
                lambda hidden_ref, up_ref, bias, *outs: lift(hidden_ref, up_ref, bias.at[:, h * units : (h + 1) * units], *outs),
                [((rows, units), BF16), ((units, rows), BF16), ((rows, units), BF16)],
                [w.hidden, up, w.bias_up],
                limit=8, flops=2 * rows * width * units, moved=8 * MIB, exps=2 * rows * units,
            )

        def turn(value, out):
            out[...] = value[...].T

        def lift_own():
            w.lift_own = lift_half(0, w.b_own)

        def lift_oth():
            w.lift_oth = lift_half(1, w.b_oth)

        def turned():
            w.hidden_t = tape.run(turn, [((width, rows), BF16)], [w.hidden], limit=8)[0]

        def lower_half(active, down, out):
            @pl.loop(0, width // tile)
            def _(i):
                at = pl.ds(pl.multiple_of(i * tile, tile), tile)
                out[:, at] = jnp.dot(active[...], down[:, at], preferred_element_type=F32)

        def lowered_own():
            w.lowered = tape.run(
                lower_half, [((rows, width), F32)], [w.lift_own[0], w.c_own],
                limit=6, flops=2 * rows * width * units, moved=6 * MIB,
            )[0]

        def lower(count, lowered_ref, active, down, normed, cot_ref, vec, output, top, top16, sums, work):
            @pl.loop(0, width // tile)
            def _(i):
                at = pl.ds(pl.multiple_of(i * tile, tile), tile)
                work[:, at] = lowered_ref[:, at] + jnp.dot(active[...], down[:, at], preferred_element_type=F32)

            sums[...] = jnp.zeros_like(sums)

            for p in range(mine):
                at = slice(p * length, (p + 1) * length)
                value = normed[at] * vec[3:4] + vec[4:5] + work[at] + vec[5:6]
                normal, spread = normed_of(value)
                output[at] = (normal * vec[6:7] + vec[7:8]).astype(BF16)
                live = lax.broadcasted_iota(jnp.int32, (length, 1), 0) < count[4 + p]
                upstream = jnp.where(live, cot_ref[at].astype(F32), 0.0)
                grad = norm_back(upstream, normal, spread, vec[6:7])
                top[at] = grad
                top16[at] = grad.astype(BF16)
                sums[0:1] += sum_rows(grad)
                sums[1:2] += sum_rows(upstream * normal)
                sums[2:3] += sum_rows(upstream)

        def lowered_all():
            w.output, w.top, w.top16, w.sums_two = tape.run(
                lower,
                [((rows, width), BF16), ((rows, width), F32), ((rows, width), BF16), ((8, width), F32)],
                [w.lowered, w.lift_oth[0], w.c_oth, w.normed_one, w.cot, vectors],
                True, limit=8, flops=2 * rows * width * units, moved=14 * MIB,
                scratch=[VMEM((rows, width), F32)],
            )

        def product(left, right, *outs):
            step = min(left.shape[0], 256)

            @pl.loop(0, left.shape[0] // step)
            def _(i):
                at = pl.ds(pl.multiple_of(i * step, step), step)
                value = jnp.dot(left[at, :], right[...], preferred_element_type=F32)
                share = value.shape[1] // len(outs)
                for g, out in enumerate(outs):
                    out[at, :] = value[:, g * share : (g + 1) * share].astype(out.dtype)

        def weight_grad(left, right, kind, pieces=2):
            shape = (left.shape[0], right.shape[1])
            return tape.run(
                product, [((shape[0], shape[1] // pieces), kind)] * pieces, [left, right],
                limit=6, flops=2 * shape[0] * shape[1] * rows, moved=8 * MIB,
            )

        sharded = lambda values, many: [v.reshape(many, grid.dp, -1, v.shape[-1]) for v in values]
        numbered = lambda values: [(v, i, 0) for i, v in enumerate(values)]

        def down_oth():
            other = sharded(weight_grad(w.lift_oth[1], w.top16, BF16, counts_of[0]), 1)
            w.scatter_c = Scatter(grid, tape, numbered(other), order=paths[3])

        def down_own():
            w.down_own = weight_grad(w.lift_own[1], w.top16, F32, counts_of[0])

        def pair_c():
            w.scatter_c.pair(sharded(w.down_own, 1), counts_of[2])

        def up_oth():
            other = sharded(weight_grad(w.hidden_t, w.sink_oth[0], BF16, counts_of[1]), 1)
            w.scatter_b = Scatter(grid, tape, numbered(other), order=paths[2])

        def up_own():
            w.up_own = weight_grad(w.hidden_t, w.sink_own[0], F32, counts_of[1])

        def pair_b():
            w.scatter_b.pair(sharded(w.up_own, 1), counts_of[3])

        def sink(top16_ref, down, slope, grad, sums):
            @pl.loop(0, units // tile)
            def _(i):
                at = pl.ds(pl.multiple_of(i * tile, tile), tile)
                value = lax.dot_general(top16_ref[...], down[at, :], NT, preferred_element_type=F32)
                value = value * slope[:, at].astype(F32)
                grad[:, at] = value.astype(BF16)
                sums[:, at] = sum_rows(value)

        def sink_half(lifted, down):
            return tape.run(
                sink, [((rows, units), BF16), ((1, units), F32)], [w.top16, down, lifted[2]], limit=8
            )

        def sink_own():
            w.sink_own = sink_half(w.lift_own, w.c_own)

        def sink_oth():
            w.sink_oth = sink_half(w.lift_oth, w.c_oth)

        def surface(grad_own, grad_oth, own, oth, top_ref, normed, inverse, vec, a_own_ref, a_oth_ref,
                    mid, mid_t, back, sums, work, mid16):
            @pl.loop(0, width // tile)
            def _(i):
                at = pl.ds(pl.multiple_of(i * tile, tile), tile)
                work[:, at] = (
                    top_ref[:, at]
                    + lax.dot_general(grad_own[...], own[at, :], NT, preferred_element_type=F32)
                    + lax.dot_general(grad_oth[...], oth[at, :], NT, preferred_element_type=F32)
                )

            sums[...] = jnp.zeros_like(sums)

            @pl.loop(0, mine)
            def _(p):
                at = pl.ds(pl.multiple_of(p * length, length), length)
                upstream, normal = work[at], normed[at]
                grad = norm_back(upstream, normal, inverse[at], vec[3:4])
                mid[at] = grad
                mid16[at] = grad.astype(BF16)
                sums[0:1] += sum_rows(grad)
                sums[1:2] += sum_rows(upstream * normal)
                sums[2:3] += sum_rows(upstream)

            mid_t[...] = mid16[...].T
            for h, ref in enumerate((a_own_ref, a_oth_ref)):
                back[:, h * cols : (h + 1) * cols] = jnp.dot(
                    mid16[...], ref[3], preferred_element_type=F32
                ).astype(BF16)

        def surfaced():
            w.mid, w.mid_t, w.back, w.sums_one = tape.run(
                surface,
                [((rows, width), F32), ((width, rows), BF16), ((rows, width), BF16), ((8, width), F32)],
                [w.sink_own[0], w.sink_oth[0], w.b_own, w.b_oth, w.top, w.normed_one, w.inverse_one, vectors,
                 w.a_own, w.a_oth],
                limit=14, flops=4 * rows * width * units + 2 * rows * width * width, moved=14 * MIB,
                scratch=[VMEM((rows, width), F32), VMEM((rows, width), BF16)],
            )

        def pair_up(s, own, oth, out):
            out[s[3]] = own[...].astype(out.dtype)
            out[1 - s[3]] = oth[...].astype(out.dtype)

        def paired(own, oth, kind):
            shape = ((cores,) + own.shape, kind)
            result = tape.run(pair_up, [shape], [own, oth], True, limit=8, spill=(0,))[0]
            return result.reshape(pairs, length, width)

        def values_back(probs_ref, back_ref, grad, sums):
            sums[...] = jnp.zeros_like(sums)

            @pl.loop(0, mine)
            def _(p):
                at = pl.ds(pl.multiple_of(p * length, length), length)
                for u in range(twins):
                    lanes = slice(u * LANES, (u + 1) * LANES)
                    value = join(lax.dot_general(
                        probs_ref[at, 2 * u * length : 2 * (u + 1) * length], back_ref[at, lanes], TN,
                        preferred_element_type=F32,
                    ))
                    grad[at, lanes] = value.astype(BF16)
                    sums[:, lanes] += sum_rows(value)

        def valued():
            w.grad_v, w.sum_v = tape.run(
                values_back, [((rows, width), BF16), ((1, width), F32)], [w.probs, w.back],
                limit=4, flops=4 * rows * length * width, moved=3 * MIB,
            )

        def attend_grad(h, kind, lefts, rights, pieces=1):
            def attend_grad_half(*refs):
                at = slice(h * cols, (h + 1) * cols)
                share = cols // pieces
                for j, (left, right) in enumerate(zip(refs[:2], refs[2:4])):
                    value = jnp.dot(left[...], right[:, at], preferred_element_type=F32)
                    for g, out in enumerate(refs[4:]):
                        out[j] = value[:, g * share : (g + 1) * share].astype(kind)

            return tape.run(
                attend_grad_half, [((2, width, cols // pieces), kind)] * pieces, lefts + rights, limit=6
            )

        def vo_oth():
            w.vo_oth = grid.core(attend_grad(1, BF16, [w.x_t, w.mid_t], [w.grad_v, w.context])[0])

        def vo_own():
            w.vo_own = attend_grad(0, F32, [w.x_t, w.mid_t], [w.grad_v, w.context])

        def qk_oth():
            pieces = cols // LANES
            other = sharded(attend_grad(1, BF16, [w.x_t, w.x_t], [w.grad_q, w.grad_k], pieces), 2)
            w.scatter_a = Scatter(grid, tape, [(v, 0, LANES * i) for i, v in enumerate(other)])

        def qk_own():
            w.qk_own = attend_grad(0, F32, [w.x_t, w.x_t], [w.grad_q, w.grad_k])

        def vo_sum():
            w.vo_sum = tape.run(add_up, [((2, width, cols), F32)], [w.vo_own[0], w.vo_oth])

        def pair_a():
            w.scatter_a.pair(sharded(w.qk_own + w.vo_sum, 2), counts_of[4])

        def attend_back(probs_ref, back_ref, qkv_ref, grad_q, grad_k, sums):
            sums[...] = jnp.zeros_like(sums)

            @pl.loop(0, mine)
            def _(p):
                at = pl.ds(pl.multiple_of(p * length, length), length)
                for u in range(twins):
                    lanes = slice(u * LANES, (u + 1) * LANES)
                    prob = probs_ref[at, 2 * u * length : 2 * (u + 1) * length].astype(F32)
                    both = lax.dot_general(
                        back_ref[at, lanes], split(qkv_ref[2, at, lanes]), NT, preferred_element_type=F32
                    )
                    parts = []
                    for h in range(2):
                        half = slice(h * length, (h + 1) * length)
                        inner = jnp.sum(prob[:, half] * both[:, half], axis=-1, keepdims=True)
                        parts.append(prob[:, half] * (both[:, half] - inner))
                    grad = jnp.concatenate(parts, axis=1).astype(BF16)
                    value = jnp.dot(grad, split(qkv_ref[1, at, lanes]), preferred_element_type=F32) * scale
                    grad_q[at, lanes] = value.astype(BF16)
                    sums[:, lanes] += sum_rows(value)
                    value = join(lax.dot_general(grad, qkv_ref[0, at, lanes], TN, preferred_element_type=F32))
                    grad_k[at, lanes] = (value * scale).astype(BF16)

        def attended_back():
            w.grad_q, w.grad_k, w.sum_q = tape.run(
                attend_back, [((rows, width), BF16), ((rows, width), BF16), ((1, width), F32)], [w.probs, w.back, w.qkv],
                limit=4, flops=16 * rows * length * width, moved=6 * MIB,
            )
        def add_up(own, oth, out):
            out[...] = own[...] + oth[...].astype(F32)

        def states_back(grad_q_ref, grad_k_ref, grad_v_ref, own, oth, mid_ref, out):
            @pl.loop(0, width // tile)
            def _(i):
                at = pl.ds(pl.multiple_of(i * tile, tile), tile)
                value = mid_ref[:, at]
                for j, ref in enumerate((grad_q_ref, grad_k_ref, grad_v_ref)):
                    for h, weight in enumerate((own, oth)):
                        value += lax.dot_general(
                            ref[:, h * cols : (h + 1) * cols], weight[j, at, :], NT, preferred_element_type=F32
                        )
                out[:, at] = value.astype(BF16)

        def states_own():
            w.states_own = tape.run(
                states_back, [((rows, width), BF16)], [w.grad_q, w.grad_k, w.grad_v, w.a_own, w.a_oth, w.mid],
                limit=8, flops=6 * rows * width * width, moved=8 * MIB,
            )[0]

        def matrix_step(index):
            def step(*refs):
                grad = refs[0][...] + refs[1][...].astype(F32)
                grad = jnp.concatenate([grad[j] for j in range(grad.shape[0])], axis=-1)[None]
                master, first, second, moment, square, way, kept, tile_ref = refs[2:]
                moment[...], square[...], value = adam(grad, first[...], second[...])
                kept[...] = master[...]
                way[...] = value + DECAY * kept[...]
                tile_ref[...] = norm_row([(index, kept[0], way[0])])

            return step

        def stepped(step, parts, masters, shapes):
            outs = [(s, F32) for _ in range(4) for s in shapes] + [((1, LANES), F32)]
            n, m = len(parts), len(masters)
            return tape.run(
                step, outs, parts + masters, limit=6, spill=range(2 * len(shapes)), plain=range(n, n + m), moved=2 * MIB
            )

        ups = [v[None] for v in (expand_up, first_up, second_up)]
        downs = [v[None] for v in (expand_down, first_down, second_down)]

        def collect(s, sum_q_ref, sum_v_ref, one, two, up_own_ref, up_oth_ref, out):
            for t in range(cores):

                @pl.when(s[3] == t)
                def _():
                    for row, ref in enumerate((sum_q_ref, sum_v_ref)):
                        for h in range(2):
                            out[row : row + 1, (h ^ t) * cols : ((h ^ t) + 1) * cols] = ref[
                                :, h * cols : (h + 1) * cols
                            ]
                    for h, ref in enumerate((up_own_ref, up_oth_ref)):
                        for i in range(units // width):
                            row = 8 + (h ^ t) * (units // width) + i
                            out[row : row + 1] = ref[:, i * width : (i + 1) * width]

            out[2:5] = one[0:3]
            out[5:8] = two[0:3]

        half = vectors.shape[0] // cores

        def collected():
            w.vector_part = tape.run(
                    collect, [(vectors.shape, F32)],
                    [w.sum_q, w.sum_v, w.sums_one, w.sums_two, w.sink_own[1], w.sink_oth[1]], True,
            )[0]

        def vector_half(s, own, oth, out):
            for t in range(cores):

                @pl.when(s[3] == t)
                def _():
                    at = slice(t * half, (t + 1) * half)
                    out[...] = own[at] + oth[at]

        def vector_shared():
            parts = [w.vector_part, grid.core(w.vector_part)]
            w.vector_share = tape.run(vector_half, [((half, width), F32)], parts, True)[0]

        def step_c():
            w.step_c = stepped(matrix_step(5), w.scatter_c.parts, downs, [downs[0].shape])

        def step_b():
            w.step_b = stepped(matrix_step(4), w.scatter_b.parts, ups, [ups[0].shape])

        def states_pair():
            w.states_grad = paired(w.states_own, grid.core(w.states_own), F32)

        def output_pair():
            w.layer_output = paired(w.output, grid.core(w.output), BF16)

        def attend_step(*refs):
            n = len(w.scatter_a.parts)
            m_in, f_in, s_in, m_out, f_out, s_out, tile_up_ref, tile_down_ref, share = refs[n : n + 9]
            mo_in, mo_out, sq_in, sq_out, way_in, way_out, kept_in, kept_out, load = refs[n + 9 :]
            entries = []
            for j in range(4):
                grad = sum((ref[j].astype(F32) for ref in refs[1:n]), refs[0][j])
                i = j if j < 3 else 0
                m, f, s, mo, sq, kept, way = (
                    (m_in, f_in, s_in, mo_in, sq_in, kept_in, way_in)
                    if j < 3
                    else (m_out, f_out, s_out, mo_out, sq_out, kept_out, way_out)
                )
                mo[i], sq[i], value = adam(grad, f[i], s[i])
                kept[i] = m[i]
                way[i] = value + DECAY * kept[i]
                entries.append((j, kept[i], way[i]))
            load[...] = jnp.zeros_like(load)
            load[0:half] = share[...]
            load[half : half + 1, 0:LANES] = norm_row(entries) + tile_up_ref[...] + tile_down_ref[...]

        shapes = [attend_in.shape, attend_out.shape]
        masters = [attend_in, first_in, second_in, attend_out, first_out, second_out]
        def step_a():
            w.step_a = tape.run(
                attend_step, [(s, F32) for _ in range(4) for s in shapes] + [((8, width), F32)],
                w.scatter_a.parts + masters + [w.step_b[4], w.step_c[4], w.vector_share],
                limit=6, spill=range(4), plain=range(len(w.scatter_a.parts), len(w.scatter_a.parts) + 6),
            )

        stages = {
            "a0": lambda: w.gather_a.merge_long(), "a1": lambda: w.gather_a.merge_short(),
            "b0": lambda: w.gather_b.merge(0), "b1": lambda: w.gather_b.merge(1), "b2": lambda: w.gather_b.merge(2),
            "c0": lambda: w.gather_c.merge(0), "c1": lambda: w.gather_c.merge(1), "c2": lambda: w.gather_c.merge(2),
            "A0": lambda: w.scatter_a.split(0), "A1": lambda: w.scatter_a.split(1), "A2": lambda: w.scatter_a.split(2),
            "B0": lambda: w.scatter_b.split(0), "B1": lambda: w.scatter_b.split(1), "B2": lambda: w.scatter_b.split(2),
            "C0": lambda: w.scatter_c.split(0), "C1": lambda: w.scatter_c.split(1), "C2": lambda: w.scatter_c.split(2),
            "castA": cast_a, "castB": cast_b, "castC": cast_c, "prep": prepared, "wholeA": whole_a, "wholeB": whole_b,
            "wholeC": whole_c, "otherA": other_a, "otherB": other_b, "otherC": other_c, "project": projected, "attend": attended, "hide": hid, "liftOwn": lift_own,
            "liftOth": lift_oth, "turn": turned, "lowerOwn": lowered_own, "lower": lowered_all, "downOth": down_oth,
            "downOwn": down_own, "pairC": pair_c, "upOth": up_oth, "upOwn": up_own, "pairB": pair_b, "sinkOwn": sink_own,
            "sinkOth": sink_oth, "surface": surfaced, "values": valued, "voOth": vo_oth, "voOwn": vo_own,
            "qkOth": qk_oth, "qkOwn": qk_own, "voSum": vo_sum, "pairA": pair_a, "back": attended_back,
            "states": states_own, "collect": collected, "share": vector_shared, "stepC": step_c, "stepB": step_b,
            "pairS": states_pair, "pairO": output_pair, "stepA": step_a,
        }
        for name in ORDER:
            stages[name]()
        moment_down, square_down, way_down, kept_down, _ = w.step_c
        moment_up, square_up, way_up, kept_up, _ = w.step_b
        moment_in, moment_out, square_in, square_out, way_in, way_out, kept_in, kept_out, load = w.step_a
        total = Total(grid, tape, load)
        total.line()
        total.sides()

        def update(s, own, oth, vec, vec_first, vec_second, *refs):
            masters, ways, outs, grad = refs[:4], refs[4:8], refs[8:-1], refs[-1]
            norms = jnp.sqrt(own[half : half + 1, 0:LANES] + oth[half : half + 1, 0:LANES])
            outs[8][0:1] = norms[:, 0:6]
            outs[8][1:2] = norms[:, 6:12]
            for i, first in enumerate((0, 3, 4, 5)):
                for j in range(masters[i].shape[0]):
                    m = first + j
                    trust = RATE * (norms[:, m : m + 1] / norms[:, 6 + m : 7 + m])
                    value = masters[i][j] - trust * ways[i][j]
                    outs[i][j], outs[4 + i][j] = value, value.astype(BF16)
            for t in range(cores):

                @pl.when(s[3] == t)
                def _():
                    grad[t * half : (t + 1) * half] = own[0:half]
                    grad[(1 - t) * half : (2 - t) * half] = oth[0:half]

            outs[10][...], outs[11][...], direction = adam(grad[...], vec_first[...], vec_second[...])
            outs[9][...] = vec[...] - RATE * direction

        masters = [kept_in, kept_out, kept_up, kept_down]
        results = tape.run(
            update,
            [(m.shape, F32) for m in masters] + [(m.shape, BF16) for m in masters] + [((2, 6), F32)]
            + [(vectors.shape, F32)] * 3,
            total.pair + [vectors, vector_first, vector_second] + masters + [way_in, way_out, way_up, way_down],
            True, limit=6, spill=range(12), plain=(2, 3, 4), moved=2 * MIB,
            scratch=[VMEM(vectors.shape, F32)],
        )
        updated_vectors, moment_vectors, square_vectors = results[9:12]

        def native(values):
            values = list(values)
            return (values[0], values[1][0].T, values[2][0], values[3][0])

        return (
            w.layer_output, w.states_grad, *native(results[:4]),
            *native([moment_in, moment_out, moment_up, moment_down]),
            *native([square_in, square_out, square_up, square_down]),
            *native(results[4:8]), updated_vectors, moment_vectors, square_vectors, results[8].T,
        )

    return body


def solution(mesh):
    rows = P("dp", None, None)
    matrices = (P(None, "dp", "tensor"), P("tensor", "dp"), P("dp", "tensor"), P(("tensor", "dp"), None))
    in_specs = (rows, rows, P("dp"), P("dp")) + matrices * 3 + (P(), P(), P())
    out_specs = (rows, rows) + matrices * 4 + (P(), P(), P(), P())
    body = make_body(Grid(mesh))
    return jax.shard_map(body, mesh=mesh, in_specs=in_specs, out_specs=out_specs, check_vma=False)
```

```python
import itertools
import math
import types

import jax
import jax.numpy as jnp
import numpy as np
from jax import lax
from jax.experimental import pallas as pl
from jax.experimental.pallas import tpu as pltpu
from jax.sharding import PartitionSpec as P

HEAD_DIM = 64
STEP = 10
NORM_EPS = 1e-05
BETA_ONE = 0.9
BETA_TWO = 0.999
ADAM_EPS = 1e-06
RATE = 0.3
DECAY = 0.01
MASKED = -1e30
AXES = ("dp", "tensor")
F32, BF16 = jnp.float32, jnp.bfloat16
VMEM = pltpu.VMEM
LANES = 128
NT = (((1,), (1,)), ((), ()))
TN = (((0,), (0,)), ((), ()))
MIB = 1 << 20
PATHS = ("zzab", "azzb", "azzb", "azzb")
COUNTS = (1, 3, 1, 1, 2)
ORDER = (
    "castA", "castB", "prep", "a0", "b0", "a1", "castC", "c0", "b1", "wholeA", "c1", "b2", "otherA",
    "project", "attend", "c2", "wholeB", "otherB", "hide", "liftOwn", "liftOth", "turn", "wholeC", "lowerOwn",
    "otherC", "lower", "sinkOth", "downOth", "downOwn", "upOth", "pairC", "sinkOwn", "upOwn", "pairB",
    "surface", "values", "voOth", "C0", "back", "qkOwn", "qkOth", "voOwn", "voSum", "C1", "B0", "pairA",
    "states", "collect", "share", "C2", "B1", "A0", "pairO", "A1", "stepC", "B2", "A2", "stepB", "stepA",
    "pairS",
)


class Grid:
    def __init__(self, mesh):
        self.dp, self.cores = mesh.shape["dp"], mesh.shape["tensor"]
        chips = mesh.devices.reshape(self.dp, self.cores)[:, 0]
        spots = [tuple(getattr(chip, "coords", ())) for chip in chips]
        if any(len(spot) != 3 for spot in spots) or len(set(spots)) != self.dp:
            side = 1 << ((self.dp.bit_length() - 1) // 3)
            spots = [(i % side, i // side % side, i // (side * side)) for i in range(self.dp)]
        spots = np.array(spots) - np.min(spots, axis=0)
        sizes = spots.max(axis=0) + 1
        order = sorted(range(3), key=lambda k: -sizes[k])
        order = order[:1] + sorted(order[1:])
        self.spots = spots[:, order].tolist()
        self.long, self.side, _ = (int(sizes[k]) for k in order)
        self.at = {tuple(spot): i for i, spot in enumerate(self.spots)}
        unit = [tuple(int(j == k) for j in range(3)) for k in range(3)]
        self.stride = [self.at.get(u, 0) for u in unit]
        self.sizes = [int(sizes[k]) for k in order]

    def send(self, value, hop):
        pairs = []
        for i, spot in enumerate(self.spots):
            for core in range(self.cores):
                offsets, turn = hop(core)
                target = self.at[tuple(u ^ v for u, v in zip(spot, offsets))]
                pairs.append((i * self.cores + core, target * self.cores + (core ^ turn)))
        return lax.ppermute(value, AXES, pairs)

    def place(self):
        index = lax.axis_index("dp")
        spot = [lax.rem(lax.div(index, s), n) if n > 1 else index * 0 for s, n in zip(self.stride, self.sizes)]
        return jnp.stack(spot + [lax.axis_index("tensor")]).astype(jnp.int32)

    def path(self, order="zzab"):
        bits = [[1 << b for b in reversed(range((n - 1).bit_length()))] for n in (self.long, self.side, self.side)]
        steps = [[(side, k) for k in bits[side]] for side in range(3)]
        stock = {"z": [steps[0][:-1], steps[0][-1:]], "a": [steps[1]], "b": [steps[2]]}
        return sum((stock[kind].pop(0) for kind in order), [])

    def exchange(self, value, step):
        side, k = step
        offsets = [(k, 0, 0), (0, k, 0), (0, 0, k)]
        return self.send(value, lambda core: (offsets[side if core == 0 else (0, 2, 1)[side]], 0))

    def bit(self, s, step):
        side, k = step
        spot = s[0] if side == 0 else jnp.where(s[3] == 0, s[side], s[3 - side])
        return lax.rem(lax.div(spot, k), 2)

    def spot(self, s, steps, bits):
        place = 0
        for (side, k), bit in zip(steps, bits):
            stride = self.stride[0] if side == 0 else jnp.where(s[3] == 0, self.stride[side], self.stride[3 - side])
            place = place + bit * k * stride
        return place

    def long_steps(self):
        return [step for step in self.path() if step[0] == 0]

    def long_bits(self, s, k):
        spot = s[0] ^ k
        return tuple(lax.rem(lax.div(spot, distance), 2) for _, distance in reversed(self.long_steps()))

    def along(self, k):
        return lambda core: ((k, 0, 0), 0)

    def cross(self, j, k):
        return lambda core: ((0, j, k), 0)

    def core(self, value):
        return self.send(value, lambda core: ((0, 0, 0), 1))


class Tape:
    def __init__(self, place):
        self.place = place
        self.token = None

    def run(self, body, outs, ins, place=False, limit=4, flops=0, moved=0, exps=0, scratch=(), spill=(), plain=(), name=None):
        ins = [v if i in plain else pltpu.with_memory_space_constraint(v, VMEM) for i, v in enumerate(ins)]
        specs = [pl.BlockSpec(memory_space=VMEM)] * len(ins)
        first = []
        if place:
            first.append((self.place, pltpu.SMEM))
        if self.token is not None:
            first.append((pltpu.with_memory_space_constraint(self.token, VMEM), VMEM))
        chained = self.token is not None
        count, results = len(ins), len(outs)

        def chain(*refs):
            refs = list(refs)
            head = [refs.pop(0)] if place else []
            if chained:
                refs.pop(0)
            last = refs.pop(count + results)
            last[...] = jnp.zeros_like(last)
            body(*head, *refs)

        shapes = [
            jax.ShapeDtypeStruct(s, d) if i in spill else VMEM(s, d) for i, (s, d) in enumerate(outs)
        ] + [VMEM((8, LANES), F32)]
        *values, self.token = pl.pallas_call(
            chain,
            out_shape=shapes,
            in_specs=[pl.BlockSpec(memory_space=m) for _, m in first] + specs,
            out_specs=[pl.BlockSpec(memory_space=VMEM)] * len(shapes),
            scratch_shapes=list(scratch),
            name=name or body.__name__,
            cost_estimate=pl.CostEstimate(flops=flops, bytes_accessed=moved, transcendentals=0),
            compiler_params=pltpu.CompilerParams(vmem_limit_bytes=limit * MIB),
        )(*[v for v, _ in first], *ins)
        return values


def part(count, group, groups=3):
    return range(count * group // groups, count * (group + 1) // groups)


class Gather:
    def __init__(self, grid, tape, shard, direct=False, order="zzab"):
        self.grid, self.tape, self.block = grid, tape, shard
        self.path = grid.path(order)
        if direct:
            self.got = [grid.send(shard, grid.along(k)) for k in range(1, grid.long)]
        else:
            self.got = grid.exchange(shard, self.path[0])

    def merge_long(self):
        grid = self.grid
        steps = grid.long_steps()

        def gather_long(s, *refs):
            for k, ref in enumerate(refs[:-1]):
                refs[-1][grid.long_bits(s, k)] = ref[...]

        shape = (2,) * len(steps) + self.block.shape
        self.block = self.tape.run(gather_long, [(shape, BF16)], [self.block] + self.got, True)[0]
        self.got = grid.exchange(self.block, self.path[len(steps)])

    def merge(self, group):
        self.merges(part(len(self.path) - 1, group))

    def merge_short(self):
        self.merges(range(len(self.grid.long_steps()), len(self.path) - 1))

    def merges(self, steps):
        grid = self.grid
        for i in steps:
            step = self.path[i]

            def gather_merge(s, own, got, out):
                bit = grid.bit(s, step)
                out[bit] = own[...]
                out[1 - bit] = got[...]

            shape = (2,) + self.block.shape
            self.block = self.tape.run(gather_merge, [(shape, BF16)], [self.block, self.got], True)[0]
            self.got = grid.exchange(self.block, self.path[i + 1])

    def whole(self):
        full, self.came = self.put_together(self.block, self.got, False)
        return full

    def other(self):
        return self.put_together(self.grid.core(self.block), self.grid.core(self.came), True)[0]

    def put_together(self, block, came, other):
        grid, path = self.grid, self.path
        many, rows, width = block.shape[-3:]

        def gather_whole(s, own, got, out, *relay):
            for ref in relay:
                ref[...] = got[...]
            s = [s[0], s[1], s[2], 1 - s[3] if other else s[3]]
            last = grid.bit(s, path[-1])
            for bits in itertools.product(range(2), repeat=len(path) - 1):
                for ref, bit in ((own, last), (got, 1 - last)):
                    spot = grid.spot(s, path, bits[::-1] + (bit,))
                    for j in range(many):
                        out[j, spot] = ref[bits + (j,)]

        shapes = [((many, grid.dp, rows, width), BF16)] + [(came.shape, BF16)] * (not other)
        return self.tape.run(gather_whole, shapes, [block, came], True)


class Scatter:
    def __init__(self, grid, tape, other, order="zzab"):
        self.grid, self.tape = grid, tape
        self.path = grid.path(order)
        self.got = [grid.core(v) for v, _, _ in other]
        self.spots = [(j, c) for _, j, c in other]

    def pair(self, own, cut=1):
        grid, path = self.grid, self.path
        _, _, rows, width = own[0].shape
        own_spots = [(g, i) for g, v in enumerate(own) for i in range(v.shape[0])]
        many, pieces, got = len(own_spots), len(own), len(self.got)
        shapes = [v.shape for v in self.got]
        lead = (2,) * (len(path) - 1)
        shape = lead + (many, rows, width)
        each = many // cut
        sends = [(lead + (each, rows, width), BF16)] * cut

        def scatter_pair(s, *refs):
            own_refs, got_refs, outs = refs[:pieces], refs[pieces : pieces + got], refs[pieces + got :]
            last = grid.bit(s, path[-1])
            for bits in itertools.product(range(2), repeat=len(path) - 1):
                for sent, bit in ((False, last), (True, 1 - last)):
                    spot = grid.spot(s, path, bits[::-1] + (bit,))
                    for j, (g, i) in enumerate(own_spots):
                        out, m = (outs[1 + j // each], j % each) if sent else (outs[0], j)
                        found = False
                        for ref, (first, column), piece in zip(got_refs, self.spots, shapes):
                            if first <= j < first + piece[0]:
                                at = slice(column, column + piece[3])
                                total = own_refs[g][i, spot, :, at] + ref[j - first, spot].astype(F32)
                                out[bits + (m, slice(None), at)] = total.astype(out.dtype)
                                found = True
                        if not found:
                            out[bits + (m,)] = own_refs[g][i, spot].astype(out.dtype)

        self.keep, *values = self.tape.run(scatter_pair, [(shape, F32)] + sends, own + self.got, True)
        self.got = [grid.exchange(v, path[-1]) for v in values]

    def split(self, group):
        self.splits(part(len(self.path) - 1, group))

    def split_short(self):
        self.splits(range(len(self.path) - 1 - len(self.grid.long_steps())))

    def split_long(self):
        grid, count = self.grid, len(self.grid.long_steps())

        assert len(self.got) == 1

        def scatter_long(s, own, got, *outs):
            for k, out in enumerate(outs):
                at = grid.long_bits(s, k)
                out[...] = (own[at] + got[at].astype(F32)).astype(out.dtype)

        shape = self.keep.shape[count:]
        keep, *values = self.tape.run(
            scatter_long, [(shape, F32)] + [(shape, BF16)] * (grid.long - 1), [self.keep] + self.got, True
        )
        self.parts = [keep] + [grid.send(v, grid.along(k + 1)) for k, v in enumerate(values)]

    def splits(self, steps):
        grid = self.grid
        for i in steps:
            step = self.path[len(self.path) - 2 - i]

            count = len(self.got)
            each = self.keep.shape[-3] // count
            free = (slice(None),) * (len(self.keep.shape) - 4)

            def scatter_split(s, own, *refs):
                keep, send = refs[count:]
                bit = grid.bit(s, step)
                for g, got in enumerate(refs[:count]):
                    at = free + (slice(g * each, (g + 1) * each),)
                    keep[at] = own[(bit,) + at] + got[bit].astype(F32)
                    send[at] = (own[(1 - bit,) + at] + got[1 - bit].astype(F32)).astype(BF16)

            shape = self.keep.shape[1:]
            self.keep, value = self.tape.run(
                scatter_split, [(shape, F32), (shape, BF16)], [self.keep] + self.got, True
            )
            self.got = [grid.exchange(value, step)]
        self.parts = [self.keep] + self.got


def tree(values):
    values = list(values)
    while len(values) > 1:
        values = [a + b for a, b in zip(values[::2], values[1::2])]
    return values[0]


class Total:
    def __init__(self, grid, tape, value):
        self.grid, self.tape = grid, tape
        self.got = [value] + [grid.send(value, grid.along(k)) for k in range(1, grid.long)]

    def add(self):
        def body(*refs):
            refs[-1][...] = tree(ref[...] for ref in refs[:-1])

        return self.tape.run(body, [(self.got[0].shape, F32)], self.got)[0]

    def line(self):
        grid, value = self.grid, self.add()
        offsets = [(j, k) for j in range(grid.side) for k in range(grid.side)]
        self.got = [value] + [grid.send(value, grid.cross(j, k)) for j, k in offsets[1:]]

    def sides(self):
        value = self.add()
        self.pair = [value, self.grid.core(value)]


def normed_of(values):
    center = values - jnp.mean(values, axis=-1, keepdims=True)
    inverse = lax.rsqrt(jnp.mean(center * center, axis=-1, keepdims=True) + NORM_EPS)
    return center * inverse, inverse


def norm_back(upstream, normed, inverse, gain):
    scaled = upstream * gain
    inner = jnp.mean(scaled * normed, axis=-1, keepdims=True)
    return inverse * (scaled - jnp.mean(scaled, axis=-1, keepdims=True) - normed * inner)


def sum_rows(values):
    return jnp.sum(values, axis=0, keepdims=True)


def adam(grad, first, second):
    first_new = BETA_ONE * first + (1.0 - BETA_ONE) * grad
    second_new = BETA_TWO * second + (1.0 - BETA_TWO) * grad * grad
    corrected = first_new / (1.0 - BETA_ONE**STEP)
    spread = jnp.sqrt(second_new / (1.0 - BETA_TWO**STEP))
    return first_new, second_new, corrected / (spread + ADAM_EPS)


def squares(values):
    return jnp.sum(sum_rows(values * values), axis=1, keepdims=True)


def norm_row(entries):
    lane = lax.broadcasted_iota(jnp.int32, (1, LANES), 1)
    row = jnp.zeros((1, LANES), F32)
    for index, weight, direction in entries:
        row = jnp.where(lane == index, squares(weight), row)
        row = jnp.where(lane == index + 6, squares(direction), row)
    return row


def make_body(grid):
    def body(
        states, cotangent, word_counts, region_counts,
        attend_in, attend_out, expand_up, expand_down,
        first_in, first_out, first_up, first_down,
        second_in, second_out, second_up, second_down,
        vectors, vector_first, vector_second,
    ):
        w = types.SimpleNamespace()
        paths, counts_of = PATHS, COUNTS
        cores = grid.cores
        pairs, length, width = states.shape
        mine = pairs // cores
        rows = mine * length
        cols = attend_in.shape[2]
        units = expand_up.shape[1]
        twins = width // LANES
        scale = HEAD_DIM**-0.5
        rank = lax.axis_index("tensor")
        counts = lax.dynamic_slice_in_dim(word_counts + region_counts, rank * mine, mine, 0)
        tape = Tape(jnp.concatenate([grid.place(), counts]))
        attend_out, first_out, second_out = (v.T[None] for v in (attend_out, first_out, second_out))

        def cast(*refs):
            spot = 0
            for ref in refs[:-1]:
                refs[-1][spot : spot + ref.shape[0]] = ref[...].astype(BF16)
                spot += ref.shape[0]

        def casted(*mats):
            many = sum(m.shape[0] for m in mats)
            shape = (many,) + mats[0].shape[1:]
            return tape.run(cast, [(shape, BF16)], mats, plain=range(len(mats)))[0]

        def cast_a():
            w.gather_a = Gather(grid, tape, casted(attend_in, attend_out), direct=True)

        def cast_b():
            w.gather_b = Gather(grid, tape, casted(expand_up[None]), order=paths[0])

        def cast_c():
            w.gather_c = Gather(grid, tape, casted(expand_down[None]), order=paths[1])


        def prepare(s, states_ref, cot_ref, vec, x_ref, x_t, mine_cot, bias_in, bias_up):
            @pl.loop(0, mine)
            def _(p):
                at = pl.ds(pl.multiple_of(p * length, length), length)
                x_ref[at, :] = states_ref[s[3] * mine + p]
                mine_cot[at, :] = cot_ref[s[3] * mine + p]

            x_t[...] = x_ref[...].T
            bias_in[1:2] = jnp.zeros((1, width), F32)
            for t in range(cores):

                @pl.when(s[3] == t)
                def _():
                    for h in range(2):
                        at, source = slice(h * cols, (h + 1) * cols), slice((h ^ t) * cols, ((h ^ t) + 1) * cols)
                        bias_in[0:1, at] = vec[0:1, source]
                        bias_in[2:3, at] = vec[1:2, source]
                        for i in range(units // width):
                            row = 8 + (h ^ t) * (units // width) + i
                            spot = h * units + i * width
                            bias_up[:, spot : spot + width] = vec[row : row + 1]

        def prepared():
            w.x, w.x_t, w.cot, w.bias_in, w.bias_up = tape.run(
                prepare,
                [((rows, width), BF16), ((width, rows), BF16), ((rows, width), BF16), ((3, width), F32),
                 ((1, 2 * units), F32)],
                [states, cotangent, vectors], True, limit=12, moved=6 * MIB, plain=(0, 1),
            )

        def whole_a():
            w.a_own = w.gather_a.whole().reshape(4, width, cols)

        def other_a():
            w.a_oth = w.gather_a.other().reshape(4, width, cols)

        def whole_b():
            w.b_own = w.gather_b.whole().reshape(width, units)

        def other_b():
            w.b_oth = w.gather_b.other().reshape(width, units)

        def whole_c():
            w.c_own = w.gather_c.whole().reshape(units, width)

        def other_c():
            w.c_oth = w.gather_c.other().reshape(units, width)

        def project(x_ref, own, oth, bias, out):
            @pl.loop(0, 3)
            def _(j):
                for h, ref in enumerate((own, oth)):
                    at = slice(h * cols, (h + 1) * cols)
                    value = jnp.dot(x_ref[...], ref[j], preferred_element_type=F32)
                    out[j, :, at] = (value + bias[pl.ds(j, 1), at]).astype(BF16)

        def projected():
            w.qkv = tape.run(
                project, [((3, rows, width), BF16)], [w.x, w.a_own, w.a_oth, w.bias_in],
                limit=8, flops=6 * rows * width * width, moved=8 * MIB,
            )[0]

        def split(v):
            low = lax.broadcasted_iota(jnp.int32, v.shape, 1) < HEAD_DIM
            zero = jnp.zeros_like(v)
            return jnp.concatenate([jnp.where(low, v, zero), jnp.where(low, zero, v)], axis=0)

        def join(v):
            low = lax.broadcasted_iota(jnp.int32, (length, LANES), 1) < HEAD_DIM
            return jnp.where(low, v[:length], v[length:])

        def attend(count, qkv_ref, probs, context):
            for p in range(mine):
                at = slice(p * length, (p + 1) * length)
                known = lax.broadcasted_iota(jnp.int32, (length, length), 1) < count[4 + p]
                for u in range(twins):
                    lanes = slice(u * LANES, (u + 1) * LANES)
                    both = lax.dot_general(
                        qkv_ref[0, at, lanes], split(qkv_ref[1, at, lanes]), NT, preferred_element_type=F32
                    )
                    soft = []
                    for h in range(2):
                        score = jnp.where(known, both[:, h * length : (h + 1) * length] * scale, MASKED)
                        power = jnp.exp(score - jnp.max(score, axis=-1, keepdims=True))
                        soft.append(power / jnp.sum(power, axis=-1, keepdims=True))
                    prob = jnp.concatenate(soft, axis=1).astype(BF16)
                    probs[at, 2 * u * length : 2 * (u + 1) * length] = prob
                    context[at, lanes] = jnp.dot(
                        prob, split(qkv_ref[2, at, lanes]), preferred_element_type=F32
                    ).astype(BF16)

        def attended():
            w.probs, w.context = tape.run(
                attend, [((rows, 2 * twins * length), BF16), ((rows, width), BF16)], [w.qkv], True,
                limit=4, flops=4 * rows * length * width * 4, moved=5 * MIB, exps=rows * twins * 2 * length,
            )

        block = min(rows, 256)

        def hide(context_ref, x_ref, own, oth, vec, hidden, normed, inverse):
            for r in range(0, rows, block):
                at = slice(r, r + block)
                value = x_ref[at].astype(F32) + vec[2:3]
                for h, ref in enumerate((own, oth)):
                    value += lax.dot_general(
                        context_ref[at, h * cols : (h + 1) * cols], ref[3], NT, preferred_element_type=F32
                    )
                normal, spread = normed_of(value)
                normed[at], inverse[at] = normal, spread
                hidden[at] = (normal * vec[3:4] + vec[4:5]).astype(BF16)

        def hid():
            w.hidden, w.normed_one, w.inverse_one = tape.run(
                hide,
                [((rows, width), BF16), ((rows, width), F32), ((rows, 1), F32)],
                [w.context, w.x, w.a_own, w.a_oth, vectors],
                limit=8, flops=2 * rows * width * width, moved=6 * MIB,
            )

        tile = 256

        def lift(hidden_ref, up, bias, active, active_t, slope):
            @pl.loop(0, units // tile)
            def _(i):
                at = pl.ds(pl.multiple_of(i * tile, tile), tile)
                value = jnp.dot(hidden_ref[...], up[:, at], preferred_element_type=F32) + bias[:, at]
                half = 0.5 * (1.0 + lax.erf(value * math.sqrt(0.5)))
                result = (value * half).astype(BF16)
                active[:, at] = result
                active_t[at, :] = result.T
                bell = jnp.exp(-0.5 * value * value) * (1.0 / math.sqrt(2.0 * math.pi))
                slope[:, at] = (half + value * bell).astype(BF16)

        def lift_half(h, up):
            return tape.run(
                lambda hidden_ref, up_ref, bias, *outs: lift(hidden_ref, up_ref, bias.at[:, h * units : (h + 1) * units], *outs),
                [((rows, units), BF16), ((units, rows), BF16), ((rows, units), BF16)],
                [w.hidden, up, w.bias_up],
                limit=8, flops=2 * rows * width * units, moved=8 * MIB, exps=2 * rows * units,
            )

        def turn(value, out):
            out[...] = value[...].T

        def lift_own():
            w.lift_own = lift_half(0, w.b_own)

        def lift_oth():
            w.lift_oth = lift_half(1, w.b_oth)

        def turned():
            w.hidden_t = tape.run(turn, [((width, rows), BF16)], [w.hidden], limit=8)[0]

        def lower_half(active, down, out):
            @pl.loop(0, width // tile)
            def _(i):
                at = pl.ds(pl.multiple_of(i * tile, tile), tile)
                out[:, at] = jnp.dot(active[...], down[:, at], preferred_element_type=F32)

        def lowered_own():
            w.lowered = tape.run(
                lower_half, [((rows, width), F32)], [w.lift_own[0], w.c_own],
                limit=6, flops=2 * rows * width * units, moved=6 * MIB,
            )[0]

        def lower(count, lowered_ref, active, down, normed, cot_ref, vec, output, top, top16, sums, work):
            @pl.loop(0, width // tile)
            def _(i):
                at = pl.ds(pl.multiple_of(i * tile, tile), tile)
                work[:, at] = lowered_ref[:, at] + jnp.dot(active[...], down[:, at], preferred_element_type=F32)

            sums[...] = jnp.zeros_like(sums)

            for p in range(mine):
                at = slice(p * length, (p + 1) * length)
                value = normed[at] * vec[3:4] + vec[4:5] + work[at] + vec[5:6]
                normal, spread = normed_of(value)
                output[at] = (normal * vec[6:7] + vec[7:8]).astype(BF16)
                live = lax.broadcasted_iota(jnp.int32, (length, 1), 0) < count[4 + p]
                upstream = jnp.where(live, cot_ref[at].astype(F32), 0.0)
                grad = norm_back(upstream, normal, spread, vec[6:7])
                top[at] = grad
                top16[at] = grad.astype(BF16)
                sums[0:1] += sum_rows(grad)
                sums[1:2] += sum_rows(upstream * normal)
                sums[2:3] += sum_rows(upstream)

        def lowered_all():
            w.output, w.top, w.top16, w.sums_two = tape.run(
                lower,
                [((rows, width), BF16), ((rows, width), F32), ((rows, width), BF16), ((8, width), F32)],
                [w.lowered, w.lift_oth[0], w.c_oth, w.normed_one, w.cot, vectors],
                True, limit=8, flops=2 * rows * width * units, moved=14 * MIB,
                scratch=[VMEM((rows, width), F32)],
            )

        def product(left, right, *outs):
            step = min(left.shape[0], 256)

            @pl.loop(0, left.shape[0] // step)
            def _(i):
                at = pl.ds(pl.multiple_of(i * step, step), step)
                value = jnp.dot(left[at, :], right[...], preferred_element_type=F32)
                share = value.shape[1] // len(outs)
                for g, out in enumerate(outs):
                    out[at, :] = value[:, g * share : (g + 1) * share].astype(out.dtype)

        def weight_grad(left, right, kind, pieces=2):
            shape = (left.shape[0], right.shape[1])
            return tape.run(
                product, [((shape[0], shape[1] // pieces), kind)] * pieces, [left, right],
                limit=6, flops=2 * shape[0] * shape[1] * rows, moved=8 * MIB,
            )

        sharded = lambda values, many: [v.reshape(many, grid.dp, -1, v.shape[-1]) for v in values]
        numbered = lambda values: [(v, i, 0) for i, v in enumerate(values)]

        def down_oth():
            other = sharded(weight_grad(w.lift_oth[1], w.top16, BF16, counts_of[0]), 1)
            w.scatter_c = Scatter(grid, tape, numbered(other), order=paths[3])

        def down_own():
            w.down_own = weight_grad(w.lift_own[1], w.top16, F32, counts_of[0])

        def pair_c():
            w.scatter_c.pair(sharded(w.down_own, 1), counts_of[2])

        def up_oth():
            other = sharded(weight_grad(w.hidden_t, w.sink_oth[0], BF16, counts_of[1]), 1)
            w.scatter_b = Scatter(grid, tape, numbered(other), order=paths[2])

        def up_own():
            w.up_own = weight_grad(w.hidden_t, w.sink_own[0], F32, counts_of[1])

        def pair_b():
            w.scatter_b.pair(sharded(w.up_own, 1), counts_of[3])

        def sink(top16_ref, down, slope, grad, sums):
            @pl.loop(0, units // tile)
            def _(i):
                at = pl.ds(pl.multiple_of(i * tile, tile), tile)
                value = lax.dot_general(top16_ref[...], down[at, :], NT, preferred_element_type=F32)
                value = value * slope[:, at].astype(F32)
                grad[:, at] = value.astype(BF16)
                sums[:, at] = sum_rows(value)

        def sink_half(lifted, down):
            return tape.run(
                sink, [((rows, units), BF16), ((1, units), F32)], [w.top16, down, lifted[2]], limit=8
            )

        def sink_own():
            w.sink_own = sink_half(w.lift_own, w.c_own)

        def sink_oth():
            w.sink_oth = sink_half(w.lift_oth, w.c_oth)

        def surface(grad_own, grad_oth, own, oth, top_ref, normed, inverse, vec, a_own_ref, a_oth_ref,
                    mid, mid_t, back, sums, work, mid16):
            @pl.loop(0, width // tile)
            def _(i):
                at = pl.ds(pl.multiple_of(i * tile, tile), tile)
                work[:, at] = (
                    top_ref[:, at]
                    + lax.dot_general(grad_own[...], own[at, :], NT, preferred_element_type=F32)
                    + lax.dot_general(grad_oth[...], oth[at, :], NT, preferred_element_type=F32)
                )

            sums[...] = jnp.zeros_like(sums)

            for p in range(mine):
                at = slice(p * length, (p + 1) * length)
                upstream, normal = work[at], normed[at]
                grad = norm_back(upstream, normal, inverse[at], vec[3:4])
                mid[at] = grad
                mid16[at] = grad.astype(BF16)
                sums[0:1] += sum_rows(grad)
                sums[1:2] += sum_rows(upstream * normal)
                sums[2:3] += sum_rows(upstream)

            mid_t[...] = mid16[...].T
            for h, ref in enumerate((a_own_ref, a_oth_ref)):
                back[:, h * cols : (h + 1) * cols] = jnp.dot(
                    mid16[...], ref[3], preferred_element_type=F32
                ).astype(BF16)

        def surfaced():
            w.mid, w.mid_t, w.back, w.sums_one = tape.run(
                surface,
                [((rows, width), F32), ((width, rows), BF16), ((rows, width), BF16), ((8, width), F32)],
                [w.sink_own[0], w.sink_oth[0], w.b_own, w.b_oth, w.top, w.normed_one, w.inverse_one, vectors,
                 w.a_own, w.a_oth],
                limit=14, flops=4 * rows * width * units + 2 * rows * width * width, moved=14 * MIB,
                scratch=[VMEM((rows, width), F32), VMEM((rows, width), BF16)],
            )

        def pair_up(s, own, oth, out):
            out[s[3]] = own[...].astype(out.dtype)
            out[1 - s[3]] = oth[...].astype(out.dtype)

        def paired(own, oth, kind):
            shape = ((cores,) + own.shape, kind)
            result = tape.run(pair_up, [shape], [own, oth], True, limit=8, spill=(0,))[0]
            return result.reshape(pairs, length, width)

        def values_back(probs_ref, back_ref, grad, sums):
            sums[...] = jnp.zeros_like(sums)

            for p in range(mine):
                at = slice(p * length, (p + 1) * length)
                for u in range(twins):
                    lanes = slice(u * LANES, (u + 1) * LANES)
                    value = join(lax.dot_general(
                        probs_ref[at, 2 * u * length : 2 * (u + 1) * length], back_ref[at, lanes], TN,
                        preferred_element_type=F32,
                    ))
                    grad[at, lanes] = value.astype(BF16)
                    sums[:, lanes] += sum_rows(value)

        def valued():
            w.grad_v, w.sum_v = tape.run(
                values_back, [((rows, width), BF16), ((1, width), F32)], [w.probs, w.back],
                limit=4, flops=4 * rows * length * width, moved=3 * MIB,
            )

        def attend_grad(h, kind, lefts, rights, pieces=1):
            def attend_grad_half(*refs):
                at = slice(h * cols, (h + 1) * cols)
                share = cols // pieces
                for j, (left, right) in enumerate(zip(refs[:2], refs[2:4])):
                    value = jnp.dot(left[...], right[:, at], preferred_element_type=F32)
                    for g, out in enumerate(refs[4:]):
                        out[j] = value[:, g * share : (g + 1) * share].astype(kind)

            return tape.run(
                attend_grad_half, [((2, width, cols // pieces), kind)] * pieces, lefts + rights, limit=6
            )

        def vo_oth():
            w.vo_oth = grid.core(attend_grad(1, BF16, [w.x_t, w.mid_t], [w.grad_v, w.context])[0])

        def vo_own():
            w.vo_own = attend_grad(0, F32, [w.x_t, w.mid_t], [w.grad_v, w.context])

        def qk_oth():
            pieces = cols // LANES
            other = sharded(attend_grad(1, BF16, [w.x_t, w.x_t], [w.grad_q, w.grad_k], pieces), 2)
            w.scatter_a = Scatter(grid, tape, [(v, 0, LANES * i) for i, v in enumerate(other)])

        def qk_own():
            w.qk_own = attend_grad(0, F32, [w.x_t, w.x_t], [w.grad_q, w.grad_k])

        def vo_sum():
            w.vo_sum = tape.run(add_up, [((2, width, cols), F32)], [w.vo_own[0], w.vo_oth])

        def pair_a():
            w.scatter_a.pair(sharded(w.qk_own + w.vo_sum, 2), counts_of[4])

        def attend_back(probs_ref, back_ref, qkv_ref, grad_q, grad_k, sums):
            sums[...] = jnp.zeros_like(sums)

            for p in range(mine):
                at = slice(p * length, (p + 1) * length)
                for u in range(twins):
                    lanes = slice(u * LANES, (u + 1) * LANES)
                    prob = probs_ref[at, 2 * u * length : 2 * (u + 1) * length].astype(F32)
                    both = lax.dot_general(
                        back_ref[at, lanes], split(qkv_ref[2, at, lanes]), NT, preferred_element_type=F32
                    )
                    parts = []
                    for h in range(2):
                        half = slice(h * length, (h + 1) * length)
                        inner = jnp.sum(prob[:, half] * both[:, half], axis=-1, keepdims=True)
                        parts.append(prob[:, half] * (both[:, half] - inner))
                    grad = jnp.concatenate(parts, axis=1).astype(BF16)
                    value = jnp.dot(grad, split(qkv_ref[1, at, lanes]), preferred_element_type=F32) * scale
                    grad_q[at, lanes] = value.astype(BF16)
                    sums[:, lanes] += sum_rows(value)
                    value = join(lax.dot_general(grad, qkv_ref[0, at, lanes], TN, preferred_element_type=F32))
                    grad_k[at, lanes] = (value * scale).astype(BF16)

        def attended_back():
            w.grad_q, w.grad_k, w.sum_q = tape.run(
                attend_back, [((rows, width), BF16), ((rows, width), BF16), ((1, width), F32)], [w.probs, w.back, w.qkv],
                limit=4, flops=16 * rows * length * width, moved=6 * MIB,
            )
        def add_up(own, oth, out):
            out[...] = own[...] + oth[...].astype(F32)

        def states_back(grad_q_ref, grad_k_ref, grad_v_ref, own, oth, mid_ref, out):
            @pl.loop(0, width // tile)
            def _(i):
                at = pl.ds(pl.multiple_of(i * tile, tile), tile)
                value = mid_ref[:, at]
                for j, ref in enumerate((grad_q_ref, grad_k_ref, grad_v_ref)):
                    for h, weight in enumerate((own, oth)):
                        value += lax.dot_general(
                            ref[:, h * cols : (h + 1) * cols], weight[j, at, :], NT, preferred_element_type=F32
                        )
                out[:, at] = value.astype(BF16)

        def states_own():
            w.states_own = tape.run(
                states_back, [((rows, width), BF16)], [w.grad_q, w.grad_k, w.grad_v, w.a_own, w.a_oth, w.mid],
                limit=8, flops=6 * rows * width * width, moved=8 * MIB,
            )[0]

        def matrix_step(index):
            def step(*refs):
                grad = refs[0][...] + refs[1][...].astype(F32)
                grad = jnp.concatenate([grad[j] for j in range(grad.shape[0])], axis=-1)[None]
                master, first, second, moment, square, way, kept, tile_ref = refs[2:]
                moment[...], square[...], value = adam(grad, first[...], second[...])
                kept[...] = master[...]
                way[...] = value + DECAY * kept[...]
                tile_ref[...] = norm_row([(index, kept[0], way[0])])

            return step

        def stepped(step, parts, masters, shapes):
            outs = [(s, F32) for _ in range(4) for s in shapes] + [((1, LANES), F32)]
            n, m = len(parts), len(masters)
            return tape.run(
                step, outs, parts + masters, limit=6, spill=range(2 * len(shapes)), plain=range(n, n + m), moved=2 * MIB
            )

        ups = [v[None] for v in (expand_up, first_up, second_up)]
        downs = [v[None] for v in (expand_down, first_down, second_down)]

        def collect(s, sum_q_ref, sum_v_ref, one, two, up_own_ref, up_oth_ref, out):
            for t in range(cores):

                @pl.when(s[3] == t)
                def _():
                    for row, ref in enumerate((sum_q_ref, sum_v_ref)):
                        for h in range(2):
                            out[row : row + 1, (h ^ t) * cols : ((h ^ t) + 1) * cols] = ref[
                                :, h * cols : (h + 1) * cols
                            ]
                    for h, ref in enumerate((up_own_ref, up_oth_ref)):
                        for i in range(units // width):
                            row = 8 + (h ^ t) * (units // width) + i
                            out[row : row + 1] = ref[:, i * width : (i + 1) * width]

            out[2:5] = one[0:3]
            out[5:8] = two[0:3]

        half = vectors.shape[0] // cores

        def collected():
            w.vector_part = tape.run(
                    collect, [(vectors.shape, F32)],
                    [w.sum_q, w.sum_v, w.sums_one, w.sums_two, w.sink_own[1], w.sink_oth[1]], True,
            )[0]

        def vector_half(s, own, oth, out):
            for t in range(cores):

                @pl.when(s[3] == t)
                def _():
                    at = slice(t * half, (t + 1) * half)
                    out[...] = own[at] + oth[at]

        def vector_shared():
            parts = [w.vector_part, grid.core(w.vector_part)]
            w.vector_share = tape.run(vector_half, [((half, width), F32)], parts, True)[0]

        def step_c():
            w.step_c = stepped(matrix_step(5), w.scatter_c.parts, downs, [downs[0].shape])

        def step_b():
            w.step_b = stepped(matrix_step(4), w.scatter_b.parts, ups, [ups[0].shape])

        def states_pair():
            w.states_grad = paired(w.states_own, grid.core(w.states_own), F32)

        def output_pair():
            w.layer_output = paired(w.output, grid.core(w.output), BF16)

        def attend_step(*refs):
            n = len(w.scatter_a.parts)
            m_in, f_in, s_in, m_out, f_out, s_out, tile_up_ref, tile_down_ref, share = refs[n : n + 9]
            mo_in, mo_out, sq_in, sq_out, way_in, way_out, kept_in, kept_out, load = refs[n + 9 :]
            entries = []
            for j in range(4):
                grad = sum((ref[j].astype(F32) for ref in refs[1:n]), refs[0][j])
                i = j if j < 3 else 0
                m, f, s, mo, sq, kept, way = (
                    (m_in, f_in, s_in, mo_in, sq_in, kept_in, way_in)
                    if j < 3
                    else (m_out, f_out, s_out, mo_out, sq_out, kept_out, way_out)
                )
                mo[i], sq[i], value = adam(grad, f[i], s[i])
                kept[i] = m[i]
                way[i] = value + DECAY * kept[i]
                entries.append((j, kept[i], way[i]))
            load[...] = jnp.zeros_like(load)
            load[0:half] = share[...]
            load[half : half + 1, 0:LANES] = norm_row(entries) + tile_up_ref[...] + tile_down_ref[...]

        shapes = [attend_in.shape, attend_out.shape]
        masters = [attend_in, first_in, second_in, attend_out, first_out, second_out]
        def step_a():
            w.step_a = tape.run(
                attend_step, [(s, F32) for _ in range(4) for s in shapes] + [((8, width), F32)],
                w.scatter_a.parts + masters + [w.step_b[4], w.step_c[4], w.vector_share],
                limit=6, spill=range(4), plain=range(len(w.scatter_a.parts), len(w.scatter_a.parts) + 6),
            )

        stages = {
            "a0": lambda: w.gather_a.merge_long(), "a1": lambda: w.gather_a.merge_short(),
            "b0": lambda: w.gather_b.merge(0), "b1": lambda: w.gather_b.merge(1), "b2": lambda: w.gather_b.merge(2),
            "c0": lambda: w.gather_c.merge(0), "c1": lambda: w.gather_c.merge(1), "c2": lambda: w.gather_c.merge(2),
            "A0": lambda: w.scatter_a.split(0), "A1": lambda: w.scatter_a.split(1), "A2": lambda: w.scatter_a.split(2),
            "B0": lambda: w.scatter_b.split(0), "B1": lambda: w.scatter_b.split(1), "B2": lambda: w.scatter_b.split(2),
            "C0": lambda: w.scatter_c.split(0), "C1": lambda: w.scatter_c.split(1), "C2": lambda: w.scatter_c.split(2),
            "castA": cast_a, "castB": cast_b, "castC": cast_c, "prep": prepared, "wholeA": whole_a, "wholeB": whole_b,
            "wholeC": whole_c, "otherA": other_a, "otherB": other_b, "otherC": other_c, "project": projected, "attend": attended, "hide": hid, "liftOwn": lift_own,
            "liftOth": lift_oth, "turn": turned, "lowerOwn": lowered_own, "lower": lowered_all, "downOth": down_oth,
            "downOwn": down_own, "pairC": pair_c, "upOth": up_oth, "upOwn": up_own, "pairB": pair_b, "sinkOwn": sink_own,
            "sinkOth": sink_oth, "surface": surfaced, "values": valued, "voOth": vo_oth, "voOwn": vo_own,
            "qkOth": qk_oth, "qkOwn": qk_own, "voSum": vo_sum, "pairA": pair_a, "back": attended_back,
            "states": states_own, "collect": collected, "share": vector_shared, "stepC": step_c, "stepB": step_b,
            "pairS": states_pair, "pairO": output_pair, "stepA": step_a,
        }
        for name in ORDER:
            stages[name]()
        moment_down, square_down, way_down, kept_down, _ = w.step_c
        moment_up, square_up, way_up, kept_up, _ = w.step_b
        moment_in, moment_out, square_in, square_out, way_in, way_out, kept_in, kept_out, load = w.step_a
        total = Total(grid, tape, load)
        total.line()
        total.sides()

        def update(s, own, oth, vec, vec_first, vec_second, *refs):
            masters, ways, outs, grad = refs[:4], refs[4:8], refs[8:-1], refs[-1]
            norms = jnp.sqrt(own[half : half + 1, 0:LANES] + oth[half : half + 1, 0:LANES])
            outs[8][0:1] = norms[:, 0:6]
            outs[8][1:2] = norms[:, 6:12]
            for i, first in enumerate((0, 3, 4, 5)):
                for j in range(masters[i].shape[0]):
                    m = first + j
                    trust = RATE * (norms[:, m : m + 1] / norms[:, 6 + m : 7 + m])
                    value = masters[i][j] - trust * ways[i][j]
                    outs[i][j], outs[4 + i][j] = value, value.astype(BF16)
            for t in range(cores):

                @pl.when(s[3] == t)
                def _():
                    grad[t * half : (t + 1) * half] = own[0:half]
                    grad[(1 - t) * half : (2 - t) * half] = oth[0:half]

            outs[10][...], outs[11][...], direction = adam(grad[...], vec_first[...], vec_second[...])
            outs[9][...] = vec[...] - RATE * direction

        masters = [kept_in, kept_out, kept_up, kept_down]
        results = tape.run(
            update,
            [(m.shape, F32) for m in masters] + [(m.shape, BF16) for m in masters] + [((2, 6), F32)]
            + [(vectors.shape, F32)] * 3,
            total.pair + [vectors, vector_first, vector_second] + masters + [way_in, way_out, way_up, way_down],
            True, limit=6, spill=range(12), plain=(2, 3, 4), moved=2 * MIB,
            scratch=[VMEM(vectors.shape, F32)],
        )
        updated_vectors, moment_vectors, square_vectors = results[9:12]

        def native(values):
            values = list(values)
            return (values[0], values[1][0].T, values[2][0], values[3][0])

        return (
            w.layer_output, w.states_grad, *native(results[:4]),
            *native([moment_in, moment_out, moment_up, moment_down]),
            *native([square_in, square_out, square_up, square_down]),
            *native(results[4:8]), updated_vectors, moment_vectors, square_vectors, results[8].T,
        )

    return body


def solution(mesh):
    rows = P("dp", None, None)
    matrices = (P(None, "dp", "tensor"), P("tensor", "dp"), P("dp", "tensor"), P(("tensor", "dp"), None))
    in_specs = (rows, rows, P("dp"), P("dp")) + matrices * 3 + (P(), P(), P())
    out_specs = (rows, rows) + matrices * 4 + (P(), P(), P(), P())
    body = make_body(Grid(mesh))
    return jax.shard_map(body, mesh=mesh, in_specs=in_specs, out_specs=out_specs, check_vma=False)
```
